256 devices in a mesh: row: 16 (over z_lo, x), col: 16 (over z_hi, y, core).
Axes of the slice: x: 4, y: 4, z: 8 (z_hi: 2, z_lo: 4; z = z_hi * 4 + z_lo), core: 2. Of those that a mesh axis runs over, the one named last changes fastest.
Arguments:
- feat: bfloat16 [512, 512, 256], P('row', 'col'), may hold values from -6 to 6
- noise_fine: float32 [512, 512, 256], P('row', 'col'), may hold values from -0.5 to 0.5
- noise_coarse: float32 [256, 256, 256], P('row', 'col'), may hold values from -0.5 to 0.5
- w_post: bfloat16 [2304, 256], replicated, may hold values from -0.125 to 0.125
- w_coarse: bfloat16 [2304, 256], replicated, may hold values from -0.125 to 0.125
- w_prior: bfloat16 [2304, 512], replicated, may hold values from -0.125 to 0.125
Outputs:
- grad_feat: bfloat16 [512, 512, 256], P('row', 'col')
- grad_post: float32 [589824], P(('row', 'col'))
- grad_coarse: float32 [589824], P(('row', 'col'))
- grad_prior: float32 [1179648], P(('row', 'col'))
The draws below stay inside these ranges and needn't reach their ends.
All inputs are finite; a program needn't handle non-finite values.
Results may differ from the reference program's by a relative error of at most 0.0075.
Values may be sent and summed in bfloat16 or wider, within the bound.
No kernel may reach another device: no remote copies, remote signals or barrier semaphores. Data moves between devices by JAX's collectives and lax.ppermute only.
A program may use at most 128 MiB of HBM per device.

```python
import math
import jax
import jax.numpy as jnp

C = 256
H = 512
W = 512
H2 = 256
W2 = 256


def with_spikes(entries, own_key, source, target, parts, factor):
    def block_of(position):
        return (jnp.arange(entries.shape[position]) // (entries.shape[position] // parts)).reshape((-1,) + (1,) * (entries.ndim - 1 - position))

    first = jax.random.permutation(own_key, parts)[block_of(target)]
    far = (block_of(target) + parts // 2) % parts
    return jnp.where((block_of(source) == first) | (block_of(source) == far), factor * entries, entries)


def steps_of(rng, shape, shards, smallest, largest):
    level = 1.0
    for position, shards_of in shards:
        heights = jax.random.uniform(jax.random.fold_in(jax.random.fold_in(rng, 6), position), (shards_of,), jnp.float32, smallest / len(shards), largest / len(shards))
        level = level * jnp.repeat(jnp.exp(heights), shape[position] // shards_of).reshape((-1,) + (1,) * (len(shape) - 1 - position))
    return level


def centred(rng, dims, width, bound, cuts=(), held_as=jnp.bfloat16):
    loudness = steps_of(rng, dims, cuts, -0.22, 0.18) if cuts else 1.0
    drawn = jax.random.normal(rng, dims, jnp.float32) * width * loudness
    return jnp.minimum(jnp.maximum(drawn, -bound), bound).astype(held_as)


def bell_draw_with(stream_key, shape, scale, limit, pieces, heavy, held_as=jnp.bfloat16):
    entries = scale * jax.random.normal(stream_key, shape, jnp.float32)
    if pieces:
        entries = entries * steps_of(stream_key, shape, pieces, -0.22, 0.18)
    return jnp.clip(with_spikes(entries, jax.random.fold_in(stream_key, 3), *heavy), -limit, limit).astype(held_as)


def setup_inputs(seed: int = 0) -> dict:
    streams_of = jax.random.split(jax.random.key(seed), 7)
    return {
        "feat": bell_draw_with(streams_of[0], (H, W, C), 1.0, 6.0, ((0, 16), (1, 16)), (0, 2, 16, 2.0)),
        "noise_fine": jnp.clip(jax.random.uniform(streams_of[1], (H, W, C), jnp.float32, -0.5, 0.5) * steps_of(streams_of[1], (H, W, C), ((0, 16), (1, 16)), -0.4, 0.0), -0.5, 0.5),
        "noise_coarse": jnp.clip(jax.random.uniform(streams_of[2], (H2, W2, C), jnp.float32, -0.5, 0.5) * steps_of(streams_of[2], (H2, W2, C), ((0, 16), (1, 16)), -0.4, 0.0), -0.5, 0.5),
        "w_post": centred(streams_of[3], (9 * C, C), (9 * C) ** -0.5, 0.125),
        "w_coarse": centred(streams_of[4], (9 * C, C), (9 * C) ** -0.5, 0.125),
        "w_prior": centred(streams_of[5], (9 * C, 2 * C), (9 * C) ** -0.5, 0.125),
    }


def conv_taps(field, weight):
    size_r, size_c, chans = field.shape
    padded = jnp.pad(field, ((1, 1), (1, 1), (0, 0)))
    total = jnp.zeros((size_r * size_c, weight.shape[1]), jnp.float32)
    for tap_row in range(3):
        for tap_col in range(3):
            index = 3 * tap_row + tap_col
            piece = padded[tap_row:tap_row + size_r, tap_col:tap_col + size_c].reshape(-1, chans)
            total = total + jnp.dot(piece, weight[index * chans:(index + 1) * chans], preferred_element_type=jnp.float32)
    return total.reshape(size_r, size_c, weight.shape[1])

def conv_back(grad, weight):
    size_r, size_c, chans_g = grad.shape
    chans_in = weight.shape[0] // 9
    padded = jnp.pad(grad, ((1, 1), (1, 1), (0, 0)))
    total = jnp.zeros((size_r * size_c, chans_in), jnp.float32)
    for tap_row in range(3):
        for tap_col in range(3):
            index = 3 * tap_row + tap_col
            piece = padded[2 - tap_row:2 - tap_row + size_r, 2 - tap_col:2 - tap_col + size_c].reshape(-1, chans_g)
            total = total + jnp.dot(piece, weight[index * chans_in:(index + 1) * chans_in].T, preferred_element_type=jnp.float32)
    return total.reshape(size_r, size_c, chans_in)

def weight_grad(field, grad):
    size_r, size_c, chans = field.shape
    padded = jnp.pad(field, ((1, 1), (1, 1), (0, 0)))
    flat_grad = grad.reshape(-1, grad.shape[-1])
    blocks = []
    for tap_row in range(3):
        for tap_col in range(3):
            piece = padded[tap_row:tap_row + size_r, tap_col:tap_col + size_c].reshape(-1, chans)
            blocks.append(jnp.dot(piece.T, flat_grad, preferred_element_type=jnp.float32))
    return jnp.concatenate(blocks, axis=0)

def repeat_two(field):
    return jnp.repeat(jnp.repeat(field, 2, axis=0), 2, axis=1)

def reference(feat, noise_fine, noise_coarse, w_post, w_coarse, w_prior):
    full_r, full_c, chans = feat.shape
    grad_scale = 1.0 / math.sqrt(full_r * full_c)
    fine = conv_taps(feat, w_post) + noise_fine
    pooled = fine.reshape(full_r // 2, 2, full_c // 2, 2, chans).mean(axis=(1, 3)).astype(jnp.bfloat16)
    coarse = conv_taps(pooled, w_coarse) + noise_coarse
    context = repeat_two(coarse.astype(jnp.bfloat16))
    prior = conv_taps(context, w_prior)
    prior_mean = prior[..., :chans]
    raw_scale = prior[..., chans:]
    prior_scale = jax.nn.softplus(raw_scale) + 0.5
    deviation = fine - prior_mean
    residual_term = deviation / (prior_scale * prior_scale)
    scale_term = 1.0 / prior_scale - deviation * deviation / (prior_scale * prior_scale * prior_scale)
    dprior = jnp.concatenate([-residual_term, scale_term * jax.nn.sigmoid(raw_scale)], axis=-1).astype(jnp.bfloat16)
    grad_prior = weight_grad(context, dprior) * grad_scale
    back_context = conv_back(dprior, w_prior)
    gcoarse = (coarse + back_context.reshape(full_r // 2, 2, full_c // 2, 2, chans).sum(axis=(1, 3))).astype(jnp.bfloat16)
    grad_coarse = weight_grad(pooled, gcoarse) * grad_scale
    back_pooled = conv_back(gcoarse, w_coarse)
    gfine = (residual_term + 0.25 * repeat_two(back_pooled)).astype(jnp.bfloat16)
    grad_post = weight_grad(feat, gfine) * grad_scale
    grad_feat = conv_back(gfine, w_post).astype(jnp.bfloat16)
    return (grad_feat, grad_post.reshape(-1), grad_coarse.reshape(-1), grad_prior.reshape(-1))
```

```python
import math

import jax
import jax.numpy as jnp
from jax import lax
from jax.sharding import PartitionSpec as P


def padded_2(cells, sides, width):
    for axis, dim in sides:
        count = lax.axis_size(axis)
        ends = count - 1
        head = lax.slice_in_dim(cells, 0, width, axis=dim)
        tail = lax.slice_in_dim(cells, cells.shape[dim] - width, cells.shape[dim], axis=dim)
        cells = jnp.concatenate(
            [
                lax.ppermute(tail, axis, [(i, (i + 1) % count) for i in range(ends)]),
                cells,
                lax.ppermute(head, axis, [((i + 1) % count, i) for i in range(ends)]),
            ],
            axis=dim,
        )
    return cells


def gather_taps(padded, size_r, size_c, reverse_taps):
    pieces = []
    for tap_row in range(3):
        for tap_col in range(3):
            top = 2 - tap_row if reverse_taps else tap_row
            left = 2 - tap_col if reverse_taps else tap_col
            pieces.append(padded[top : top + size_r, left : left + size_c])
    stacked = jnp.concatenate(pieces, axis=-1)
    return stacked.reshape(size_r * size_c, stacked.shape[-1])


def turned_weight(weight):
    chans_in = weight.shape[0] // 9
    chans_out = weight.shape[1]
    return (
        weight.reshape(9, chans_in, chans_out).transpose(0, 2, 1).reshape(9 * chans_out, chans_in)
    )


def weight_grad(columns, grad):
    return lax.dot_general(
        columns, grad, (((0,), (0,)), ((), ())), preferred_element_type=jnp.float32
    )


def repeat_two(field):
    return jnp.repeat(jnp.repeat(field, 2, axis=0), 2, axis=1)


def digits():
    places = []
    for d in range(256):
        row, col = d // 16, d % 16
        places.append({"zl": row // 4, "x": row % 4, "zh": col // 8, "y": (col // 2) % 4, "core": col % 2})
    return places


RADIX = {"core": 2, "x": 4, "y": 4, "zl": 4, "zh": 2}


def index_of(place):
    return (place["zl"] * 4 + place["x"]) * 16 + (place["zh"] * 4 + place["y"]) * 2 + place["core"]


def my_place():
    row, col = lax.axis_index("row"), lax.axis_index("col")
    return {"zl": row // 4, "x": row % 4, "zh": col // 8, "y": (col // 2) % 4, "core": col % 2}


def moved(place, name, step):
    return {**place, name: (place[name] + step) % RADIX[name]}


def sum_stage(part, name):
    radix = RADIX[name]
    here = my_place()[name]
    share = part.shape[0] // radix
    cut = part.reshape(radix, share, part.shape[1])
    total = lax.dynamic_index_in_dim(cut, here, 0, keepdims=False).astype(jnp.float32)
    order = (1, 3, 2) if radix == 4 else (1,)
    arrived = []
    for step in order:
        piece = lax.dynamic_index_in_dim(cut, (here + step) % radix, 0, keepdims=False)
        pairs = [(index_of(p), index_of(moved(p, name, step))) for p in digits()]
        arrived.append(lax.ppermute(piece, ("row", "col"), pairs))
    for piece in arrived:
        total = total + piece.astype(jnp.float32)
    return total.astype(jnp.bfloat16)


def reduce_scatter(part, stages):
    for name in stages:
        part = sum_stage(part, name)
    halves = part.reshape(2, part.shape[0] // 2, part.shape[1])
    last = my_place()["zh"]
    total = 0.0
    for flip in (0, 1):
        pairs = []
        for p in digits():
            chunk = 0
            for name in stages:
                chunk = chunk * RADIX[name] + p[name]
            pairs.append((index_of(p), chunk * 2 + (p["zh"] + flip) % 2))
        piece = lax.dynamic_index_in_dim(halves, (last + flip) % 2, 0, keepdims=False)
        total = total + lax.ppermute(piece, ("row", "col"), pairs).astype(jnp.float32)
    return total


def on_device(feat, noise_fine, noise_coarse, w_post, w_coarse, w_prior):
    tile_rows, tile_cols, chans = feat.shape
    half_rows = tile_rows // 2
    half_cols = tile_cols // 2
    grad_scale = 1.0 / math.sqrt(
        tile_rows * lax.axis_size("row") * tile_cols * lax.axis_size("col")
    )
    feat_pad = padded_2(feat, (("row", 0), ("col", 1)), 1)
    feat_columns = gather_taps(feat_pad, tile_rows, tile_cols, False)
    fine = (
        jnp.dot(feat_columns, w_post, preferred_element_type=jnp.float32).reshape(
            tile_rows, tile_cols, chans
        )
        + noise_fine
    )
    pooled = fine.reshape(half_rows, 2, half_cols, 2, chans).mean(axis=(1, 3)).astype(jnp.bfloat16)
    pooled_pad = padded_2(pooled, (("row", 0), ("col", 1)), 1)
    pooled_columns = gather_taps(pooled_pad, half_rows, half_cols, False)
    coarse = (
        jnp.dot(pooled_columns, w_coarse, preferred_element_type=jnp.float32).reshape(
            half_rows, half_cols, chans
        )
        + noise_coarse
    )
    latent_bf = coarse.astype(jnp.bfloat16)
    context_pad = padded_2(repeat_two(latent_bf), (("row", 0), ("col", 1)), 1)
    context_columns = gather_taps(context_pad, tile_rows, tile_cols, False)
    prior = jnp.dot(context_columns, w_prior, preferred_element_type=jnp.float32).reshape(
        tile_rows, tile_cols, 2 * chans
    )
    prior_mean = prior[..., :chans]
    raw_scale = prior[..., chans:]
    prior_scale = jax.nn.softplus(raw_scale) + 0.5
    deviation = fine - prior_mean
    residual_term = deviation / (prior_scale * prior_scale)
    scale_term = 1.0 / prior_scale - deviation * deviation / (
        prior_scale * prior_scale * prior_scale
    )
    dprior = jnp.concatenate(
        [-residual_term, scale_term * jax.nn.sigmoid(raw_scale)], axis=-1
    ).astype(jnp.bfloat16)
    grad_prior = (
        weight_grad(context_columns, dprior.reshape(tile_rows * tile_cols, 2 * chans)) * grad_scale
    )
    dprior_pad = padded_2(dprior, (("row", 0), ("col", 1)), 1)
    back_context = jnp.dot(
        gather_taps(dprior_pad, tile_rows, tile_cols, True),
        turned_weight(w_prior),
        preferred_element_type=jnp.float32,
    )
    back_context = back_context.reshape(half_rows, 2, half_cols, 2, chans).sum(axis=(1, 3))
    gcoarse = (coarse + back_context).astype(jnp.bfloat16)
    grad_coarse = (
        weight_grad(pooled_columns, gcoarse.reshape(half_rows * half_cols, chans)) * grad_scale
    )
    gcoarse_pad = padded_2(gcoarse, (("row", 0), ("col", 1)), 1)
    back_pooled = jnp.dot(
        gather_taps(gcoarse_pad, half_rows, half_cols, True),
        turned_weight(w_coarse),
        preferred_element_type=jnp.float32,
    )
    back_pooled = back_pooled.reshape(half_rows, half_cols, chans)
    gfine = (residual_term + 0.25 * repeat_two(back_pooled)).astype(jnp.bfloat16)
    grad_post = weight_grad(feat_columns, gfine.reshape(tile_rows * tile_cols, chans)) * grad_scale
    gfine_pad = padded_2(gfine, (("row", 0), ("col", 1)), 1)
    grad_feat = jnp.dot(
        gather_taps(gfine_pad, tile_rows, tile_cols, True),
        turned_weight(w_post),
        preferred_element_type=jnp.float32,
    )
    grad_feat = grad_feat.reshape(tile_rows, tile_cols, chans).astype(jnp.bfloat16)
    summed_prior = reduce_scatter(grad_prior.astype(jnp.bfloat16), ("core", "x", "y", "zl"))
    summed_coarse = reduce_scatter(grad_coarse.astype(jnp.bfloat16), ("core", "y", "x", "zl"))
    summed_post = reduce_scatter(grad_post.astype(jnp.bfloat16), ("core", "y", "x", "zl"))
    return (grad_feat, summed_post.reshape(-1), summed_coarse.reshape(-1), summed_prior.reshape(-1))


def solution(mesh):
    return jax.shard_map(
        on_device,
        mesh=mesh,
        in_specs=(
            P("row", "col", None),
            P("row", "col", None),
            P("row", "col", None),
            P(),
            P(),
            P(),
        ),
        out_specs=(P("row", "col", None), P(("row", "col")), P(("row", "col")), P(("row", "col"))),
        check_vma=False,
    )
```

```python
import functools
import math

import jax
import jax.numpy as jnp
from jax import lax
from jax.experimental import pallas as pl
from jax.experimental.pallas import tpu as pltpu
from jax.sharding import PartitionSpec as P

BF = jnp.bfloat16
F32 = jnp.float32
VARIANT = ((1, -1), (0, 0), (1, 0), (0, 1))
FOLD = (3, 1, 2, 0)
VMEM_LIMIT = 60 * 1024 * 1024


def digits():
    places = []
    for d in range(256):
        row, col = d // 16, d % 16
        places.append({"zl": row // 4, "x": row % 4, "zh": col // 8, "y": (col // 2) % 4, "core": col % 2})
    return places


RADIX = {"core": 2, "x": 4, "y": 4, "zl": 4, "zh": 2}


def index_of(place):
    return (place["zl"] * 4 + place["x"]) * 16 + (place["zh"] * 4 + place["y"]) * 2 + place["core"]


def my_place():
    row, col = lax.axis_index("row"), lax.axis_index("col")
    return {"zl": row // 4, "x": row % 4, "zh": col // 8, "y": (col // 2) % 4, "core": col % 2}


def moved(place, name, step):
    return {**place, name: (place[name] + step) % RADIX[name]}


def sum_stage(part, name):
    radix = RADIX[name]
    here = my_place()[name]
    share = part.shape[0] // radix
    cut = part.reshape(radix, share, part.shape[1])
    total = lax.dynamic_index_in_dim(cut, here, 0, keepdims=False).astype(jnp.float32)
    order = (1, 3, 2) if radix == 4 else (1,)
    arrived = []
    for step in order:
        piece = lax.dynamic_index_in_dim(cut, (here + step) % radix, 0, keepdims=False)
        pairs = [(index_of(p), index_of(moved(p, name, step))) for p in digits()]
        arrived.append(lax.ppermute(piece, ("row", "col"), pairs))
    for piece in arrived:
        total = total + piece.astype(jnp.float32)
    return total.astype(jnp.bfloat16)


def reduce_scatter(part, stages):
    for name in stages:
        part = sum_stage(part, name)
    halves = part.reshape(2, part.shape[0] // 2, part.shape[1])
    last = my_place()["zh"]
    total = 0.0
    for flip in (0, 1):
        pairs = []
        for p in digits():
            chunk = 0
            for name in stages:
                chunk = chunk * RADIX[name] + p[name]
            pairs.append((index_of(p), chunk * 2 + (p["zh"] + flip) % 2))
        piece = lax.dynamic_index_in_dim(halves, (last + flip) % 2, 0, keepdims=False)
        total = total + lax.ppermute(piece, ("row", "col"), pairs).astype(jnp.float32)
    return total


def in_vmem(count):
    return [pl.BlockSpec(memory_space=pltpu.VMEM)] * count


def split_lanes(ref, value):
    for half in range(2):
        ref[:, :, half] = value[..., 128 * half:128 * (half + 1)]


def phase_of(ref, row, col):
    return jnp.concatenate([ref[:, row, half, pl.ds(col, 16, stride=2), :] for half in range(2)], axis=-1)


def line_of(ref, line, col):
    return jnp.concatenate(
        [ref[line // 2, line % 2, half, pl.ds(col, 16, stride=2), :] for half in range(2)], axis=-1)


def pack_kernel(feat_ref, fine_ref, low_ref, own_ref, top_ref, bottom_ref, left_ref, right_ref, wide, noise, side):
    split_lanes(wide, feat_ref[...].astype(F32))
    split_lanes(noise, fine_ref[...])
    for out, first, fine_first, low_first in ((top_ref, 0, 0, 0), (bottom_ref, 23, 24, 13)):
        for r in range(9):
            for col in range(2):
                out[2 * r + col] = line_of(wide, first + r, col).astype(BF)
        for r in range(8):
            for col in range(2):
                out[18 + 2 * r + col] = line_of(noise, fine_first + r, col).astype(BF)
        out[34:37] = low_ref[low_first:low_first + 3].astype(BF)
    for row in range(2):
        for col in range(2):
            own_ref[2 * row + col] = phase_of(wide, row, col).astype(BF)
    side[:, 32:40, :] = jnp.zeros((16, 8, 256), F32)
    for out, long, long_from, other_from, low_from in ((left_ref, 0, 0, 0, 0), (right_ref, 1, 11, 12, 13)):
        for row in range(2):
            at = 17 * row
            side[:, at:at + 5, :] = phase_of(wide, row, long)[:, long_from:long_from + 5]
            side[:, at + 5:at + 9, :] = phase_of(wide, row, 1 - long)[:, other_from:other_from + 4]
            for col in range(2):
                side[:, at + 9 + 4 * col:at + 13 + 4 * col, :] = (
                    phase_of(noise, row, col)[:, other_from:other_from + 4])
        side[:, 34:37, :] = low_ref[:, low_from:low_from + 3, :]
        out[...] = side[...].astype(BF)


def flat(block):
    return block.reshape(block.shape[0] * 32, block.shape[2])


def back_in_rows(block):
    return block.reshape(block.shape[0] // 32, 32, block.shape[1])


def before(block):
    return pltpu.roll(block, 1, 0)


def after(block):
    return pltpu.roll(block, block.shape[0] - 1, 0)


def dot(left, right):
    return jnp.dot(left, right, preferred_element_type=F32)


def inside(place_ref, first_row, rows):
    cell = lax.broadcasted_iota(jnp.int32, (rows * 32, 256), 0)
    line = cell // 32 + first_row + 16 * place_ref[0]
    column = cell % 32 - 8 + 16 * place_ref[1]
    return (line >= 0) & (line < 256) & (column >= 0) & (column < 256)


def three_wide(value, ref, first, rows):
    c = value.shape[1]
    for at, part in enumerate((before(value), value, after(value))):
        ref[pl.ds(first, rows), :, c * at:c * (at + 1)] = back_in_rows(part.astype(BF))


def own_cells(block):
    return block.astype(F32)[:, 8:24, :].reshape(256, block.shape[2]).astype(BF)


def turned(block):
    return own_cells(block).T


def main_kernel(scale, place_ref, own_ref, fine_ref, low_ref, up_ref, down_ref, left_ref, right_ref, ul_ref, ur_ref,
                dl_ref, dr_ref, w_post, w_coarse, fold, fold_t, w_coarse_t,
                g_post, g_coarse, g_prior, g_fine,
                field, fine, noise, low, cat, pool_cat, coarse, ctx_cat, err, d_cat, gc_cat, gf_own, turn):
    split_lanes(noise, fine_ref[...])
    for row in range(2):
        for col in range(2):
            p = 2 * row + col
            field[p, 5:21, 8:24, :] = own_ref[p].astype(F32)
            fine[p, 4:20, 8:24, :] = phase_of(noise, row, col)
    low[3:19, 8:24, :] = low_ref[...]
    for ref, first, fine_first, low_first in ((up_ref, -9, -8, 0), (down_ref, 32, 32, 19)):
        for r in range(9):
            line = first + r
            for col in range(2):
                field[2 * (line % 2) + col, line // 2 + 5, 8:24, :] = ref[2 * r + col].astype(F32)
        for r in range(8):
            line = fine_first + r
            for col in range(2):
                fine[2 * (line % 2) + col, line // 2 + 4, 8:24, :] = ref[18 + 2 * r + col].astype(F32)
        low[low_first:low_first + 3, 8:24, :] = ref[34:37].astype(F32)
    sides = (
        (left_ref, True, 0, 16, 0), (right_ref, False, 0, 16, 0),
        (ul_ref, True, -5, 5, -1), (ur_ref, False, -5, 5, -1), (dl_ref, True, 16, 5, 1), (dr_ref, False, 16, 5, 1),
    )
    for ref, on_left, first, rows, corner in sides:
        block = ref[...].astype(F32)
        fine_rows, low_rows = (slice(0, 16), slice(0, 16))
        if corner == -1:
            fine_rows, low_rows = slice(1, 5), slice(2, 5)
        if corner == 1:
            fine_rows, low_rows = slice(0, 4), slice(0, 3)
        fine_at, low_at = first + 4 + fine_rows.start, first + 3 + low_rows.start
        n_fine, n_low = fine_rows.stop - fine_rows.start, low_rows.stop - low_rows.start
        long = 1 if on_left else 0
        long_at = 3 if on_left else 24
        other_at = 4 if on_left else 24
        low_col = 5 if on_left else 24
        for row in range(2):
            at = 17 * row
            field[2 * row + long, first + 5:first + 5 + rows, long_at:long_at + 5, :] = block[:, at:at + 5, :]
            field[2 * row + 1 - long, first + 5:first + 5 + rows, other_at:other_at + 4, :] = block[:, at + 5:at + 9, :]
            for col in range(2):
                fine[2 * row + col, fine_at:fine_at + n_fine, other_at:other_at + 4, :] = (
                    block[fine_rows, at + 9 + 4 * col:at + 13 + 4 * col, :])
        low[low_at:low_at + n_low, low_col:low_col + 3, :] = block[low_rows, 34:37, :]

    @pl.loop(0, 2)
    def _(half):
        for row in range(2):
            rows = pl.ds(half * 13, 13)
            even, odd = flat(field[2 * row, rows]), flat(field[2 * row + 1, rows])
            for at, part in enumerate((before(odd), even, odd, after(even))):
                cat[row, rows, :, 256 * at:256 * (at + 1)] = back_in_rows(part.astype(BF))

    @pl.loop(0, 3)
    def _(step):
        total = jnp.zeros((256, 256), F32)
        for row in range(2):
            for col in range(2):
                p = 2 * row + col
                value = flat(fine[p, pl.ds(step * 8, 8)])
                for a in range(3):
                    phase, shift = VARIANT[row + a]
                    cells = flat(cat[phase, pl.ds(step * 8 + 1 + shift, 8), :, 256 * col:256 * col + 768])
                    value = value + dot(cells, w_post[768 * a:768 * (a + 1)])
                fine[p, pl.ds(step * 8, 8)] = back_in_rows(value)
                total = total + value
        total = jnp.where(inside(place_ref, step * 8 - 4, 8), total * 0.25, 0.0)
        three_wide(total, pool_cat, step * 8, 8)

    @pl.loop(0, 2)
    def _(step):
        value = flat(low[pl.ds(step * 11, 11)])
        for a in range(3):
            value = value + dot(flat(pool_cat[pl.ds(step * 11 + a, 11)]), w_coarse[768 * a:768 * (a + 1)])
        value = jnp.where(inside(place_ref, step * 11 - 3, 11), value, 0.0)
        coarse[pl.ds(step * 11, 11)] = back_in_rows(value)
        three_wide(value, ctx_cat, step * 11, 11)

    for row in range(2):
        @pl.loop(0, 3)
        def _(step):
            valid = inside(place_ref, step * 7 - 2 - row, 7)
            pieces = []
            for col in range(2):
                prior = jnp.zeros((224, 512), F32)
                for k in range(2):
                    cells = flat(ctx_cat[pl.ds(step * 7 + k, 7), :, 256 * col:256 * col + 512])
                    prior = prior + dot(cells, fold[2 * row + k, 512 * col:512 * col + 512])
                raw = prior[:, 256:]
                small = jnp.exp(-jnp.abs(raw))
                more = 1.0 + small
                sigma = jnp.maximum(raw, 0.0) + jnp.log(more) + 0.5
                gate = jnp.where(raw >= 0.0, 1.0, small) / more
                inverse = 1.0 / sigma
                deviation = flat(fine[2 * row + col, pl.ds(step * 7 + 2 - row, 7)]) - prior[:, :256]
                residual = deviation * inverse * inverse
                err[2 * row + col, pl.ds(step * 7, 7)] = back_in_rows(residual)
                pieces.append(jnp.where(valid, -residual, 0.0))
                pieces.append(jnp.where(valid, (inverse - residual * deviation * inverse) * gate, 0.0))
            parts = (before(pieces[2]), before(pieces[3]), pieces[0], pieces[1], pieces[2], pieces[3],
                     after(pieces[0]), after(pieces[1]))
            for at, part in enumerate(parts):
                d_cat[row, pl.ds(step * 7, 7), :, 256 * at:256 * (at + 1)] = back_in_rows(part.astype(BF))

    for i in range(3):
        for j in range(3):
            turn[3 * i + j] = turned(ctx_cat[2 + i:18 + i, :, 256 * j:256 * (j + 1)])
    for j in range(2):
        rights = []
        for row in range(2):
            for col in range(2):
                rights.append(jnp.concatenate(
                    [own_cells(d_cat[row, 2 + row:18 + row, :, 512 * (1 + col) + 256 * j:512 * (1 + col) + 256 * (j + 1)])],
                    axis=1))
        right = jnp.concatenate(rights, axis=0)
        for a in range(3):
            for b in range(3):
                lefts = [turn[3 * ((row + a + 1) // 2) + (col + b + 1) // 2] for row in range(2) for col in range(2)]
                tap = 3 * a + b
                g_prior[256 * tap:256 * (tap + 1), 256 * j:256 * (j + 1)] = (
                    dot(jnp.concatenate(lefts, axis=1), right) * scale).astype(BF)

    @pl.loop(0, 2)
    def _(step):
        value = flat(coarse[pl.ds(step * 10 + 1, 10)])
        for k in range(4):
            phase, shift = VARIANT[k]
            at = step * 10 + shift + phase
            value = value + dot(flat(d_cat[phase, pl.ds(at, 10)]), fold_t[k])
        value = jnp.where(inside(place_ref, step * 10 - 2, 10), value, 0.0)
        three_wide(value, gc_cat, step * 10, 10)

    right = own_cells(gc_cat[2:18, :, 256:512])
    for i in range(3):
        for j in range(3):
            left = turned(pool_cat[3 + i:19 + i, :, 256 * j:256 * (j + 1)])
            tap = 3 * i + j
            g_coarse[256 * tap:256 * (tap + 1), :] = (dot(left, right) * scale).astype(BF)

    @pl.loop(0, 2)
    def _(step):
        value = jnp.zeros((288, 256), F32)
        for a in range(3):
            value = value + dot(flat(gc_cat[pl.ds(step * 9 + a, 9)]), w_coarse_t[768 * a:768 * (a + 1)])
        value = value * 0.25
        valid = inside(place_ref, step * 9 - 1, 9)
        for row in range(2):
            even, odd = [
                jnp.where(valid, flat(err[2 * row + col, pl.ds(step * 9 + 1 + row, 9)]) + value, 0.0)
                for col in range(2)
            ]
            for at, part in enumerate((before(odd), even, odd, after(even))):
                compact = part.reshape(9, 32, 256)[:, 8:24, :]
                gf_own[row, pl.ds(step * 9, 9), :, 256 * at:256 * (at + 1)] = compact.astype(BF)
    g_fine[...] = gf_own[...]

    for k in range(4):
        phase, shift = VARIANT[k]
        for at in range(4):
            turn[4 * k + at] = turned(cat[phase, 5 + shift:21 + shift, :, 256 * at:256 * (at + 1)])
    right = jnp.concatenate(
        [gf_own[row, 1:17, :, 256 * (1 + col):256 * (2 + col)].reshape(256, 256) for row in range(2) for col in range(2)],
        axis=0)
    for a in range(3):
        for b in range(3):
            lefts = [turn[4 * (row + a) + col + b] for row in range(2) for col in range(2)]
            tap = 3 * a + b
            g_post[256 * tap:256 * (tap + 1), :] = (dot(jnp.concatenate(lefts, axis=1), right) * scale).astype(BF)


def feat_kernel(g_fine, w_post_t, out_ref, wide):
    for row in range(2):
        for col in range(2):
            value = jnp.zeros((256, 256), F32)
            for a in range(3):
                phase, shift = VARIANT[row + a]
                cells = g_fine[phase, 1 + shift:17 + shift, :, 256 * col:256 * col + 768].reshape(256, 768)
                value = value + dot(cells, w_post_t[768 * a:768 * (a + 1)])
            for half in range(2):
                wide[:, row, half, pl.ds(col, 16, stride=2), :] = (
                    value[:, 128 * half:128 * (half + 1)].reshape(16, 16, 128))
    for half in range(2):
        out_ref[:, :, :, 128 * half:128 * (half + 1)] = wide[:, :, half].astype(BF)


def turned_weight(weight):
    chans_in, chans_out = weight.shape[0] // 9, weight.shape[1]
    return weight.reshape(9, chans_in, chans_out)[::-1].transpose(0, 2, 1).reshape(9 * chans_out, chans_in)


def folded_weight(weight):
    taps = weight.astype(F32).reshape(3, 3, 256, 512)
    rows = jnp.stack([taps[0], taps[1] + taps[2], taps[0] + taps[1], taps[2]])
    return jnp.stack([rows[:, 0], rows[:, 1] + rows[:, 2], rows[:, 0] + rows[:, 1], rows[:, 2]], axis=1).astype(BF)


def sent(strip, down, right):
    pairs = [
        (r * 16 + c, (r + down) * 16 + c + right)
        for r in range(16) for c in range(16) if 0 <= r + down < 16 and 0 <= c + right < 16
    ]
    return lax.ppermute(strip, ("row", "col"), pairs)


def on_device(feat, noise_fine, noise_coarse, w_post, w_coarse, w_prior):
    scale = 1.0 / 512.0
    params = pltpu.CompilerParams(vmem_limit_bytes=VMEM_LIMIT)
    feat_rows = feat.reshape(16, 2, 32, 256)
    noise_rows = noise_fine.reshape(16, 2, 32, 256)
    own, top, bottom, left, right = pl.pallas_call(
        pack_kernel,
        out_shape=[
            jax.ShapeDtypeStruct((4, 16, 16, 256), BF),
            jax.ShapeDtypeStruct((37, 16, 256), BF),
            jax.ShapeDtypeStruct((37, 16, 256), BF),
            jax.ShapeDtypeStruct((16, 40, 256), BF),
            jax.ShapeDtypeStruct((16, 40, 256), BF),
        ],
        in_specs=in_vmem(3),
        out_specs=in_vmem(5),
        scratch_shapes=[
            pltpu.VMEM((16, 2, 2, 32, 128), F32),
            pltpu.VMEM((16, 2, 2, 32, 128), F32),
            pltpu.VMEM((16, 40, 256), F32),
        ],
        compiler_params=params,
        name="pack",
    )(feat_rows, noise_rows, noise_coarse)
    from_up = sent(bottom, 1, 0)
    from_down = sent(top, -1, 0)
    from_left = sent(right, 0, 1)
    from_right = sent(left, 0, -1)
    from_ul = sent(right[11:], 1, 1)
    from_ur = sent(left[11:], 1, -1)
    from_dl = sent(right[:5], -1, 1)
    from_dr = sent(left[:5], -1, -1)
    fold = folded_weight(w_prior)
    fold_t = jnp.stack([
        jnp.concatenate([fold[FOLD[k], FOLD[l]].T for l in range(4)], axis=0) for k in range(4)
    ])
    fold = fold.reshape(4, 1024, 512)
    place = jnp.stack([lax.axis_index("row"), lax.axis_index("col")]).astype(jnp.int32)
    g_post, g_coarse, g_prior, g_fine = pl.pallas_call(
        functools.partial(main_kernel, scale),
        out_shape=[
            jax.ShapeDtypeStruct((2304, 256), BF),
            jax.ShapeDtypeStruct((2304, 256), BF),
            jax.ShapeDtypeStruct((2304, 512), BF),
            jax.ShapeDtypeStruct((2, 18, 16, 1024), BF),
        ],
        in_specs=[pl.BlockSpec(memory_space=pltpu.SMEM)] + in_vmem(16),
        out_specs=in_vmem(4),
        scratch_shapes=[
            pltpu.VMEM((4, 26, 32, 256), F32),
            pltpu.VMEM((4, 24, 32, 256), F32),
            pltpu.VMEM((16, 2, 2, 32, 128), F32),
            pltpu.VMEM((22, 32, 256), F32),
            pltpu.VMEM((2, 26, 32, 1024), BF),
            pltpu.VMEM((24, 32, 768), BF),
            pltpu.VMEM((22, 32, 256), F32),
            pltpu.VMEM((22, 32, 768), BF),
            pltpu.VMEM((4, 21, 32, 256), F32),
            pltpu.VMEM((2, 21, 32, 2048), BF),
            pltpu.VMEM((20, 32, 768), BF),
            pltpu.VMEM((2, 18, 16, 1024), BF),
            pltpu.VMEM((16, 256, 256), BF),
        ],
        compiler_params=params,
        name="tile",
    )(place, own, noise_rows, noise_coarse, from_up, from_down, from_left, from_right, from_ul, from_ur,
      from_dl, from_dr, w_post, w_coarse, fold, fold_t, turned_weight(w_coarse))
    grad_feat = pl.pallas_call(
        feat_kernel,
        out_shape=jax.ShapeDtypeStruct((16, 2, 32, 256), BF),
        in_specs=in_vmem(2),
        out_specs=pl.BlockSpec(memory_space=pltpu.VMEM),
        scratch_shapes=[pltpu.VMEM((16, 2, 2, 32, 128), F32)],
        compiler_params=params,
        cost_estimate=pl.CostEstimate(flops=1200000000, bytes_accessed=3000000, transcendentals=0),
        name="feat",
    )(g_fine, turned_weight(w_post)).reshape(32, 32, 256)
    gradients = jnp.concatenate([g_prior, g_coarse, g_post], axis=1)
    summed = reduce_scatter(gradients, ("core", "x", "y", "zl"))
    return (
        grad_feat,
        summed[:, 768:].reshape(-1),
        summed[:, 512:768].reshape(-1),
        summed[:, :512].reshape(-1),
    )


def solution(mesh):
    return jax.shard_map(
        on_device,
        mesh=mesh,
        in_specs=(
            P("row", "col", None),
            P("row", "col", None),
            P("row", "col", None),
            P(),
            P(),
            P(),
        ),
        out_specs=(P("row", "col", None), P(("row", "col")), P(("row", "col")), P(("row", "col"))),
        check_vma=False,
    )
```

```python
import functools
import math

import jax
import jax.numpy as jnp
from jax import lax
from jax.experimental import pallas as pl
from jax.experimental.pallas import tpu as pltpu
from jax.sharding import PartitionSpec as P

BF = jnp.bfloat16
F32 = jnp.float32
VARIANT = ((1, -1), (0, 0), (1, 0), (0, 1))
FOLD = (3, 1, 2, 0)
VMEM_LIMIT = 60 * 1024 * 1024


def digits():
    places = []
    for d in range(256):
        row, col = d // 16, d % 16
        places.append({"zl": row // 4, "x": row % 4, "zh": col // 8, "y": (col // 2) % 4, "core": col % 2})
    return places


RADIX = {"core": 2, "x": 4, "y": 4, "zl": 4, "zh": 2}


def index_of(place):
    return (place["zl"] * 4 + place["x"]) * 16 + (place["zh"] * 4 + place["y"]) * 2 + place["core"]


def my_place():
    row, col = lax.axis_index("row"), lax.axis_index("col")
    return {"zl": row // 4, "x": row % 4, "zh": col // 8, "y": (col // 2) % 4, "core": col % 2}


def moved(place, name, step):
    return {**place, name: (place[name] + step) % RADIX[name]}


def sum_stage(part, name, dim):
    radix = RADIX[name]
    here = my_place()[name]
    arrived = []
    for step in (1, 3, 2) if radix == 4 else (1,):
        piece = lax.dynamic_index_in_dim(part, (here + step) % radix, dim, keepdims=False)
        pairs = [(index_of(p), index_of(moved(p, name, step))) for p in digits()]
        arrived.append(lax.ppermute(piece, ("row", "col"), pairs))
    total = lax.dynamic_index_in_dim(part, here, dim, keepdims=False).astype(F32)
    for piece in arrived:
        total = total + piece.astype(F32)
    return total.astype(BF)


def reduce_scatter(parts):
    parts = sum_stage(parts.reshape(2, 2, 1152, 512), "core", 1)
    first = parts[0].reshape(4, 4, 72, 512)
    second = parts[1].reshape(4, 4, 72, 512)
    first, second = sum_stage(first, "x", 0), sum_stage(second, "y", 1)
    first, second = sum_stage(first, "y", 0), sum_stage(second, "x", 0)
    parts = sum_stage(jnp.stack([first, second]).reshape(2, 4, 18, 512), "zl", 1)
    halves = parts.reshape(2, 2, 9, 512)
    last = my_place()["zh"]
    total = 0.0
    for flip in (0, 1):
        pairs = []
        for p in digits():
            chunk = (((p["core"] * 4 + p["x"]) * 4 + p["y"]) * 4 + p["zl"]) * 2 + (p["zh"] + flip) % 2
            pairs.append((index_of(p), chunk))
        piece = lax.dynamic_index_in_dim(halves, (last + flip) % 2, 1, keepdims=False)
        total = total + lax.ppermute(piece, ("row", "col"), pairs).astype(F32)
    return total


def in_vmem(count):
    return [pl.BlockSpec(memory_space=pltpu.VMEM)] * count


def split_lanes(ref, value):
    for half in range(2):
        ref[:, :, half] = value[..., 128 * half:128 * (half + 1)]


def phase_of(ref, row, col):
    return jnp.concatenate([ref[:, row, half, pl.ds(col, 16, stride=2), :] for half in range(2)], axis=-1)


def line_of(ref, line, col):
    return jnp.concatenate(
        [ref[line // 2, line % 2, half, pl.ds(col, 16, stride=2), :] for half in range(2)], axis=-1)


def pack_kernel(feat_ref, fine_ref, low_ref, own_ref, top_ref, bottom_ref, left_ref, right_ref, lu_ref, ld_ref, ru_ref, rd_ref,
                wide, noise, side):
    split_lanes(wide, feat_ref[...].astype(F32))
    split_lanes(noise, fine_ref[...])
    for out, first, fine_first, low_first in ((top_ref, 0, 0, 0), (bottom_ref, 23, 24, 13)):
        for r in range(9):
            for col in range(2):
                out[2 * r + col] = line_of(wide, first + r, col).astype(BF)
        for r in range(8):
            for col in range(2):
                out[18 + 2 * r + col] = line_of(noise, fine_first + r, col).astype(BF)
        out[34:37] = low_ref[low_first:low_first + 3].astype(BF)
    for row in range(2):
        for col in range(2):
            own_ref[2 * row + col] = phase_of(wide, row, col).astype(BF)
    side[:, 32:40, :] = jnp.zeros((16, 8, 256), F32)
    for out, up, down, long, long_from, other_from, low_from in (
            (left_ref, lu_ref, ld_ref, 0, 0, 0, 0), (right_ref, ru_ref, rd_ref, 1, 11, 12, 13)):
        for row in range(2):
            at = 17 * row
            side[:, at:at + 5, :] = phase_of(wide, row, long)[:, long_from:long_from + 5]
            side[:, at + 5:at + 9, :] = phase_of(wide, row, 1 - long)[:, other_from:other_from + 4]
            for col in range(2):
                side[:, at + 9 + 4 * col:at + 13 + 4 * col, :] = (
                    phase_of(noise, row, col)[:, other_from:other_from + 4])
        side[:, 34:37, :] = low_ref[:, low_from:low_from + 3, :]
        out[...] = side[...].astype(BF)
        up[...] = side[0:5].astype(BF)
        down[...] = side[11:16].astype(BF)


def flat(block):
    return block.reshape(block.shape[0] * 32, block.shape[2])


def back_in_rows(block):
    return block.reshape(block.shape[0] // 32, 32, block.shape[1])


def before(block):
    return pltpu.roll(block, 1, 0)


def after(block):
    return pltpu.roll(block, block.shape[0] - 1, 0)


def dot(left, right):
    return jnp.dot(left, right, preferred_element_type=F32)


def inside(place_ref, first_row, rows):
    cell = lax.broadcasted_iota(jnp.int32, (rows * 32, 256), 0)
    line = cell // 32 + first_row + 16 * place_ref[0]
    column = cell % 32 - 8 + 16 * place_ref[1]
    return (line >= 0) & (line < 256) & (column >= 0) & (column < 256)


def three_wide(value, ref, first, rows):
    c = value.shape[1]
    for at, part in enumerate((before(value), value, after(value))):
        ref[pl.ds(first, rows), :, c * at:c * (at + 1)] = back_in_rows(part.astype(BF))


def own_cells(block):
    return block.astype(F32)[:, 8:24, :].reshape(256, block.shape[2]).astype(BF)


def turned(block):
    return own_cells(block).T


def main_kernel(scale, place_ref, own_ref, fine_ref, low_ref, up_ref, down_ref, left_ref, right_ref, ul_ref, ur_ref,
                dl_ref, dr_ref, w_post, w_coarse, fold, fold_t, w_coarse_t,
                grads, g_fine,
                field, fine, noise, low, cat, pool_cat, coarse, ctx_cat, err, d_cat, gc_cat, gf_own, turn):
    split_lanes(noise, fine_ref[...])
    for row in range(2):
        for col in range(2):
            p = 2 * row + col
            field[p, 5:21, 8:24, :] = own_ref[p].astype(F32)
            fine[p, 4:20, 8:24, :] = phase_of(noise, row, col)
    low[3:19, 8:24, :] = low_ref[...]
    for ref, first, fine_first, low_first in ((up_ref, -9, -8, 0), (down_ref, 32, 32, 19)):
        for r in range(9):
            line = first + r
            for col in range(2):
                field[2 * (line % 2) + col, line // 2 + 5, 8:24, :] = ref[2 * r + col].astype(F32)
        for r in range(8):
            line = fine_first + r
            for col in range(2):
                fine[2 * (line % 2) + col, line // 2 + 4, 8:24, :] = ref[18 + 2 * r + col].astype(F32)
        low[low_first:low_first + 3, 8:24, :] = ref[34:37].astype(F32)
    sides = (
        (left_ref, True, 0, 16, 0), (right_ref, False, 0, 16, 0),
        (ul_ref, True, -5, 5, -1), (ur_ref, False, -5, 5, -1), (dl_ref, True, 16, 5, 1), (dr_ref, False, 16, 5, 1),
    )
    for ref, on_left, first, rows, corner in sides:
        block = ref[...].astype(F32)
        fine_rows, low_rows = (slice(0, 16), slice(0, 16))
        if corner == -1:
            fine_rows, low_rows = slice(1, 5), slice(2, 5)
        if corner == 1:
            fine_rows, low_rows = slice(0, 4), slice(0, 3)
        fine_at, low_at = first + 4 + fine_rows.start, first + 3 + low_rows.start
        n_fine, n_low = fine_rows.stop - fine_rows.start, low_rows.stop - low_rows.start
        long = 1 if on_left else 0
        long_at = 3 if on_left else 24
        other_at = 4 if on_left else 24
        low_col = 5 if on_left else 24
        for row in range(2):
            at = 17 * row
            field[2 * row + long, first + 5:first + 5 + rows, long_at:long_at + 5, :] = block[:, at:at + 5, :]
            field[2 * row + 1 - long, first + 5:first + 5 + rows, other_at:other_at + 4, :] = block[:, at + 5:at + 9, :]
            for col in range(2):
                fine[2 * row + col, fine_at:fine_at + n_fine, other_at:other_at + 4, :] = (
                    block[fine_rows, at + 9 + 4 * col:at + 13 + 4 * col, :])
        low[low_at:low_at + n_low, low_col:low_col + 3, :] = block[low_rows, 34:37, :]

    @pl.loop(0, 2)
    def _(half):
        for row in range(2):
            rows = pl.ds(half * 13, 13)
            even, odd = flat(field[2 * row, rows]), flat(field[2 * row + 1, rows])
            for at, part in enumerate((before(odd), even, odd, after(even))):
                cat[row, rows, :, 256 * at:256 * (at + 1)] = back_in_rows(part.astype(BF))

    @pl.loop(0, 3)
    def _(step):
        total = jnp.zeros((256, 256), F32)
        for row in range(2):
            for col in range(2):
                p = 2 * row + col
                value = flat(fine[p, pl.ds(step * 8, 8)])
                for a in range(3):
                    phase, shift = VARIANT[row + a]
                    cells = flat(cat[phase, pl.ds(step * 8 + 1 + shift, 8), :, 256 * col:256 * col + 768])
                    value = value + dot(cells, w_post[768 * a:768 * (a + 1)])
                fine[p, pl.ds(step * 8, 8)] = back_in_rows(value)
                total = total + value
        total = jnp.where(inside(place_ref, step * 8 - 4, 8), total * 0.25, 0.0)
        three_wide(total, pool_cat, step * 8, 8)

    @pl.loop(0, 2)
    def _(step):
        value = flat(low[pl.ds(step * 11, 11)])
        for a in range(3):
            value = value + dot(flat(pool_cat[pl.ds(step * 11 + a, 11)]), w_coarse[768 * a:768 * (a + 1)])
        value = jnp.where(inside(place_ref, step * 11 - 3, 11), value, 0.0)
        coarse[pl.ds(step * 11, 11)] = back_in_rows(value)
        three_wide(value, ctx_cat, step * 11, 11)

    for row in range(2):
        @pl.loop(0, 3)
        def _(step):
            valid = inside(place_ref, step * 7 - 2 - row, 7)
            pieces = []
            for col in range(2):
                prior = jnp.zeros((224, 512), F32)
                for k in range(2):
                    cells = flat(ctx_cat[pl.ds(step * 7 + k, 7), :, 256 * col:256 * col + 512])
                    prior = prior + dot(cells, fold[2 * row + k, 512 * col:512 * col + 512])
                raw = prior[:, 256:]
                small = jnp.exp(-jnp.abs(raw))
                more = 1.0 + small
                sigma = jnp.maximum(raw, 0.0) + jnp.log(more) + 0.5
                gate = jnp.where(raw >= 0.0, 1.0, small) / more
                inverse = 1.0 / sigma
                deviation = flat(fine[2 * row + col, pl.ds(step * 7 + 2 - row, 7)]) - prior[:, :256]
                residual = deviation * inverse * inverse
                err[2 * row + col, pl.ds(step * 7, 7)] = back_in_rows(residual)
                pieces.append(jnp.where(valid, -residual, 0.0))
                pieces.append(jnp.where(valid, (inverse - residual * deviation * inverse) * gate, 0.0))
            parts = (before(pieces[2]), before(pieces[3]), pieces[0], pieces[1], pieces[2], pieces[3],
                     after(pieces[0]), after(pieces[1]))
            for at, part in enumerate(parts):
                d_cat[row, pl.ds(step * 7, 7), :, 256 * at:256 * (at + 1)] = back_in_rows(part.astype(BF))

    for i in range(3):
        for j in range(3):
            turn[3 * i + j] = turned(ctx_cat[2 + i:18 + i, :, 256 * j:256 * (j + 1)])
    for j in range(2):
        rights = []
        for row in range(2):
            for col in range(2):
                rights.append(jnp.concatenate(
                    [own_cells(d_cat[row, 2 + row:18 + row, :, 512 * (1 + col) + 256 * j:512 * (1 + col) + 256 * (j + 1)])],
                    axis=1))
        right = jnp.concatenate(rights, axis=0)
        for a in range(3):
            for b in range(3):
                lefts = [turn[3 * ((row + a + 1) // 2) + (col + b + 1) // 2] for row in range(2) for col in range(2)]
                tap = 3 * a + b
                grads[0, 256 * tap:256 * (tap + 1), 256 * j:256 * (j + 1)] = (
                    dot(jnp.concatenate(lefts, axis=1), right) * scale).astype(BF)

    @pl.loop(0, 2)
    def _(step):
        value = flat(coarse[pl.ds(step * 10 + 1, 10)])
        for k in range(4):
            phase, shift = VARIANT[k]
            at = step * 10 + shift + phase
            value = value + dot(flat(d_cat[phase, pl.ds(at, 10)]), fold_t[k])
        value = jnp.where(inside(place_ref, step * 10 - 2, 10), value, 0.0)
        three_wide(value, gc_cat, step * 10, 10)

    right = own_cells(gc_cat[2:18, :, 256:512])
    for i in range(3):
        for j in range(3):
            left = turned(pool_cat[3 + i:19 + i, :, 256 * j:256 * (j + 1)])
            tap = 3 * i + j
            grads[1, 256 * tap:256 * (tap + 1), 0:256] = (dot(left, right) * scale).astype(BF)

    @pl.loop(0, 2)
    def _(step):
        value = jnp.zeros((288, 256), F32)
        for a in range(3):
            value = value + dot(flat(gc_cat[pl.ds(step * 9 + a, 9)]), w_coarse_t[768 * a:768 * (a + 1)])
        value = value * 0.25
        valid = inside(place_ref, step * 9 - 1, 9)
        for row in range(2):
            even, odd = [
                jnp.where(valid, flat(err[2 * row + col, pl.ds(step * 9 + 1 + row, 9)]) + value, 0.0)
                for col in range(2)
            ]
            for at, part in enumerate((before(odd), even, odd, after(even))):
                compact = part.reshape(9, 32, 256)[:, 8:24, :]
                gf_own[row, pl.ds(step * 9, 9), :, 256 * at:256 * (at + 1)] = compact.astype(BF)
    g_fine[...] = gf_own[...]

    for k in range(4):
        phase, shift = VARIANT[k]
        for at in range(4):
            turn[4 * k + at] = turned(cat[phase, 5 + shift:21 + shift, :, 256 * at:256 * (at + 1)])
    right = jnp.concatenate(
        [gf_own[row, 1:17, :, 256 * (1 + col):256 * (2 + col)].reshape(256, 256) for row in range(2) for col in range(2)],
        axis=0)
    for a in range(3):
        for b in range(3):
            lefts = [turn[4 * (row + a) + col + b] for row in range(2) for col in range(2)]
            tap = 3 * a + b
            grads[1, 256 * tap:256 * (tap + 1), 256:512] = (dot(jnp.concatenate(lefts, axis=1), right) * scale).astype(BF)


def feat_kernel(g_fine, w_post_t, out_ref, wide):
    for row in range(2):
        for col in range(2):
            value = jnp.zeros((256, 256), F32)
            for a in range(3):
                phase, shift = VARIANT[row + a]
                cells = g_fine[phase, 1 + shift:17 + shift, :, 256 * col:256 * col + 768].reshape(256, 768)
                value = value + dot(cells, w_post_t[768 * a:768 * (a + 1)])
            for half in range(2):
                wide[:, row, half, pl.ds(col, 16, stride=2), :] = (
                    value[:, 128 * half:128 * (half + 1)].reshape(16, 16, 128))
    for half in range(2):
        out_ref[:, :, :, 128 * half:128 * (half + 1)] = wide[:, :, half].astype(BF)


TAPS_OF = ((0,), (1, 2), (0, 1), (2,))


def weight_kernel(w_post, w_coarse, w_prior, fold, fold_t, w_post_t, w_coarse_t):
    for i in range(4):
        for j in range(4):
            taps = [3 * a + b for a in TAPS_OF[i] for b in TAPS_OF[j]]
            total = w_prior[256 * taps[0]:256 * (taps[0] + 1)].astype(F32)
            for tap in taps[1:]:
                total = total + w_prior[256 * tap:256 * (tap + 1)].astype(F32)
            total = total.astype(BF)
            fold[i, 256 * j:256 * (j + 1)] = total
            k, l = FOLD.index(i), FOLD.index(j)
            fold_t[k, 512 * l:512 * (l + 1)] = total.T
    for tap in range(9):
        w_coarse_t[256 * tap:256 * (tap + 1)] = w_coarse[256 * (8 - tap):256 * (9 - tap)].T
        w_post_t[256 * tap:256 * (tap + 1)] = w_post[256 * (8 - tap):256 * (9 - tap)].T


def sent(strip, down, right):
    pairs = [
        (r * 16 + c, (r + down) * 16 + c + right)
        for r in range(16) for c in range(16) if 0 <= r + down < 16 and 0 <= c + right < 16
    ]
    return lax.ppermute(strip, ("row", "col"), pairs)


def on_device(feat, noise_fine, noise_coarse, w_post, w_coarse, w_prior):
    scale = 1.0 / 512.0
    params = pltpu.CompilerParams(vmem_limit_bytes=VMEM_LIMIT)
    feat_rows = feat.reshape(16, 2, 32, 256)
    noise_rows = noise_fine.reshape(16, 2, 32, 256)
    own, top, bottom, left, right, lu, ld, ru, rd = pl.pallas_call(
        pack_kernel,
        out_shape=[
            jax.ShapeDtypeStruct((4, 16, 16, 256), BF),
            jax.ShapeDtypeStruct((37, 16, 256), BF),
            jax.ShapeDtypeStruct((37, 16, 256), BF),
            jax.ShapeDtypeStruct((16, 40, 256), BF),
            jax.ShapeDtypeStruct((16, 40, 256), BF),
        ] + [jax.ShapeDtypeStruct((5, 40, 256), BF)] * 4,
        in_specs=in_vmem(3),
        out_specs=in_vmem(9),
        scratch_shapes=[
            pltpu.VMEM((16, 2, 2, 32, 128), F32),
            pltpu.VMEM((16, 2, 2, 32, 128), F32),
            pltpu.VMEM((16, 40, 256), F32),
        ],
        compiler_params=params,
        name="pack",
    )(feat_rows, noise_rows, noise_coarse)
    from_up = sent(bottom, 1, 0)
    from_down = sent(top, -1, 0)
    from_left = sent(right, 0, 1)
    from_right = sent(left, 0, -1)
    from_ul = sent(rd, 1, 1)
    from_ur = sent(ld, 1, -1)
    from_dl = sent(ru, -1, 1)
    from_dr = sent(lu, -1, -1)
    fold, fold_t, w_post_t, w_coarse_t = pl.pallas_call(
        weight_kernel,
        out_shape=[
            jax.ShapeDtypeStruct((4, 1024, 512), BF),
            jax.ShapeDtypeStruct((4, 2048, 256), BF),
            jax.ShapeDtypeStruct((2304, 256), BF),
            jax.ShapeDtypeStruct((2304, 256), BF),
        ],
        in_specs=in_vmem(3),
        out_specs=in_vmem(4),
        compiler_params=params,
        cost_estimate=pl.CostEstimate(flops=10000000, bytes_accessed=15000000, transcendentals=0),
        name="weights",
    )(w_post, w_coarse, w_prior)
    place = jnp.stack([lax.axis_index("row"), lax.axis_index("col")]).astype(jnp.int32)
    grads, g_fine = pl.pallas_call(
        functools.partial(main_kernel, scale),
        out_shape=[
            jax.ShapeDtypeStruct((2, 2304, 512), BF),
            jax.ShapeDtypeStruct((2, 18, 16, 1024), BF),
        ],
        in_specs=[pl.BlockSpec(memory_space=pltpu.SMEM)] + in_vmem(16),
        out_specs=in_vmem(2),
        scratch_shapes=[
            pltpu.VMEM((4, 26, 32, 256), F32),
            pltpu.VMEM((4, 24, 32, 256), F32),
            pltpu.VMEM((16, 2, 2, 32, 128), F32),
            pltpu.VMEM((22, 32, 256), F32),
            pltpu.VMEM((2, 26, 32, 1024), BF),
            pltpu.VMEM((24, 32, 768), BF),
            pltpu.VMEM((22, 32, 256), F32),
            pltpu.VMEM((22, 32, 768), BF),
            pltpu.VMEM((4, 21, 32, 256), F32),
            pltpu.VMEM((2, 21, 32, 2048), BF),
            pltpu.VMEM((20, 32, 768), BF),
            pltpu.VMEM((2, 18, 16, 1024), BF),
            pltpu.VMEM((16, 256, 256), BF),
        ],
        compiler_params=params,
        name="tile",
    )(place, own, noise_rows, noise_coarse, from_up, from_down, from_left, from_right, from_ul, from_ur,
      from_dl, from_dr, w_post, w_coarse, fold, fold_t, w_coarse_t)
    grad_feat = pl.pallas_call(
        feat_kernel,
        out_shape=jax.ShapeDtypeStruct((16, 2, 32, 256), BF),
        in_specs=in_vmem(2),
        out_specs=pl.BlockSpec(memory_space=pltpu.VMEM),
        scratch_shapes=[pltpu.VMEM((16, 2, 2, 32, 128), F32)],
        compiler_params=params,
        cost_estimate=pl.CostEstimate(flops=1200000000, bytes_accessed=3000000, transcendentals=0),
        name="feat",
    )(g_fine, w_post_t).reshape(32, 32, 256)
    summed = reduce_scatter(grads)
    return grad_feat, summed[1, :, 256:].reshape(-1), summed[1, :, :256].reshape(-1), summed[0].reshape(-1)


def solution(mesh):
    return jax.shard_map(
        on_device,
        mesh=mesh,
        in_specs=(
            P("row", "col", None),
            P("row", "col", None),
            P("row", "col", None),
            P(),
            P(),
            P(),
        ),
        out_specs=(P("row", "col", None), P(("row", "col")), P(("row", "col")), P(("row", "col"))),
        check_vma=False,
    )
```

```python
import functools
import math

import jax
import jax.numpy as jnp
from jax import lax
from jax.experimental import pallas as pl
from jax.experimental.pallas import tpu as pltpu
from jax.sharding import PartitionSpec as P

BF = jnp.bfloat16
F32 = jnp.float32
VARIANT = ((1, -1), (0, 0), (1, 0), (0, 1))
FOLD = (3, 1, 2, 0)
VMEM_LIMIT = 60 * 1024 * 1024


def digits():
    places = []
    for d in range(256):
        row, col = d // 16, d % 16
        places.append({"zl": row // 4, "x": row % 4, "zh": col // 8, "y": (col // 2) % 4, "core": col % 2})
    return places


def index_of(place):
    return (place["zl"] * 4 + place["x"]) * 16 + (place["zh"] * 4 + place["y"]) * 2 + place["core"]


def my_place():
    row, col = lax.axis_index("row"), lax.axis_index("col")
    return {"zl": row // 4, "x": row % 4, "zh": col // 8, "y": (col // 2) % 4, "core": col % 2}


def flipped(place, name, bits):
    return {**place, name: place[name] ^ bits}


def sum_stage(part, name, dim):
    here = my_place()[name]
    arrived = []
    for bits in (1, 3, 2):
        piece = lax.dynamic_index_in_dim(part, here ^ bits, dim, keepdims=False)
        pairs = [(index_of(p), index_of(flipped(p, name, bits))) for p in digits()]
        arrived.append(lax.ppermute(piece, ("row", "col"), pairs))
    total = lax.dynamic_index_in_dim(part, here, dim, keepdims=False).astype(F32)
    for piece in arrived:
        total = total + piece.astype(F32)
    return total.astype(BF)


def reduce_scatter(parts):
    pairs = [(index_of(p), index_of(flipped(p, "core", 1))) for p in digits()]
    other = lax.ppermute(parts[1], ("row", "col"), pairs)
    parts = (parts[0].astype(F32) + other.astype(F32)).astype(BF)
    first = parts[0].reshape(4, 4, 72, 512)
    second = parts[1].reshape(4, 4, 72, 512)
    first, second = sum_stage(first, "x", 0), sum_stage(second, "y", 1)
    first, second = sum_stage(first, "y", 0), sum_stage(second, "x", 0)
    parts = sum_stage(jnp.stack([first, second]).reshape(2, 4, 18, 512), "zl", 1)
    halves = parts.reshape(2, 2, 9, 512)
    last = my_place()["zh"]
    total = 0.0
    for flip in (0, 1):
        pairs = []
        for p in digits():
            chunk = (((p["core"] * 4 + p["x"]) * 4 + p["y"]) * 4 + p["zl"]) * 2 + (p["zh"] + flip) % 2
            pairs.append((index_of(p), chunk))
        piece = lax.dynamic_index_in_dim(halves, (last + flip) % 2, 1, keepdims=False)
        total = total + lax.ppermute(piece, ("row", "col"), pairs).astype(F32)
    return total


def in_vmem(count):
    return [pl.BlockSpec(memory_space=pltpu.VMEM)] * count


def split_lanes(ref, value):
    for half in range(2):
        ref[:, :, half] = value[..., 128 * half:128 * (half + 1)]


def phase_of(ref, row, col):
    return jnp.concatenate([ref[:, row, half, pl.ds(col, 16, stride=2), :] for half in range(2)], axis=-1)


def line_of(ref, line, col):
    return jnp.concatenate(
        [ref[line // 2, line % 2, half, pl.ds(col, 16, stride=2), :] for half in range(2)], axis=-1)


def split_lanes(ref, value):
    for half in range(2):
        ref[:, :, half] = value[..., 128 * half:128 * (half + 1)]


def phase_of(ref, row, col):
    return jnp.concatenate([ref[:, row, half, pl.ds(col, 16, stride=2), :] for half in range(2)], axis=-1)


def first_kernel(feat_ref, fine_ref, low_ref, w_post, own_ref, part_ref, top_ref, bottom_ref,
                 wide, noise, field, cat, spill):
    split_lanes(wide, feat_ref[...].astype(F32))
    split_lanes(noise, fine_ref[...])
    field[...] = jnp.zeros(field.shape, F32)
    for row in range(2):
        for col in range(2):
            cells = phase_of(wide, row, col)
            own_ref[2 * row + col] = cells.astype(BF)
            field[col, 1:17, 8:24, :] = cells
        even, odd = flat(field[0]), flat(field[1])
        for at, part in enumerate((before(odd), even, odd, after(even))):
            cat[row, :, :, 256 * at:256 * (at + 1)] = back_in_rows(part.astype(BF))
    for row in range(2):
        for col in range(2):
            value = jnp.zeros((544, 256), F32)
            for a in range(3):
                phase, shift = VARIANT[row + a]
                at = 1 + shift - row
                cells = flat(cat[phase, at:at + 17, :, 256 * col:256 * col + 768])
                value = value + dot(cells, w_post[768 * a:768 * (a + 1)])
            part_ref[2 * row + col] = back_in_rows(value)
            part_ref[2 * row + col, row:row + 16, 8:24, :] += phase_of(noise, row, col)
    spill[...] = jnp.zeros(spill.shape, F32)
    for out, first, low_first in ((top_ref, -1, 0), (bottom_ref, 24, 13)):
        for r in range(9):
            line = first + r
            row = line % 2
            at = line // 2 + row
            for col in range(2):
                e = 2 * r + col
                out[e] = part_ref[2 * row + col, at, 8:24, :].astype(BF)
                edge = 7 if col else 24
                spill[e:e + 1, :] = part_ref[2 * row + col, at, edge:edge + 1, :]
        out[18:21] = low_ref[low_first:low_first + 3].astype(BF)
        out[21:23] = spill[...].reshape(2, 16, 256).astype(BF)


def middle_kernel(part_ref, low_ref, up_ref, down_ref, left_ref, right_ref, side, spill):
    lows = ((4, low_ref[...]), (1, up_ref[18:21].astype(F32)), (20, down_ref[18:21].astype(F32)))
    for out, long, long_from, other_from, low_from in ((left_ref, 1, -1, 0, 0), (right_ref, 0, 12, 12, 13)):
        side[...] = jnp.zeros(side.shape, F32)
        for row in range(2):
            at = 9 * row
            rows = slice(4 - row, 21 - row)
            side[rows, at:at + 5, :] = part_ref[2 * row + long, :, 8 + long_from:13 + long_from, :]
            side[rows, at + 5:at + 9, :] = part_ref[2 * row + 1 - long, :, 8 + other_from:12 + other_from, :]
        for ref, first in ((up_ref, -8), (down_ref, 31)):
            spill[...] = ref[21:23].astype(F32).reshape(32, 256)
            for r in range(9):
                line = first + r
                row = line % 2
                here, at = line // 2 + 4, 9 * row
                cells = ref[2 * r + long].astype(F32)
                end = spill[2 * r + long:2 * r + long + 1, :]
                if long:
                    side[here, at:at + 1, :] += end
                    side[here, at + 1:at + 5, :] += cells[0:4]
                else:
                    side[here, at:at + 4, :] += cells[12:16]
                    side[here, at + 4:at + 5, :] += end
                side[here, at + 5:at + 9, :] += ref[2 * r + 1 - long].astype(F32)[other_from:other_from + 4]
        for here, block in lows:
            side[here:here + block.shape[0], 18:21, :] = block[:, low_from:low_from + 3, :]
        out[...] = side[...].astype(BF)


def flat(block):
    return block.reshape(block.shape[0] * 32, block.shape[2])


def back_in_rows(block):
    return block.reshape(block.shape[0] // 32, 32, block.shape[1])


def before(block):
    return pltpu.roll(block, 1, 0)


def after(block):
    return pltpu.roll(block, block.shape[0] - 1, 0)


def dot(left, right):
    return jnp.dot(left, right, preferred_element_type=F32)


def inside(place_ref, first_row, rows):
    cell = lax.broadcasted_iota(jnp.int32, (rows * 32, 256), 0)
    line = cell // 32 + first_row + 16 * place_ref[0]
    column = cell % 32 - 8 + 16 * place_ref[1]
    return (line >= 0) & (line < 256) & (column >= 0) & (column < 256)


def three_wide(value, ref, first, rows):
    c = value.shape[1]
    for at, part in enumerate((before(value), value, after(value))):
        ref[pl.ds(first, rows), :, c * at:c * (at + 1)] = back_in_rows(part.astype(BF))


def own_cells(block):
    return block.astype(F32)[:, 8:24, :].reshape(256, block.shape[2]).astype(BF)


def turned(block):
    return own_cells(block).T


def main_kernel(scale, place_ref, own_ref, part_ref, low_ref, up_ref, down_ref, left_ref, right_ref,
                w_coarse, fold, fold_t, w_coarse_t, grads, g_fine,
                fine, low, pool_cat, coarse, ctx_cat, err, d_cat, d_own, gc_cat, gc_own, spill):
    def put(which, tap, lanes, value):
        value = (value * scale).astype(BF)
        for half, first, start, stop in ((0, 256 * tap, 0, 256), (1, 256 * tap - 1152, 0, 256)):
            start, stop = max(start, -first), min(stop, 1152 - first)
            if start < stop:
                slot = (place_ref[2] + half) % 2
                grads[slot, which, first + start:first + stop, lanes] = value[start:stop]

    fine[...] = jnp.zeros(fine.shape, F32)
    for row in range(2):
        for col in range(2):
            fine[2 * row + col, 4 - row:21 - row] = part_ref[2 * row + col]
    low[3:19, 8:24, :] = low_ref[...]
    for ref, first, low_first in ((up_ref, -8, 0), (down_ref, 31, 19)):
        spill[...] = ref[21:23].astype(F32).reshape(32, 256)
        for r in range(9):
            line = first + r
            for col in range(2):
                e = 2 * r + col
                edge = 7 if col else 24
                fine[2 * (line % 2) + col, line // 2 + 4, 8:24, :] += ref[e].astype(F32)
                fine[2 * (line % 2) + col, line // 2 + 4, edge:edge + 1, :] += spill[e:e + 1, :]
        low[low_first:low_first + 3, 8:24, :] = ref[18:21].astype(F32)
    for ref, long, long_at, other_at, low_at in ((left_ref, 0, 4, 4, 5), (right_ref, 1, 23, 24, 24)):
        block = ref[...].astype(F32)
        for row in range(2):
            at = 9 * row
            fine[2 * row + long, :, long_at:long_at + 5, :] += block[:, at:at + 5, :]
            fine[2 * row + 1 - long, :, other_at:other_at + 4, :] += block[:, at + 5:at + 9, :]
        low[:, low_at:low_at + 3, :] = block[1:23, 18:21, :]

    @pl.loop(0, 3)
    def _(step):
        total = flat(fine[0, pl.ds(step * 8, 8)])
        for p in range(1, 4):
            total = total + flat(fine[p, pl.ds(step * 8, 8)])
        total = jnp.where(inside(place_ref, step * 8 - 4, 8), total * 0.25, 0.0)
        three_wide(total, pool_cat, step * 8, 8)

    @pl.loop(0, 2)
    def _(step):
        value = flat(low[pl.ds(step * 11, 11)])
        for a in range(3):
            value = value + dot(flat(pool_cat[pl.ds(step * 11 + a, 11)]), w_coarse[768 * a:768 * (a + 1)])
        value = jnp.where(inside(place_ref, step * 11 - 3, 11), value, 0.0)
        coarse[pl.ds(step * 11, 11)] = back_in_rows(value)
        three_wide(value, ctx_cat, step * 11, 11)

    for row in range(2):
        @pl.loop(0, 3)
        def _(step):
            valid = inside(place_ref, step * 7 - 2 - row, 7)
            pieces = []
            for col in range(2):
                prior = jnp.zeros((224, 512), F32)
                for k in range(2):
                    cells = flat(ctx_cat[pl.ds(step * 7 + k, 7), :, 256 * col:256 * col + 512])
                    prior = prior + dot(cells, fold[2 * row + k, 512 * col:512 * col + 512])
                raw = prior[:, 256:]
                small = jnp.exp(-jnp.abs(raw))
                more = 1.0 + small
                sigma = jnp.maximum(raw, 0.0) + jnp.log(more) + 0.5
                gate = jnp.where(raw >= 0.0, 1.0, small) / more
                inverse = 1.0 / sigma
                deviation = flat(fine[2 * row + col, pl.ds(step * 7 + 2 - row, 7)]) - prior[:, :256]
                residual = deviation * inverse * inverse
                err[2 * row + col, pl.ds(step * 7, 7)] = back_in_rows(residual)
                pieces.append(jnp.where(valid, -residual, 0.0))
                pieces.append(jnp.where(valid, (inverse - residual * deviation * inverse) * gate, 0.0))
            parts = (before(pieces[2]), before(pieces[3]), pieces[0], pieces[1], pieces[2], pieces[3],
                     after(pieces[0]), after(pieces[1]))
            for at, part in enumerate(parts):
                part = back_in_rows(part)
                d_cat[row, pl.ds(step * 7, 7), :, 256 * at:256 * (at + 1)] = part.astype(BF)
                d_own[row, pl.ds(step * 7, 7), :, 256 * at:256 * (at + 1)] = part[:, 8:24, :].astype(BF)

    left = turned(ctx_cat[3:19, :, 256:512])
    left = jnp.concatenate([left] * 4, axis=1)
    for a in range(3):
        for b in range(3):
            rights = []
            for k in (2 - a, 3 - a):
                phase, shift = VARIANT[k]
                at = 2 + phase + shift
                for l in (2 - b, 3 - b):
                    rights.append(d_own[phase, at:at + 16, :, 512 * l:512 * (l + 1)].reshape(256, 512))
            put(0, 3 * a + b, slice(0, 512), dot(left, jnp.concatenate(rights, axis=0)))

    @pl.loop(0, 2)
    def _(step):
        value = flat(coarse[pl.ds(step * 10 + 1, 10)])
        for k in range(4):
            phase, shift = VARIANT[k]
            at = step * 10 + shift + phase
            value = value + dot(flat(d_cat[phase, pl.ds(at, 10)]), fold_t[k])
        value = jnp.where(inside(place_ref, step * 10 - 2, 10), value, 0.0)
        three_wide(value, gc_cat, step * 10, 10)
        for at, part in enumerate((before(value), value, after(value))):
            gc_own[pl.ds(step * 10, 10), :, 256 * at:256 * (at + 1)] = back_in_rows(part)[:, 8:24, :].astype(BF)

    left = turned(pool_cat[4:20, :, 256:512])
    for a in range(3):
        for b in range(3):
            right = gc_own[3 - a:19 - a, :, 256 * (2 - b):256 * (3 - b)].reshape(256, 256)
            put(1, 3 * a + b, slice(0, 256), dot(left, right))

    @pl.loop(0, 2)
    def _(step):
        value = jnp.zeros((288, 256), F32)
        for a in range(3):
            value = value + dot(flat(gc_cat[pl.ds(step * 9 + a, 9)]), w_coarse_t[768 * a:768 * (a + 1)])
        value = value * 0.25
        valid = inside(place_ref, step * 9 - 1, 9)
        for row in range(2):
            even, odd = [
                jnp.where(valid, flat(err[2 * row + col, pl.ds(step * 9 + 1 + row, 9)]) + value, 0.0)
                for col in range(2)
            ]
            for at, part in enumerate((before(odd), even, odd, after(even))):
                compact = part.reshape(9, 32, 256)[:, 8:24, :]
                g_fine[row, pl.ds(step * 9, 9), :, 256 * at:256 * (at + 1)] = compact.astype(BF)

    left = jnp.concatenate([own_ref[p].reshape(256, 256).T for p in range(4)], axis=1)
    for a in range(3):
        for b in range(3):
            rights = []
            for row in range(2):
                phase, shift = VARIANT[row + 2 - a]
                for col in range(2):
                    at = col + 2 - b
                    rights.append(g_fine[phase, 1 + shift:17 + shift, :, 256 * at:256 * (at + 1)].reshape(256, 256))
            put(1, 3 * a + b, slice(256, 512), dot(left, jnp.concatenate(rights, axis=0)))


def feat_kernel(g_fine, w_post_t, out_ref, wide):
    for row in range(2):
        for col in range(2):
            value = jnp.zeros((256, 256), F32)
            for a in range(3):
                phase, shift = VARIANT[row + a]
                cells = g_fine[phase, 1 + shift:17 + shift, :, 256 * col:256 * col + 768].reshape(256, 768)
                value = value + dot(cells, w_post_t[768 * a:768 * (a + 1)])
            for half in range(2):
                wide[:, row, half, pl.ds(col, 16, stride=2), :] = (
                    value[:, 128 * half:128 * (half + 1)].reshape(16, 16, 128))
    for half in range(2):
        out_ref[:, :, :, 128 * half:128 * (half + 1)] = wide[:, :, half].astype(BF)


TAPS_OF = ((0,), (1, 2), (0, 1), (2,))


def weight_kernel(w_post, w_coarse, w_prior, fold, fold_t, w_post_t, w_coarse_t):
    for i in range(4):
        for j in range(4):
            taps = [3 * a + b for a in TAPS_OF[i] for b in TAPS_OF[j]]
            total = w_prior[256 * taps[0]:256 * (taps[0] + 1)].astype(F32)
            for tap in taps[1:]:
                total = total + w_prior[256 * tap:256 * (tap + 1)].astype(F32)
            total = total.astype(BF)
            fold[i, 256 * j:256 * (j + 1)] = total
            k, l = FOLD.index(i), FOLD.index(j)
            fold_t[k, 512 * l:512 * (l + 1)] = total.T
    for tap in range(9):
        w_coarse_t[256 * tap:256 * (tap + 1)] = w_coarse[256 * (8 - tap):256 * (9 - tap)].T
        w_post_t[256 * tap:256 * (tap + 1)] = w_post[256 * (8 - tap):256 * (9 - tap)].T


def sent(strip, down, right):
    pairs = [
        (r * 16 + c, (r + down) * 16 + c + right)
        for r in range(16) for c in range(16) if 0 <= r + down < 16 and 0 <= c + right < 16
    ]
    return lax.ppermute(strip, ("row", "col"), pairs)


def on_device(feat, noise_fine, noise_coarse, w_post, w_coarse, w_prior):
    scale = 1.0 / 512.0
    params = pltpu.CompilerParams(vmem_limit_bytes=VMEM_LIMIT)
    own, part, top, bottom = pl.pallas_call(
        first_kernel,
        out_shape=[
            jax.ShapeDtypeStruct((4, 16, 16, 256), BF),
            jax.ShapeDtypeStruct((4, 17, 32, 256), F32),
            jax.ShapeDtypeStruct((23, 16, 256), BF),
            jax.ShapeDtypeStruct((23, 16, 256), BF),
        ],
        in_specs=in_vmem(4),
        out_specs=in_vmem(4),
        scratch_shapes=[
            pltpu.VMEM((16, 2, 2, 32, 128), F32),
            pltpu.VMEM((16, 2, 2, 32, 128), F32),
            pltpu.VMEM((2, 18, 32, 256), F32),
            pltpu.VMEM((2, 18, 32, 1024), BF),
            pltpu.VMEM((32, 256), F32),
        ],
        compiler_params=params,
        name="first",
    )(feat.reshape(16, 2, 32, 256), noise_fine.reshape(16, 2, 32, 256), noise_coarse, w_post)
    from_up, from_down = sent(bottom, 1, 0), sent(top, -1, 0)
    fold, fold_t, w_post_t, w_coarse_t = pl.pallas_call(
        weight_kernel,
        out_shape=[
            jax.ShapeDtypeStruct((4, 1024, 512), BF),
            jax.ShapeDtypeStruct((4, 2048, 256), BF),
            jax.ShapeDtypeStruct((2304, 256), BF),
            jax.ShapeDtypeStruct((2304, 256), BF),
        ],
        in_specs=in_vmem(3),
        out_specs=in_vmem(4),
        compiler_params=params,
        cost_estimate=pl.CostEstimate(flops=10000000, bytes_accessed=15000000, transcendentals=0),
        name="weights",
    )(w_post, w_coarse, w_prior)
    left, right = pl.pallas_call(
        middle_kernel,
        out_shape=[jax.ShapeDtypeStruct((24, 24, 256), BF)] * 2,
        in_specs=in_vmem(4),
        out_specs=in_vmem(2),
        scratch_shapes=[pltpu.VMEM((24, 24, 256), F32), pltpu.VMEM((32, 256), F32)],
        compiler_params=params,
        name="middle",
    )(part, noise_coarse, from_up, from_down)
    from_left, from_right = sent(right, 0, 1), sent(left, 0, -1)
    row, col = lax.axis_index("row"), lax.axis_index("col")
    place = jnp.stack([row, col, col % 2]).astype(jnp.int32)
    grads, g_fine = pl.pallas_call(
        functools.partial(main_kernel, scale),
        out_shape=[
            jax.ShapeDtypeStruct((2, 2, 1152, 512), BF),
            jax.ShapeDtypeStruct((2, 18, 16, 1024), BF),
        ],
        in_specs=[pl.BlockSpec(memory_space=pltpu.SMEM)] + in_vmem(11),
        out_specs=in_vmem(2),
        scratch_shapes=[
            pltpu.VMEM((4, 24, 32, 256), F32),
            pltpu.VMEM((22, 32, 256), F32),
            pltpu.VMEM((24, 32, 768), BF),
            pltpu.VMEM((22, 32, 256), F32),
            pltpu.VMEM((22, 32, 768), BF),
            pltpu.VMEM((4, 21, 32, 256), F32),
            pltpu.VMEM((2, 21, 32, 2048), BF),
            pltpu.VMEM((2, 21, 16, 2048), BF),
            pltpu.VMEM((20, 32, 768), BF),
            pltpu.VMEM((20, 16, 768), BF),
            pltpu.VMEM((32, 256), F32),
        ],
        compiler_params=params,
        name="tile",
    )(place, own, part, noise_coarse, from_up, from_down, from_left, from_right,
      w_coarse, fold, fold_t, w_coarse_t)
    grad_feat = pl.pallas_call(
        feat_kernel,
        out_shape=jax.ShapeDtypeStruct((16, 2, 32, 256), BF),
        in_specs=in_vmem(2),
        out_specs=pl.BlockSpec(memory_space=pltpu.VMEM),
        scratch_shapes=[pltpu.VMEM((16, 2, 2, 32, 128), F32)],
        compiler_params=params,
        cost_estimate=pl.CostEstimate(flops=1200000000, bytes_accessed=3000000, transcendentals=0),
        name="feat",
    )(g_fine, w_post_t).reshape(32, 32, 256)
    summed = reduce_scatter(grads)
    return grad_feat, summed[1, :, 256:].reshape(-1), summed[1, :, :256].reshape(-1), summed[0].reshape(-1)


def solution(mesh):
    return jax.shard_map(
        on_device,
        mesh=mesh,
        in_specs=(
            P("row", "col", None),
            P("row", "col", None),
            P("row", "col", None),
            P(),
            P(),
            P(),
        ),
        out_specs=(P("row", "col", None), P(("row", "col")), P(("row", "col")), P(("row", "col"))),
        check_vma=False,
    )
```

```python
import functools
import math

import jax
import jax.numpy as jnp
from jax import lax
from jax.experimental import pallas as pl
from jax.experimental.pallas import tpu as pltpu
from jax.sharding import PartitionSpec as P

BF = jnp.bfloat16
F32 = jnp.float32
VARIANT = ((1, -1), (0, 0), (1, 0), (0, 1))
FOLD = (3, 1, 2, 0)


def digits():
    places = []
    for d in range(256):
        row, col = d // 16, d % 16
        places.append({"zl": row // 4, "x": row % 4, "zh": col // 8, "y": (col // 2) % 4, "core": col % 2})
    return places


def index_of(place):
    return (place["zl"] * 4 + place["x"]) * 16 + (place["zh"] * 4 + place["y"]) * 2 + place["core"]


def my_place():
    row, col = lax.axis_index("row"), lax.axis_index("col")
    return {"zl": row // 4, "x": row % 4, "zh": col // 8, "y": (col // 2) % 4, "core": col % 2}


def flipped(place, name, bits):
    return {**place, name: place[name] ^ bits}


def sum_stage(part, name, dim):
    here = my_place()[name]
    arrived = []
    for bits in (1, 3, 2):
        piece = lax.dynamic_index_in_dim(part, here ^ bits, dim, keepdims=False)
        pairs = [(index_of(p), index_of(flipped(p, name, bits))) for p in digits()]
        arrived.append(lax.ppermute(piece, ("row", "col"), pairs))
    total = lax.dynamic_index_in_dim(part, here, dim, keepdims=False).astype(F32)
    for piece in arrived:
        total = total + piece.astype(F32)
    return total.astype(BF)


def reduce_scatter(parts, beside):
    pairs = [(index_of(p), index_of(flipped(p, "core", 1))) for p in digits()]
    other, beside = lax.optimization_barrier((lax.ppermute(parts[1], ("row", "col"), pairs), beside))
    parts = (parts[0].astype(F32) + other.astype(F32)).astype(BF)
    first = parts[0].reshape(4, 4, 72, 512)
    second = parts[1].reshape(4, 4, 72, 512)
    first, second = sum_stage(first, "x", 0), sum_stage(second, "y", 1)
    first, second = sum_stage(first, "y", 0), sum_stage(second, "x", 0)
    parts = sum_stage(jnp.stack([first, second]).reshape(2, 4, 18, 512), "zl", 1)
    halves = parts.reshape(2, 2, 9, 512)
    last = my_place()["zh"]
    total = 0.0
    for flip in (0, 1):
        pairs = []
        for p in digits():
            chunk = (((p["core"] * 4 + p["x"]) * 4 + p["y"]) * 4 + p["zl"]) * 2 + (p["zh"] + flip) % 2
            pairs.append((index_of(p), chunk))
        piece = lax.dynamic_index_in_dim(halves, (last + flip) % 2, 1, keepdims=False)
        total = total + lax.ppermute(piece, ("row", "col"), pairs).astype(F32)
    return total, beside


def room(mib):
    return pltpu.CompilerParams(vmem_limit_bytes=mib * 1024 * 1024)


def in_vmem(count):
    return [pl.BlockSpec(memory_space=pltpu.VMEM)] * count


def split_lanes(ref, value):
    for half in range(2):
        ref[:, :, half] = value[..., 128 * half:128 * (half + 1)]


def phase_of(ref, row, col):
    return jnp.concatenate([ref[:, row, half, pl.ds(col, 16, stride=2), :] for half in range(2)], axis=-1)


def line_of(ref, line, col):
    return jnp.concatenate(
        [ref[line // 2, line % 2, half, pl.ds(col, 16, stride=2), :] for half in range(2)], axis=-1)


def split_lanes(ref, value):
    for half in range(2):
        ref[:, :, half] = value[..., 128 * half:128 * (half + 1)]


def phase_of(ref, row, col):
    return jnp.concatenate([ref[:, row, half, pl.ds(col, 16, stride=2), :] for half in range(2)], axis=-1)


def first_kernel(feat_ref, fine_ref, low_ref, w_post, own_ref, part_ref, top_ref, bottom_ref,
                 wide, noise, field, cat, spill):
    split_lanes(wide, feat_ref[...].astype(F32))
    split_lanes(noise, fine_ref[...])
    field[...] = jnp.zeros(field.shape, F32)
    for row in range(2):
        for col in range(2):
            cells = phase_of(wide, row, col)
            own_ref[2 * row + col] = cells.astype(BF)
            field[col, 1:17, 8:24, :] = cells
        even, odd = flat(field[0]), flat(field[1])
        for at, part in enumerate((before(odd), even, odd, after(even))):
            cat[row, :, :, 256 * at:256 * (at + 1)] = back_in_rows(part.astype(BF))
    for row in range(2):
        for col in range(2):
            value = jnp.zeros((544, 256), F32)
            for a in range(3):
                phase, shift = VARIANT[row + a]
                at = 1 + shift - row
                cells = flat(cat[phase, at:at + 17, :, 256 * col:256 * col + 768])
                value = value + dot(cells, w_post[768 * a:768 * (a + 1)])
            part_ref[2 * row + col] = back_in_rows(value)
            part_ref[2 * row + col, row:row + 16, 8:24, :] += phase_of(noise, row, col)
    spill[...] = jnp.zeros(spill.shape, F32)
    for out, first, low_first in ((top_ref, -1, 0), (bottom_ref, 24, 13)):
        for r in range(9):
            line = first + r
            row = line % 2
            at = line // 2 + row
            for col in range(2):
                e = 2 * r + col
                out[e] = part_ref[2 * row + col, at, 8:24, :].astype(BF)
                edge = 7 if col else 24
                spill[e:e + 1, :] = part_ref[2 * row + col, at, edge:edge + 1, :]
        out[18:21] = low_ref[low_first:low_first + 3].astype(BF)
        out[21:23] = spill[...].reshape(2, 16, 256).astype(BF)


def middle_kernel(part_ref, low_ref, up_ref, down_ref, left_ref, right_ref, side, spill):
    lows = ((4, low_ref[...]), (1, up_ref[18:21].astype(F32)), (20, down_ref[18:21].astype(F32)))
    for out, long, long_from, other_from, low_from in ((left_ref, 1, -1, 0, 0), (right_ref, 0, 12, 12, 13)):
        side[...] = jnp.zeros(side.shape, F32)
        for row in range(2):
            at = 9 * row
            rows = slice(4 - row, 21 - row)
            side[rows, at:at + 5, :] = part_ref[2 * row + long, :, 8 + long_from:13 + long_from, :]
            side[rows, at + 5:at + 9, :] = part_ref[2 * row + 1 - long, :, 8 + other_from:12 + other_from, :]
        for ref, first in ((up_ref, -8), (down_ref, 31)):
            spill[...] = ref[21:23].astype(F32).reshape(32, 256)
            for r in range(9):
                line = first + r
                row = line % 2
                here, at = line // 2 + 4, 9 * row
                cells = ref[2 * r + long].astype(F32)
                end = spill[2 * r + long:2 * r + long + 1, :]
                if long:
                    side[here, at:at + 1, :] += end
                    side[here, at + 1:at + 5, :] += cells[0:4]
                else:
                    side[here, at:at + 4, :] += cells[12:16]
                    side[here, at + 4:at + 5, :] += end
                side[here, at + 5:at + 9, :] += ref[2 * r + 1 - long].astype(F32)[other_from:other_from + 4]
        for here, block in lows:
            side[here:here + block.shape[0], 18:21, :] = block[:, low_from:low_from + 3, :]
        out[...] = side[...].astype(BF)


def flat(block):
    return block.reshape(block.shape[0] * 32, block.shape[2])


def back_in_rows(block):
    return block.reshape(block.shape[0] // 32, 32, block.shape[1])


def before(block):
    return pltpu.roll(block, 1, 0)


def after(block):
    return pltpu.roll(block, block.shape[0] - 1, 0)


def dot(left, right):
    return jnp.dot(left, right, preferred_element_type=F32)


def inside(place_ref, first_row, rows):
    cell = lax.broadcasted_iota(jnp.int32, (rows * 32, 256), 0)
    line = cell // 32 + first_row + 16 * place_ref[0]
    column = cell % 32 - 8 + 16 * place_ref[1]
    return (line >= 0) & (line < 256) & (column >= 0) & (column < 256)


def three_wide(value, ref, first, rows):
    c = value.shape[1]
    for at, part in enumerate((before(value), value, after(value))):
        ref[pl.ds(first, rows), :, c * at:c * (at + 1)] = back_in_rows(part.astype(BF))


def own_cells(block):
    return block.astype(F32)[:, 8:24, :].reshape(256, block.shape[2]).astype(BF)


def turned(block):
    return own_cells(block).T


def main_kernel(scale, place_ref, own_ref, part_ref, low_ref, up_ref, down_ref, left_ref, right_ref,
                w_coarse, fold, fold_t, w_coarse_t, grads, g_fine,
                fine, low, pool_cat, coarse, ctx_cat, err, d_cat, d_own, gc_cat, gc_own, spill):
    def put(which, tap, lanes, value):
        value = (value * scale).astype(BF)
        for half, first, start, stop in ((0, 256 * tap, 0, 256), (1, 256 * tap - 1152, 0, 256)):
            start, stop = max(start, -first), min(stop, 1152 - first)
            if start < stop:
                slot = (place_ref[2] + half) % 2
                grads[slot, which, first + start:first + stop, lanes] = value[start:stop]

    fine[...] = jnp.zeros(fine.shape, F32)
    for row in range(2):
        for col in range(2):
            fine[2 * row + col, 4 - row:21 - row] = part_ref[2 * row + col]
    low[3:19, 8:24, :] = low_ref[...]
    for ref, first, low_first in ((up_ref, -8, 0), (down_ref, 31, 19)):
        spill[...] = ref[21:23].astype(F32).reshape(32, 256)
        for r in range(9):
            line = first + r
            for col in range(2):
                e = 2 * r + col
                edge = 7 if col else 24
                fine[2 * (line % 2) + col, line // 2 + 4, 8:24, :] += ref[e].astype(F32)
                fine[2 * (line % 2) + col, line // 2 + 4, edge:edge + 1, :] += spill[e:e + 1, :]
        low[low_first:low_first + 3, 8:24, :] = ref[18:21].astype(F32)
    for ref, long, long_at, other_at, low_at in ((left_ref, 0, 4, 4, 5), (right_ref, 1, 23, 24, 24)):
        block = ref[...].astype(F32)
        for row in range(2):
            at = 9 * row
            fine[2 * row + long, :, long_at:long_at + 5, :] += block[:, at:at + 5, :]
            fine[2 * row + 1 - long, :, other_at:other_at + 4, :] += block[:, at + 5:at + 9, :]
        low[:, low_at:low_at + 3, :] = block[1:23, 18:21, :]

    @pl.loop(0, 3)
    def _(step):
        total = flat(fine[0, pl.ds(step * 8, 8)])
        for p in range(1, 4):
            total = total + flat(fine[p, pl.ds(step * 8, 8)])
        total = jnp.where(inside(place_ref, step * 8 - 4, 8), total * 0.25, 0.0)
        three_wide(total, pool_cat, step * 8, 8)

    @pl.loop(0, 2)
    def _(step):
        value = flat(low[pl.ds(step * 11, 11)])
        for a in range(3):
            value = value + dot(flat(pool_cat[pl.ds(step * 11 + a, 11)]), w_coarse[768 * a:768 * (a + 1)])
        value = jnp.where(inside(place_ref, step * 11 - 3, 11), value, 0.0)
        coarse[pl.ds(step * 11, 11)] = back_in_rows(value)
        three_wide(value, ctx_cat, step * 11, 11)

    for row in range(2):
        @pl.loop(0, 3)
        def _(step):
            valid = inside(place_ref, step * 7 - 2 - row, 7)
            pieces = []
            for col in range(2):
                prior = jnp.zeros((224, 512), F32)
                for k in range(2):
                    cells = flat(ctx_cat[pl.ds(step * 7 + k, 7), :, 256 * col:256 * col + 512])
                    prior = prior + dot(cells, fold[2 * row + k, 512 * col:512 * col + 512])
                raw = prior[:, 256:]
                small = jnp.exp(-jnp.abs(raw))
                more = 1.0 + small
                sigma = jnp.maximum(raw, 0.0) + jnp.log(more) + 0.5
                gate = jnp.where(raw >= 0.0, 1.0, small) / more
                inverse = 1.0 / sigma
                deviation = flat(fine[2 * row + col, pl.ds(step * 7 + 2 - row, 7)]) - prior[:, :256]
                residual = deviation * inverse * inverse
                err[2 * row + col, pl.ds(step * 7, 7)] = back_in_rows(residual)
                pieces.append(jnp.where(valid, -residual, 0.0))
                pieces.append(jnp.where(valid, (inverse - residual * deviation * inverse) * gate, 0.0))
            parts = (before(pieces[2]), before(pieces[3]), pieces[0], pieces[1], pieces[2], pieces[3],
                     after(pieces[0]), after(pieces[1]))
            for at, part in enumerate(parts):
                part = back_in_rows(part)
                d_cat[row, pl.ds(step * 7, 7), :, 256 * at:256 * (at + 1)] = part.astype(BF)
                d_own[row, pl.ds(step * 7, 7), :, 256 * at:256 * (at + 1)] = part[:, 8:24, :].astype(BF)

    left = turned(ctx_cat[3:19, :, 256:512])
    left = jnp.concatenate([left] * 4, axis=1)
    for a in range(3):
        for b in range(3):
            rights = []
            for k in (2 - a, 3 - a):
                phase, shift = VARIANT[k]
                at = 2 + phase + shift
                for l in (2 - b, 3 - b):
                    rights.append(d_own[phase, at:at + 16, :, 512 * l:512 * (l + 1)].reshape(256, 512))
            put(0, 3 * a + b, slice(0, 512), dot(left, jnp.concatenate(rights, axis=0)))

    @pl.loop(0, 2)
    def _(step):
        value = flat(coarse[pl.ds(step * 10 + 1, 10)])
        for k in range(4):
            phase, shift = VARIANT[k]
            at = step * 10 + shift + phase
            value = value + dot(flat(d_cat[phase, pl.ds(at, 10)]), fold_t[k])
        value = jnp.where(inside(place_ref, step * 10 - 2, 10), value, 0.0)
        three_wide(value, gc_cat, step * 10, 10)
        for at, part in enumerate((before(value), value, after(value))):
            gc_own[pl.ds(step * 10, 10), :, 256 * at:256 * (at + 1)] = back_in_rows(part)[:, 8:24, :].astype(BF)

    left = turned(pool_cat[4:20, :, 256:512])
    for a in range(3):
        for b in range(3):
            right = gc_own[3 - a:19 - a, :, 256 * (2 - b):256 * (3 - b)].reshape(256, 256)
            put(1, 3 * a + b, slice(0, 256), dot(left, right))

    @pl.loop(0, 2)
    def _(step):
        value = jnp.zeros((288, 256), F32)
        for a in range(3):
            value = value + dot(flat(gc_cat[pl.ds(step * 9 + a, 9)]), w_coarse_t[768 * a:768 * (a + 1)])
        value = value * 0.25
        valid = inside(place_ref, step * 9 - 1, 9)
        for row in range(2):
            even, odd = [
                jnp.where(valid, flat(err[2 * row + col, pl.ds(step * 9 + 1 + row, 9)]) + value, 0.0)
                for col in range(2)
            ]
            for at, part in enumerate((before(odd), even, odd, after(even))):
                compact = part.reshape(9, 32, 256)[:, 8:24, :]
                g_fine[row, pl.ds(step * 9, 9), :, 256 * at:256 * (at + 1)] = compact.astype(BF)

    left = jnp.concatenate([own_ref[p].reshape(256, 256).T for p in range(4)], axis=1)
    for a in range(3):
        for b in range(3):
            rights = []
            for row in range(2):
                phase, shift = VARIANT[row + 2 - a]
                for col in range(2):
                    at = col + 2 - b
                    rights.append(g_fine[phase, 1 + shift:17 + shift, :, 256 * at:256 * (at + 1)].reshape(256, 256))
            put(1, 3 * a + b, slice(256, 512), dot(left, jnp.concatenate(rights, axis=0)))


def feat_kernel(g_fine, w_post_t, out_ref, wide):
    for row in range(2):
        for col in range(2):
            value = jnp.zeros((256, 256), F32)
            for a in range(3):
                phase, shift = VARIANT[row + a]
                cells = g_fine[phase, 1 + shift:17 + shift, :, 256 * col:256 * col + 768].reshape(256, 768)
                value = value + dot(cells, w_post_t[768 * a:768 * (a + 1)])
            for half in range(2):
                wide[:, row, half, pl.ds(col, 16, stride=2), :] = (
                    value[:, 128 * half:128 * (half + 1)].reshape(16, 16, 128))
    for half in range(2):
        out_ref[:, :, :, 128 * half:128 * (half + 1)] = wide[:, :, half].astype(BF)


TAPS_OF = ((0,), (1, 2), (0, 1), (2,))


def weight_kernel(w_post, w_coarse, w_prior, fold, fold_t, w_post_t, w_coarse_t):
    for i in range(4):
        for j in range(4):
            taps = [3 * a + b for a in TAPS_OF[i] for b in TAPS_OF[j]]
            total = w_prior[256 * taps[0]:256 * (taps[0] + 1)].astype(F32)
            for tap in taps[1:]:
                total = total + w_prior[256 * tap:256 * (tap + 1)].astype(F32)
            total = total.astype(BF)
            fold[i, 256 * j:256 * (j + 1)] = total
            k, l = FOLD.index(i), FOLD.index(j)
            fold_t[k, 512 * l:512 * (l + 1)] = total.T
    for tap in range(9):
        w_coarse_t[256 * tap:256 * (tap + 1)] = w_coarse[256 * (8 - tap):256 * (9 - tap)].T
        w_post_t[256 * tap:256 * (tap + 1)] = w_post[256 * (8 - tap):256 * (9 - tap)].T


def sent(strip, down, right):
    pairs = [
        (r * 16 + c, (r + down) * 16 + c + right)
        for r in range(16) for c in range(16) if 0 <= r + down < 16 and 0 <= c + right < 16
    ]
    return lax.ppermute(strip, ("row", "col"), pairs)


def on_device(feat, noise_fine, noise_coarse, w_post, w_coarse, w_prior):
    scale = 1.0 / 512.0
    own, part, top, bottom = pl.pallas_call(
        first_kernel,
        out_shape=[
            jax.ShapeDtypeStruct((4, 16, 16, 256), BF),
            jax.ShapeDtypeStruct((4, 17, 32, 256), F32),
            jax.ShapeDtypeStruct((23, 16, 256), BF),
            jax.ShapeDtypeStruct((23, 16, 256), BF),
        ],
        in_specs=in_vmem(4),
        out_specs=in_vmem(4),
        scratch_shapes=[
            pltpu.VMEM((16, 2, 2, 32, 128), F32),
            pltpu.VMEM((16, 2, 2, 32, 128), F32),
            pltpu.VMEM((2, 18, 32, 256), F32),
            pltpu.VMEM((2, 18, 32, 1024), BF),
            pltpu.VMEM((32, 256), F32),
        ],
        compiler_params=room(16),
        name="first",
    )(feat.reshape(16, 2, 32, 256), noise_fine.reshape(16, 2, 32, 256), noise_coarse, w_post)
    from_up, from_down = sent(bottom, 1, 0), sent(top, -1, 0)
    fold, fold_t, w_post_t, w_coarse_t = pl.pallas_call(
        weight_kernel,
        out_shape=[
            jax.ShapeDtypeStruct((4, 1024, 512), BF),
            jax.ShapeDtypeStruct((4, 2048, 256), BF),
            jax.ShapeDtypeStruct((2304, 256), BF),
            jax.ShapeDtypeStruct((2304, 256), BF),
        ],
        in_specs=in_vmem(3),
        out_specs=in_vmem(4),
        compiler_params=room(20),
        cost_estimate=pl.CostEstimate(flops=10000000, bytes_accessed=15000000, transcendentals=0),
        name="weights",
    )(w_post, w_coarse, w_prior)
    left, right = pl.pallas_call(
        middle_kernel,
        out_shape=[jax.ShapeDtypeStruct((24, 24, 256), BF)] * 2,
        in_specs=in_vmem(4),
        out_specs=in_vmem(2),
        scratch_shapes=[pltpu.VMEM((24, 24, 256), F32), pltpu.VMEM((32, 256), F32)],
        compiler_params=room(10),
        name="middle",
    )(part, noise_coarse, from_up, from_down)
    from_left, from_right = sent(right, 0, 1), sent(left, 0, -1)
    row, col = lax.axis_index("row"), lax.axis_index("col")
    place = jnp.stack([row, col, col % 2]).astype(jnp.int32)
    grads, g_fine = pl.pallas_call(
        functools.partial(main_kernel, scale),
        out_shape=[
            jax.ShapeDtypeStruct((2, 2, 1152, 512), BF),
            jax.ShapeDtypeStruct((2, 18, 16, 1024), BF),
        ],
        in_specs=[pl.BlockSpec(memory_space=pltpu.SMEM)] + in_vmem(11),
        out_specs=in_vmem(2),
        scratch_shapes=[
            pltpu.VMEM((4, 24, 32, 256), F32),
            pltpu.VMEM((22, 32, 256), F32),
            pltpu.VMEM((24, 32, 768), BF),
            pltpu.VMEM((22, 32, 256), F32),
            pltpu.VMEM((22, 32, 768), BF),
            pltpu.VMEM((4, 21, 32, 256), F32),
            pltpu.VMEM((2, 21, 32, 2048), BF),
            pltpu.VMEM((2, 21, 16, 2048), BF),
            pltpu.VMEM((20, 32, 768), BF),
            pltpu.VMEM((20, 16, 768), BF),
            pltpu.VMEM((32, 256), F32),
        ],
        compiler_params=room(28),
        name="tile",
    )(place, own, part, noise_coarse, from_up, from_down, from_left, from_right,
      w_coarse, fold, fold_t, w_coarse_t)
    grad_feat = pl.pallas_call(
        feat_kernel,
        out_shape=jax.ShapeDtypeStruct((16, 2, 32, 256), BF),
        in_specs=in_vmem(2),
        out_specs=pl.BlockSpec(memory_space=pltpu.VMEM),
        scratch_shapes=[pltpu.VMEM((16, 2, 2, 32, 128), F32)],
        compiler_params=room(12),
        cost_estimate=pl.CostEstimate(flops=1200000000, bytes_accessed=3000000, transcendentals=0),
        name="feat",
    )(g_fine, w_post_t).reshape(32, 32, 256)
    summed, grad_feat = reduce_scatter(grads, grad_feat)
    return grad_feat, summed[1, :, 256:].reshape(-1), summed[1, :, :256].reshape(-1), summed[0].reshape(-1)


def solution(mesh):
    return jax.shard_map(
        on_device,
        mesh=mesh,
        in_specs=(
            P("row", "col", None),
            P("row", "col", None),
            P("row", "col", None),
            P(),
            P(),
            P(),
        ),
        out_specs=(P("row", "col", None), P(("row", "col")), P(("row", "col")), P(("row", "col"))),
        check_vma=False,
    )
```

```python
import functools
import math

import jax
import jax.numpy as jnp
from jax import lax
from jax.experimental import pallas as pl
from jax.experimental.pallas import tpu as pltpu
from jax.sharding import PartitionSpec as P

BF = jnp.bfloat16
F32 = jnp.float32
VARIANT = ((1, -1), (0, 0), (1, 0), (0, 1))
FOLD = (3, 1, 2, 0)


def digits():
    places = []
    for d in range(256):
        row, col = d // 16, d % 16
        places.append({"zl": row // 4, "x": row % 4, "zh": col // 8, "y": (col // 2) % 4, "core": col % 2})
    return places


def index_of(place):
    return (place["zl"] * 4 + place["x"]) * 16 + (place["zh"] * 4 + place["y"]) * 2 + place["core"]


def my_place():
    row, col = lax.axis_index("row"), lax.axis_index("col")
    return {"zl": row // 4, "x": row % 4, "zh": col // 8, "y": (col // 2) % 4, "core": col % 2}


def flipped(place, name, bits):
    return {**place, name: place[name] ^ bits}


def sum_stage(part, name, dim):
    here = my_place()[name]
    arrived = []
    for bits in (1, 3, 2):
        piece = lax.dynamic_index_in_dim(part, here ^ bits, dim, keepdims=False)
        pairs = [(index_of(p), index_of(flipped(p, name, bits))) for p in digits()]
        arrived.append(lax.ppermute(piece, ("row", "col"), pairs))
    total = lax.dynamic_index_in_dim(part, here, dim, keepdims=False).astype(F32)
    for piece in arrived:
        total = total + piece.astype(F32)
    return total.astype(BF)


def reduce_scatter(keep, send, beside):
    pairs = [(index_of(p), index_of(flipped(p, "core", 1))) for p in digits()]
    other, beside = lax.optimization_barrier((lax.ppermute(send, ("row", "col"), pairs), beside))
    parts = pl.pallas_call(
        join_kernel,
        out_shape=jax.ShapeDtypeStruct((2, 1152, 512), BF),
        in_specs=in_vmem(2),
        out_specs=pl.BlockSpec(memory_space=pltpu.VMEM),
        compiler_params=room(9),
        name="join",
    )(keep, other)
    first = parts[0].reshape(4, 4, 72, 512)
    second = parts[1].reshape(4, 4, 72, 512)
    first, second = sum_stage(first, "x", 0), sum_stage(second, "y", 1)
    first, second = sum_stage(first, "y", 0), sum_stage(second, "x", 0)
    parts = sum_stage(jnp.stack([first, second]).reshape(2, 4, 18, 512), "zl", 1)
    halves = parts.reshape(2, 2, 9, 512)
    last = my_place()["zh"]
    total = 0.0
    for flip in (0, 1):
        pairs = []
        for p in digits():
            chunk = (((p["core"] * 4 + p["x"]) * 4 + p["y"]) * 4 + p["zl"]) * 2 + (p["zh"] + flip) % 2
            pairs.append((index_of(p), chunk))
        piece = lax.dynamic_index_in_dim(halves, (last + flip) % 2, 1, keepdims=False)
        total = total + lax.ppermute(piece, ("row", "col"), pairs).astype(F32)
    return total, beside


def room(mib):
    return pltpu.CompilerParams(vmem_limit_bytes=mib * 1024 * 1024)


def in_vmem(count):
    return [pl.BlockSpec(memory_space=pltpu.VMEM)] * count


def split_lanes(ref, value):
    for half in range(2):
        ref[:, :, half] = value[..., 128 * half:128 * (half + 1)]


def phase_of(ref, row, col):
    return jnp.concatenate([ref[:, row, half, pl.ds(col, 16, stride=2), :] for half in range(2)], axis=-1)


def line_of(ref, line, col):
    return jnp.concatenate(
        [ref[line // 2, line % 2, half, pl.ds(col, 16, stride=2), :] for half in range(2)], axis=-1)


def split_lanes(ref, value):
    for half in range(2):
        ref[:, :, half] = value[..., 128 * half:128 * (half + 1)]


def phase_of(ref, row, col):
    return jnp.concatenate([ref[:, row, half, pl.ds(col, 16, stride=2), :] for half in range(2)], axis=-1)


def first_kernel(feat_hbm, fine_hbm, low_hbm, post_hbm, own_ref, part_ref, top_ref, bottom_ref,
                 feat_ref, fine_ref, low_ref, w_post, wide, noise, field, cat, spill, sems):
    pairs = ((feat_hbm, feat_ref), (post_hbm.at[:768], w_post.at[:768]), (post_hbm.at[768:1536], w_post.at[768:1536]),
             (post_hbm.at[1536:], w_post.at[1536:]), (fine_hbm.at[:8], fine_ref.at[:8]),
             (fine_hbm.at[8:], fine_ref.at[8:]), (low_hbm, low_ref))
    copies = [pltpu.make_async_copy(source, target, sems.at[at]) for at, (source, target) in enumerate(pairs)]
    for copy in copies:
        copy.start()
    field[...] = jnp.zeros(field.shape, F32)
    spill[...] = jnp.zeros(spill.shape, F32)
    copies[0].wait()
    split_lanes(wide, feat_ref[...].astype(F32))
    for row in range(2):
        for col in range(2):
            cells = phase_of(wide, row, col)
            own_ref[2 * row + col] = cells.astype(BF)
            field[col, 1:17, 8:24, :] = cells
        even, odd = flat(field[0]), flat(field[1])
        for at, part in enumerate((before(odd), even, odd, after(even))):
            cat[row, :, :, 256 * at:256 * (at + 1)] = back_in_rows(part.astype(BF))
    for copy in copies[1:]:
        copy.wait()
    split_lanes(noise, fine_ref[...])
    for row in range(2):
        for col in range(2):
            value = jnp.zeros((544, 256), F32)
            for a in range(3):
                phase, shift = VARIANT[row + a]
                at = 1 + shift - row
                cells = flat(cat[phase, at:at + 17, :, 256 * col:256 * col + 768])
                value = value + dot(cells, w_post[768 * a:768 * (a + 1)])
            part_ref[2 * row + col] = back_in_rows(value)
            part_ref[2 * row + col, row:row + 16, 8:24, :] += phase_of(noise, row, col)
    for out, first, low_first in ((top_ref, -1, 0), (bottom_ref, 24, 13)):
        for r in range(9):
            line = first + r
            row = line % 2
            at = line // 2 + row
            for col in range(2):
                e = 2 * r + col
                out[e] = part_ref[2 * row + col, at, 8:24, :].astype(BF)
                edge = 7 if col else 24
                spill[e:e + 1, :] = part_ref[2 * row + col, at, edge:edge + 1, :]
        out[18:21] = low_ref[low_first:low_first + 3].astype(BF)
        out[21:23] = spill[...].reshape(2, 16, 256).astype(BF)


def middle_kernel(part_ref, low_ref, up_ref, down_ref, left_ref, right_ref, side, spill):
    lows = ((4, low_ref[...]), (1, up_ref[18:21].astype(F32)), (20, down_ref[18:21].astype(F32)))
    for out, long, long_from, other_from, low_from in ((left_ref, 1, -1, 0, 0), (right_ref, 0, 12, 12, 13)):
        side[...] = jnp.zeros(side.shape, F32)
        for row in range(2):
            at = 9 * row
            rows = slice(4 - row, 21 - row)
            side[rows, at:at + 5, :] = part_ref[2 * row + long, :, 8 + long_from:13 + long_from, :]
            side[rows, at + 5:at + 9, :] = part_ref[2 * row + 1 - long, :, 8 + other_from:12 + other_from, :]
        for ref, first in ((up_ref, -8), (down_ref, 31)):
            spill[...] = ref[21:23].astype(F32).reshape(32, 256)
            for r in range(9):
                line = first + r
                row = line % 2
                here, at = line // 2 + 4, 9 * row
                cells = ref[2 * r + long].astype(F32)
                end = spill[2 * r + long:2 * r + long + 1, :]
                if long:
                    side[here, at:at + 1, :] += end
                    side[here, at + 1:at + 5, :] += cells[0:4]
                else:
                    side[here, at:at + 4, :] += cells[12:16]
                    side[here, at + 4:at + 5, :] += end
                side[here, at + 5:at + 9, :] += ref[2 * r + 1 - long].astype(F32)[other_from:other_from + 4]
        for here, block in lows:
            side[here:here + block.shape[0], 18:21, :] = block[:, low_from:low_from + 3, :]
        out[...] = side[...].astype(BF)


def flat(block):
    return block.reshape(block.shape[0] * 32, block.shape[2])


def back_in_rows(block):
    return block.reshape(block.shape[0] // 32, 32, block.shape[1])


def before(block):
    return pltpu.roll(block, 1, 0)


def after(block):
    return pltpu.roll(block, block.shape[0] - 1, 0)


def dot(left, right):
    return jnp.dot(left, right, preferred_element_type=F32)


def inside(place_ref, first_row, rows):
    cell = lax.broadcasted_iota(jnp.int32, (rows * 32, 256), 0)
    line = cell // 32 + first_row + 16 * place_ref[0]
    column = cell % 32 - 8 + 16 * place_ref[1]
    return (line >= 0) & (line < 256) & (column >= 0) & (column < 256)


def three_wide(value, ref, first, rows):
    c = value.shape[1]
    for at, part in enumerate((before(value), value, after(value))):
        ref[pl.ds(first, rows), :, c * at:c * (at + 1)] = back_in_rows(part.astype(BF))


def own_cells(block):
    return block.astype(F32)[:, 8:24, :].reshape(256, block.shape[2]).astype(BF)


def turned(block):
    return own_cells(block).T


def main_kernel(scale, place_ref, own_ref, part_ref, low_ref, up_ref, down_ref, left_ref, right_ref,
                w_coarse, fold, fold_t, w_coarse_t, keep_ref, send_ref, g_fine,
                fine, low, pool_cat, coarse, ctx_cat, err, d_cat, d_own, gc_cat, gc_own, spill, grads):
    def put(which, tap, lanes, value):
        value = (value * scale).astype(BF)
        for half, first, start, stop in ((0, 256 * tap, 0, 256), (1, 256 * tap - 1152, 0, 256)):
            start, stop = max(start, -first), min(stop, 1152 - first)
            if start < stop:
                slot = (place_ref[2] + half) % 2
                grads[slot, which, first + start:first + stop, lanes] = value[start:stop]

    fine[...] = jnp.zeros(fine.shape, F32)
    for row in range(2):
        for col in range(2):
            fine[2 * row + col, 4 - row:21 - row] = part_ref[2 * row + col]
    low[3:19, 8:24, :] = low_ref[...]
    for ref, first, low_first in ((up_ref, -8, 0), (down_ref, 31, 19)):
        spill[...] = ref[21:23].astype(F32).reshape(32, 256)
        for r in range(9):
            line = first + r
            for col in range(2):
                e = 2 * r + col
                edge = 7 if col else 24
                fine[2 * (line % 2) + col, line // 2 + 4, 8:24, :] += ref[e].astype(F32)
                fine[2 * (line % 2) + col, line // 2 + 4, edge:edge + 1, :] += spill[e:e + 1, :]
        low[low_first:low_first + 3, 8:24, :] = ref[18:21].astype(F32)
    for ref, long, long_at, other_at, low_at in ((left_ref, 0, 4, 4, 5), (right_ref, 1, 23, 24, 24)):
        block = ref[...].astype(F32)
        for row in range(2):
            at = 9 * row
            fine[2 * row + long, :, long_at:long_at + 5, :] += block[:, at:at + 5, :]
            fine[2 * row + 1 - long, :, other_at:other_at + 4, :] += block[:, at + 5:at + 9, :]
        low[:, low_at:low_at + 3, :] = block[1:23, 18:21, :]

    @pl.loop(0, 3)
    def _(step):
        total = flat(fine[0, pl.ds(step * 8, 8)])
        for p in range(1, 4):
            total = total + flat(fine[p, pl.ds(step * 8, 8)])
        total = jnp.where(inside(place_ref, step * 8 - 4, 8), total * 0.25, 0.0)
        three_wide(total, pool_cat, step * 8, 8)

    @pl.loop(0, 2)
    def _(step):
        value = flat(low[pl.ds(step * 11, 11)])
        for a in range(3):
            value = value + dot(flat(pool_cat[pl.ds(step * 11 + a, 11)]), w_coarse[768 * a:768 * (a + 1)])
        value = jnp.where(inside(place_ref, step * 11 - 3, 11), value, 0.0)
        coarse[pl.ds(step * 11, 11)] = back_in_rows(value)
        three_wide(value, ctx_cat, step * 11, 11)

    for row in range(2):
        @pl.loop(0, 3)
        def _(step):
            valid = inside(place_ref, step * 7 - 2 - row, 7)
            pieces = []
            for col in range(2):
                prior = jnp.zeros((224, 512), F32)
                for k in range(2):
                    cells = flat(ctx_cat[pl.ds(step * 7 + k, 7), :, 256 * col:256 * col + 512])
                    prior = prior + dot(cells, fold[2 * row + k, 512 * col:512 * col + 512])
                raw = prior[:, 256:]
                small = jnp.exp(-jnp.abs(raw))
                more = 1.0 + small
                sigma = jnp.maximum(raw, 0.0) + jnp.log(more) + 0.5
                gate = jnp.where(raw >= 0.0, 1.0, small) / more
                inverse = 1.0 / sigma
                deviation = flat(fine[2 * row + col, pl.ds(step * 7 + 2 - row, 7)]) - prior[:, :256]
                residual = deviation * inverse * inverse
                err[2 * row + col, pl.ds(step * 7, 7)] = back_in_rows(residual)
                pieces.append(jnp.where(valid, -residual, 0.0))
                pieces.append(jnp.where(valid, (inverse - residual * deviation * inverse) * gate, 0.0))
            parts = (before(pieces[2]), before(pieces[3]), pieces[0], pieces[1], pieces[2], pieces[3],
                     after(pieces[0]), after(pieces[1]))
            for at, part in enumerate(parts):
                part = back_in_rows(part)
                d_cat[row, pl.ds(step * 7, 7), :, 256 * at:256 * (at + 1)] = part.astype(BF)
                d_own[row, pl.ds(step * 7, 7), :, 256 * at:256 * (at + 1)] = part[:, 8:24, :].astype(BF)

    left = turned(ctx_cat[3:19, :, 256:512])
    left = jnp.concatenate([left] * 4, axis=1)
    for a in range(3):
        for b in range(3):
            rights = []
            for k in (2 - a, 3 - a):
                phase, shift = VARIANT[k]
                at = 2 + phase + shift
                for l in (2 - b, 3 - b):
                    rights.append(d_own[phase, at:at + 16, :, 512 * l:512 * (l + 1)].reshape(256, 512))
            put(0, 3 * a + b, slice(0, 512), dot(left, jnp.concatenate(rights, axis=0)))

    @pl.loop(0, 2)
    def _(step):
        value = flat(coarse[pl.ds(step * 10 + 1, 10)])
        for k in range(4):
            phase, shift = VARIANT[k]
            at = step * 10 + shift + phase
            value = value + dot(flat(d_cat[phase, pl.ds(at, 10)]), fold_t[k])
        value = jnp.where(inside(place_ref, step * 10 - 2, 10), value, 0.0)
        three_wide(value, gc_cat, step * 10, 10)
        for at, part in enumerate((before(value), value, after(value))):
            gc_own[pl.ds(step * 10, 10), :, 256 * at:256 * (at + 1)] = back_in_rows(part)[:, 8:24, :].astype(BF)

    left = turned(pool_cat[4:20, :, 256:512])
    for a in range(3):
        for b in range(3):
            right = gc_own[3 - a:19 - a, :, 256 * (2 - b):256 * (3 - b)].reshape(256, 256)
            put(1, 3 * a + b, slice(0, 256), dot(left, right))

    @pl.loop(0, 2)
    def _(step):
        value = jnp.zeros((288, 256), F32)
        for a in range(3):
            value = value + dot(flat(gc_cat[pl.ds(step * 9 + a, 9)]), w_coarse_t[768 * a:768 * (a + 1)])
        value = value * 0.25
        valid = inside(place_ref, step * 9 - 1, 9)
        for row in range(2):
            even, odd = [
                jnp.where(valid, flat(err[2 * row + col, pl.ds(step * 9 + 1 + row, 9)]) + value, 0.0)
                for col in range(2)
            ]
            for at, part in enumerate((before(odd), even, odd, after(even))):
                compact = part.reshape(9, 32, 256)[:, 8:24, :]
                g_fine[row, pl.ds(step * 9, 9), :, 256 * at:256 * (at + 1)] = compact.astype(BF)

    left = jnp.concatenate([own_ref[p].reshape(256, 256).T for p in range(4)], axis=1)
    for a in range(3):
        for b in range(3):
            rights = []
            for row in range(2):
                phase, shift = VARIANT[row + 2 - a]
                for col in range(2):
                    at = col + 2 - b
                    rights.append(g_fine[phase, 1 + shift:17 + shift, :, 256 * at:256 * (at + 1)].reshape(256, 256))
            put(1, 3 * a + b, slice(256, 512), dot(left, jnp.concatenate(rights, axis=0)))
    keep_ref[...] = grads[0]
    send_ref[...] = grads[1]


def join_kernel(keep_ref, other_ref, out_ref):
    out_ref[...] = (keep_ref[...].astype(F32) + other_ref[...].astype(F32)).astype(BF)


def feat_kernel(g_fine, w_post_t, out_ref, wide):
    for row in range(2):
        for col in range(2):
            value = jnp.zeros((256, 256), F32)
            for a in range(3):
                phase, shift = VARIANT[row + a]
                cells = g_fine[phase, 1 + shift:17 + shift, :, 256 * col:256 * col + 768].reshape(256, 768)
                value = value + dot(cells, w_post_t[768 * a:768 * (a + 1)])
            for half in range(2):
                wide[:, row, half, pl.ds(col, 16, stride=2), :] = (
                    value[:, 128 * half:128 * (half + 1)].reshape(16, 16, 128))
    for half in range(2):
        out_ref[:, :, :, 128 * half:128 * (half + 1)] = wide[:, :, half].astype(BF)


TAPS_OF = ((0,), (1, 2), (0, 1), (2,))


def weight_kernel(w_post, w_coarse, w_prior, fold, fold_t, w_post_t, w_coarse_t):
    for i in range(4):
        for j in range(4):
            taps = [3 * a + b for a in TAPS_OF[i] for b in TAPS_OF[j]]
            total = w_prior[256 * taps[0]:256 * (taps[0] + 1)].astype(F32)
            for tap in taps[1:]:
                total = total + w_prior[256 * tap:256 * (tap + 1)].astype(F32)
            total = total.astype(BF)
            fold[i, 256 * j:256 * (j + 1)] = total
            k, l = FOLD.index(i), FOLD.index(j)
            fold_t[k, 512 * l:512 * (l + 1)] = total.T
    for tap in range(9):
        w_coarse_t[256 * tap:256 * (tap + 1)] = w_coarse[256 * (8 - tap):256 * (9 - tap)].T
        w_post_t[256 * tap:256 * (tap + 1)] = w_post[256 * (8 - tap):256 * (9 - tap)].T


def sent(strip, down, right):
    pairs = [
        (r * 16 + c, (r + down) * 16 + c + right)
        for r in range(16) for c in range(16) if 0 <= r + down < 16 and 0 <= c + right < 16
    ]
    return lax.ppermute(strip, ("row", "col"), pairs)


def on_device(feat, noise_fine, noise_coarse, w_post, w_coarse, w_prior):
    scale = 1.0 / 512.0
    own, part, top, bottom = pl.pallas_call(
        first_kernel,
        out_shape=[
            jax.ShapeDtypeStruct((4, 16, 16, 256), BF),
            jax.ShapeDtypeStruct((4, 17, 32, 256), F32),
            jax.ShapeDtypeStruct((23, 16, 256), BF),
            jax.ShapeDtypeStruct((23, 16, 256), BF),
        ],
        in_specs=[pl.BlockSpec(memory_space=pltpu.HBM)] * 4,
        out_specs=in_vmem(4),
        scratch_shapes=[
            pltpu.VMEM((16, 2, 32, 256), BF),
            pltpu.VMEM((16, 2, 32, 256), F32),
            pltpu.VMEM((16, 16, 256), F32),
            pltpu.VMEM((2304, 256), BF),
            pltpu.VMEM((16, 2, 2, 32, 128), F32),
            pltpu.VMEM((16, 2, 2, 32, 128), F32),
            pltpu.VMEM((2, 18, 32, 256), F32),
            pltpu.VMEM((2, 18, 32, 1024), BF),
            pltpu.VMEM((32, 256), F32),
            pltpu.SemaphoreType.DMA((7,)),
        ],
        compiler_params=room(59),
        name="first",
    )(feat.reshape(16, 2, 32, 256), noise_fine.reshape(16, 2, 32, 256), noise_coarse, w_post)
    from_up, from_down = sent(bottom, 1, 0), sent(top, -1, 0)
    fold, fold_t, w_post_t, w_coarse_t = pl.pallas_call(
        weight_kernel,
        out_shape=[
            jax.ShapeDtypeStruct((4, 1024, 512), BF),
            jax.ShapeDtypeStruct((4, 2048, 256), BF),
            jax.ShapeDtypeStruct((2304, 256), BF),
            jax.ShapeDtypeStruct((2304, 256), BF),
        ],
        in_specs=in_vmem(3),
        out_specs=in_vmem(4),
        compiler_params=room(20),
        cost_estimate=pl.CostEstimate(flops=10000000, bytes_accessed=15000000, transcendentals=0),
        name="weights",
    )(w_post, w_coarse, w_prior)
    left, right = pl.pallas_call(
        middle_kernel,
        out_shape=[jax.ShapeDtypeStruct((24, 24, 256), BF)] * 2,
        in_specs=in_vmem(4),
        out_specs=in_vmem(2),
        scratch_shapes=[pltpu.VMEM((24, 24, 256), F32), pltpu.VMEM((32, 256), F32)],
        compiler_params=room(10),
        name="middle",
    )(part, noise_coarse, from_up, from_down)
    from_left, from_right = sent(right, 0, 1), sent(left, 0, -1)
    row, col = lax.axis_index("row"), lax.axis_index("col")
    place = jnp.stack([row, col, col % 2]).astype(jnp.int32)
    keep, send, g_fine = pl.pallas_call(
        functools.partial(main_kernel, scale),
        out_shape=[
            jax.ShapeDtypeStruct((2, 1152, 512), BF),
            jax.ShapeDtypeStruct((2, 1152, 512), BF),
            jax.ShapeDtypeStruct((2, 18, 16, 1024), BF),
        ],
        in_specs=[pl.BlockSpec(memory_space=pltpu.SMEM)] + in_vmem(11),
        out_specs=in_vmem(3),
        scratch_shapes=[
            pltpu.VMEM((4, 24, 32, 256), F32),
            pltpu.VMEM((22, 32, 256), F32),
            pltpu.VMEM((24, 32, 768), BF),
            pltpu.VMEM((22, 32, 256), F32),
            pltpu.VMEM((22, 32, 768), BF),
            pltpu.VMEM((4, 21, 32, 256), F32),
            pltpu.VMEM((2, 21, 32, 2048), BF),
            pltpu.VMEM((2, 21, 16, 2048), BF),
            pltpu.VMEM((20, 32, 768), BF),
            pltpu.VMEM((20, 16, 768), BF),
            pltpu.VMEM((32, 256), F32),
            pltpu.VMEM((2, 2, 1152, 512), BF),
        ],
        compiler_params=room(32),
        name="tile",
    )(place, own, part, noise_coarse, from_up, from_down, from_left, from_right,
      w_coarse, fold, fold_t, w_coarse_t)
    grad_feat = pl.pallas_call(
        feat_kernel,
        out_shape=jax.ShapeDtypeStruct((16, 2, 32, 256), BF),
        in_specs=in_vmem(2),
        out_specs=pl.BlockSpec(memory_space=pltpu.VMEM),
        scratch_shapes=[pltpu.VMEM((16, 2, 2, 32, 128), F32)],
        compiler_params=room(8),
        cost_estimate=pl.CostEstimate(flops=1200000000, bytes_accessed=3000000, transcendentals=0),
        name="feat",
    )(g_fine, w_post_t).reshape(32, 32, 256)
    summed, grad_feat = reduce_scatter(keep, send, grad_feat)
    return grad_feat, summed[1, :, 256:].reshape(-1), summed[1, :, :256].reshape(-1), summed[0].reshape(-1)


def solution(mesh):
    return jax.shard_map(
        on_device,
        mesh=mesh,
        in_specs=(
            P("row", "col", None),
            P("row", "col", None),
            P("row", "col", None),
            P(),
            P(),
            P(),
        ),
        out_specs=(P("row", "col", None), P(("row", "col")), P(("row", "col")), P(("row", "col"))),
        check_vma=False,
    )
```

```python
import functools
import math

import jax
import jax.numpy as jnp
from jax import lax
from jax.experimental import pallas as pl
from jax.experimental.pallas import tpu as pltpu
from jax.sharding import PartitionSpec as P

BF = jnp.bfloat16
F32 = jnp.float32
VARIANT = ((1, -1), (0, 0), (1, 0), (0, 1))
FOLD = (3, 1, 2, 0)


def digits():
    places = []
    for d in range(256):
        row, col = d // 16, d % 16
        places.append({"zl": row // 4, "x": row % 4, "zh": col // 8, "y": (col // 2) % 4, "core": col % 2})
    return places


def index_of(place):
    return (place["zl"] * 4 + place["x"]) * 16 + (place["zh"] * 4 + place["y"]) * 2 + place["core"]


def my_place():
    row, col = lax.axis_index("row"), lax.axis_index("col")
    return {"zl": row // 4, "x": row % 4, "zh": col // 8, "y": (col // 2) % 4, "core": col % 2}


def flipped(place, name, bits):
    return {**place, name: place[name] ^ bits}


def sum_stage(part, name, dim):
    here = my_place()[name]
    arrived = []
    for bits in (1, 3, 2):
        piece = lax.dynamic_index_in_dim(part, here ^ bits, dim, keepdims=False)
        pairs = [(index_of(p), index_of(flipped(p, name, bits))) for p in digits()]
        arrived.append(lax.ppermute(piece, ("row", "col"), pairs))
    total = lax.dynamic_index_in_dim(part, here, dim, keepdims=False).astype(F32)
    for piece in arrived:
        total = total + piece.astype(F32)
    return total.astype(BF)


def reduce_scatter(keep, send, beside):
    pairs = [(index_of(p), index_of(flipped(p, "core", 1))) for p in digits()]
    other, beside = lax.optimization_barrier((lax.ppermute(send, ("row", "col"), pairs), beside))
    parts = pl.pallas_call(
        join_kernel,
        out_shape=jax.ShapeDtypeStruct((2, 1152, 512), BF),
        in_specs=in_vmem(2),
        out_specs=pl.BlockSpec(memory_space=pltpu.VMEM),
        compiler_params=room(9),
        name="join",
    )(keep, other)
    first = parts[0].reshape(4, 4, 72, 512)
    second = parts[1].reshape(4, 4, 72, 512)
    first, second = sum_stage(first, "x", 0), sum_stage(second, "y", 1)
    first, second = sum_stage(first, "y", 0), sum_stage(second, "x", 0)
    parts = sum_stage(jnp.stack([first, second]).reshape(2, 4, 18, 512), "zl", 1)
    halves = parts.reshape(2, 2, 9, 512)
    last = my_place()["zh"]
    total = 0.0
    for flip in (0, 1):
        pairs = []
        for p in digits():
            chunk = (((p["core"] * 4 + p["x"]) * 4 + p["y"]) * 4 + p["zl"]) * 2 + (p["zh"] + flip) % 2
            pairs.append((index_of(p), chunk))
        piece = lax.dynamic_index_in_dim(halves, (last + flip) % 2, 1, keepdims=False)
        total = total + lax.ppermute(piece, ("row", "col"), pairs).astype(F32)
    return total, beside


def room(mib):
    return pltpu.CompilerParams(vmem_limit_bytes=mib * 1024 * 1024)


def in_vmem(count):
    return [pl.BlockSpec(memory_space=pltpu.VMEM)] * count


def split_lanes(ref, value):
    for half in range(2):
        ref[:, :, half] = value[..., 128 * half:128 * (half + 1)]


def phase_of(ref, row, col):
    return jnp.concatenate([ref[:, row, half, pl.ds(col, 16, stride=2), :] for half in range(2)], axis=-1)


def line_of(ref, line, col):
    return jnp.concatenate(
        [ref[line // 2, line % 2, half, pl.ds(col, 16, stride=2), :] for half in range(2)], axis=-1)


def split_lanes(ref, value):
    for half in range(2):
        ref[:, :, half] = value[..., 128 * half:128 * (half + 1)]


def phase_of(ref, row, col):
    return jnp.concatenate([ref[:, row, half, pl.ds(col, 16, stride=2), :] for half in range(2)], axis=-1)


def first_kernel(feat_hbm, fine_hbm, low_hbm, post_hbm, own_ref, part_ref, top_ref, bottom_ref,
                 left_ref, right_ref, feat_ref, fine_ref, low_ref, w_post, wide, noise, field, cat, spill, side, sems):
    pairs = ((feat_hbm, feat_ref), (post_hbm.at[:768], w_post.at[:768]), (post_hbm.at[768:1536], w_post.at[768:1536]),
             (post_hbm.at[1536:], w_post.at[1536:]), (fine_hbm.at[:8], fine_ref.at[:8]),
             (fine_hbm.at[8:], fine_ref.at[8:]), (low_hbm, low_ref))
    copies = [pltpu.make_async_copy(source, target, sems.at[at]) for at, (source, target) in enumerate(pairs)]
    for copy in copies:
        copy.start()
    field[...] = jnp.zeros(field.shape, F32)
    spill[...] = jnp.zeros(spill.shape, F32)
    copies[0].wait()
    split_lanes(wide, feat_ref[...].astype(F32))
    for row in range(2):
        for col in range(2):
            cells = phase_of(wide, row, col)
            own_ref[2 * row + col] = cells.astype(BF)
            field[col, 1:17, 8:24, :] = cells
        even, odd = flat(field[0]), flat(field[1])
        for at, part in enumerate((before(odd), even, odd, after(even))):
            cat[row, :, :, 256 * at:256 * (at + 1)] = back_in_rows(part.astype(BF))
    for copy in copies[1:]:
        copy.wait()
    split_lanes(noise, fine_ref[...])
    for row in range(2):
        for col in range(2):
            value = jnp.zeros((544, 256), F32)
            for a in range(3):
                phase, shift = VARIANT[row + a]
                at = 1 + shift - row
                cells = flat(cat[phase, at:at + 17, :, 256 * col:256 * col + 768])
                value = value + dot(cells, w_post[768 * a:768 * (a + 1)])
            part_ref[2 * row + col] = back_in_rows(value)
            part_ref[2 * row + col, row:row + 16, 8:24, :] += phase_of(noise, row, col)
    for out, first, low_first in ((top_ref, -1, 0), (bottom_ref, 24, 13)):
        for r in range(9):
            line = first + r
            row = line % 2
            at = line // 2 + row
            for col in range(2):
                e = 2 * r + col
                out[e] = part_ref[2 * row + col, at, 8:24, :].astype(BF)
                edge = 7 if col else 24
                spill[e:e + 1, :] = part_ref[2 * row + col, at, edge:edge + 1, :]
        out[18:21] = low_ref[low_first:low_first + 3].astype(BF)
        out[21:23] = spill[...].reshape(2, 16, 256).astype(BF)
    for out, long, long_from, other_from, low_from in ((left_ref, 1, -1, 0, 0), (right_ref, 0, 12, 12, 13)):
        side[...] = jnp.zeros(side.shape, F32)
        for row in range(2):
            at = 9 * row
            rows = slice(1 - row, 18 - row)
            side[rows, at:at + 5, :] = part_ref[2 * row + long, :, 8 + long_from:13 + long_from, :]
            side[rows, at + 5:at + 9, :] = part_ref[2 * row + 1 - long, :, 8 + other_from:12 + other_from, :]
        side[1:17, 18:21, :] = low_ref[:, low_from:low_from + 3, :]
        out[...] = side[...].astype(BF)


def middle_kernel(up_ref, down_ref, left_ref, right_ref, side, spill):
    for out, long, other_from, low_from in ((left_ref, 1, 0, 0), (right_ref, 0, 12, 13)):
        side[...] = jnp.zeros(side.shape, F32)
        for ref, first, offset in ((up_ref, -8, 4), (down_ref, 31, -10)):
            spill[...] = ref[21:23].astype(F32).reshape(32, 256)
            for r in range(9):
                line = first + r
                row = line % 2
                here, at = line // 2 + offset, 9 * row
                cells = ref[2 * r + long].astype(F32)
                end = spill[2 * r + long:2 * r + long + 1, :]
                if long:
                    side[here, at:at + 1, :] = end
                    side[here, at + 1:at + 5, :] = cells[0:4]
                else:
                    side[here, at:at + 4, :] = cells[12:16]
                    side[here, at + 4:at + 5, :] = end
                side[here, at + 5:at + 9, :] = ref[2 * r + 1 - long].astype(F32)[other_from:other_from + 4]
        side[1:4, 18:21, :] = up_ref[18:21].astype(F32)[:, low_from:low_from + 3, :]
        side[6:9, 18:21, :] = down_ref[18:21].astype(F32)[:, low_from:low_from + 3, :]
        out[...] = side[...].astype(BF)


def flat(block):
    return block.reshape(block.shape[0] * 32, block.shape[2])


def back_in_rows(block):
    return block.reshape(block.shape[0] // 32, 32, block.shape[1])


def before(block):
    return pltpu.roll(block, 1, 0)


def after(block):
    return pltpu.roll(block, block.shape[0] - 1, 0)


def dot(left, right):
    return jnp.dot(left, right, preferred_element_type=F32)


def inside(place_ref, first_row, rows):
    cell = lax.broadcasted_iota(jnp.int32, (rows * 32, 256), 0)
    line = cell // 32 + first_row + 16 * place_ref[0]
    column = cell % 32 - 8 + 16 * place_ref[1]
    return (line >= 0) & (line < 256) & (column >= 0) & (column < 256)


def three_wide(value, ref, first, rows):
    c = value.shape[1]
    for at, part in enumerate((before(value), value, after(value))):
        ref[pl.ds(first, rows), :, c * at:c * (at + 1)] = back_in_rows(part.astype(BF))


def own_cells(block):
    return block.astype(F32)[:, 8:24, :].reshape(256, block.shape[2]).astype(BF)


def turned(block):
    return own_cells(block).T


def main_kernel(scale, place_ref, own_ref, part_ref, low_ref, up_ref, down_ref, left_ref, right_ref, more_left_ref, more_right_ref,
                w_coarse, fold, fold_t, w_coarse_t, keep_ref, send_ref, g_fine,
                fine, low, pool_cat, coarse, ctx_cat, err, d_cat, d_own, gc_cat, gc_own, spill, grads):
    def put(which, tap, lanes, value):
        value = (value * scale).astype(BF)
        for half, first, start, stop in ((0, 256 * tap, 0, 256), (1, 256 * tap - 1152, 0, 256)):
            start, stop = max(start, -first), min(stop, 1152 - first)
            if start < stop:
                slot = (place_ref[2] + half) % 2
                grads[slot, which, first + start:first + stop, lanes] = value[start:stop]

    fine[...] = jnp.zeros(fine.shape, F32)
    for row in range(2):
        for col in range(2):
            fine[2 * row + col, 4 - row:21 - row] = part_ref[2 * row + col]
    low[3:19, 8:24, :] = low_ref[...]
    for ref, first, low_first in ((up_ref, -8, 0), (down_ref, 31, 19)):
        spill[...] = ref[21:23].astype(F32).reshape(32, 256)
        for r in range(9):
            line = first + r
            for col in range(2):
                e = 2 * r + col
                edge = 7 if col else 24
                fine[2 * (line % 2) + col, line // 2 + 4, 8:24, :] += ref[e].astype(F32)
                fine[2 * (line % 2) + col, line // 2 + 4, edge:edge + 1, :] += spill[e:e + 1, :]
        low[low_first:low_first + 3, 8:24, :] = ref[18:21].astype(F32)
    for ref, more, long, long_at, other_at, low_at in (
            (left_ref, more_left_ref, 0, 4, 4, 5), (right_ref, more_right_ref, 1, 23, 24, 24)):
        block, rest = ref[...].astype(F32), more[...].astype(F32)
        for rows, cells in ((slice(3, 21), block), (slice(0, 5), rest[0:5]), (slice(19, 24), rest[5:10])):
            for row in range(2):
                at = 9 * row
                fine[2 * row + long, rows, long_at:long_at + 5, :] += cells[:, at:at + 5, :]
                fine[2 * row + 1 - long, rows, other_at:other_at + 4, :] += cells[:, at + 5:at + 9, :]
        low[3:19, low_at:low_at + 3, :] = block[1:17, 18:21, :]
        low[0:3, low_at:low_at + 3, :] = rest[1:4, 18:21, :]
        low[19:22, low_at:low_at + 3, :] = rest[6:9, 18:21, :]

    @pl.loop(0, 3)
    def _(step):
        total = flat(fine[0, pl.ds(step * 8, 8)])
        for p in range(1, 4):
            total = total + flat(fine[p, pl.ds(step * 8, 8)])
        total = jnp.where(inside(place_ref, step * 8 - 4, 8), total * 0.25, 0.0)
        three_wide(total, pool_cat, step * 8, 8)

    @pl.loop(0, 2)
    def _(step):
        value = flat(low[pl.ds(step * 11, 11)])
        for a in range(3):
            value = value + dot(flat(pool_cat[pl.ds(step * 11 + a, 11)]), w_coarse[768 * a:768 * (a + 1)])
        value = jnp.where(inside(place_ref, step * 11 - 3, 11), value, 0.0)
        coarse[pl.ds(step * 11, 11)] = back_in_rows(value)
        three_wide(value, ctx_cat, step * 11, 11)

    for row in range(2):
        @pl.loop(0, 3)
        def _(step):
            valid = inside(place_ref, step * 7 - 2 - row, 7)
            pieces = []
            for col in range(2):
                prior = jnp.zeros((224, 512), F32)
                for k in range(2):
                    cells = flat(ctx_cat[pl.ds(step * 7 + k, 7), :, 256 * col:256 * col + 512])
                    prior = prior + dot(cells, fold[2 * row + k, 512 * col:512 * col + 512])
                raw = prior[:, 256:]
                small = jnp.exp(-jnp.abs(raw))
                more = 1.0 + small
                sigma = jnp.maximum(raw, 0.0) + jnp.log(more) + 0.5
                gate = jnp.where(raw >= 0.0, 1.0, small) / more
                inverse = 1.0 / sigma
                deviation = flat(fine[2 * row + col, pl.ds(step * 7 + 2 - row, 7)]) - prior[:, :256]
                residual = deviation * inverse * inverse
                err[2 * row + col, pl.ds(step * 7, 7)] = back_in_rows(residual)
                pieces.append(jnp.where(valid, -residual, 0.0))
                pieces.append(jnp.where(valid, (inverse - residual * deviation * inverse) * gate, 0.0))
            parts = (before(pieces[2]), before(pieces[3]), pieces[0], pieces[1], pieces[2], pieces[3],
                     after(pieces[0]), after(pieces[1]))
            for at, part in enumerate(parts):
                part = back_in_rows(part)
                d_cat[row, pl.ds(step * 7, 7), :, 256 * at:256 * (at + 1)] = part.astype(BF)
                d_own[row, pl.ds(step * 7, 7), :, 256 * at:256 * (at + 1)] = part[:, 8:24, :].astype(BF)

    left = turned(ctx_cat[3:19, :, 256:512])
    left = jnp.concatenate([left] * 4, axis=1)
    for a in range(3):
        for b in range(3):
            rights = []
            for k in (2 - a, 3 - a):
                phase, shift = VARIANT[k]
                at = 2 + phase + shift
                for l in (2 - b, 3 - b):
                    rights.append(d_own[phase, at:at + 16, :, 512 * l:512 * (l + 1)].reshape(256, 512))
            put(0, 3 * a + b, slice(0, 512), dot(left, jnp.concatenate(rights, axis=0)))

    @pl.loop(0, 2)
    def _(step):
        value = flat(coarse[pl.ds(step * 10 + 1, 10)])
        for k in range(4):
            phase, shift = VARIANT[k]
            at = step * 10 + shift + phase
            value = value + dot(flat(d_cat[phase, pl.ds(at, 10)]), fold_t[k])
        value = jnp.where(inside(place_ref, step * 10 - 2, 10), value, 0.0)
        three_wide(value, gc_cat, step * 10, 10)
        for at, part in enumerate((before(value), value, after(value))):
            gc_own[pl.ds(step * 10, 10), :, 256 * at:256 * (at + 1)] = back_in_rows(part)[:, 8:24, :].astype(BF)

    left = turned(pool_cat[4:20, :, 256:512])
    for a in range(3):
        for b in range(3):
            right = gc_own[3 - a:19 - a, :, 256 * (2 - b):256 * (3 - b)].reshape(256, 256)
            put(1, 3 * a + b, slice(0, 256), dot(left, right))

    @pl.loop(0, 2)
    def _(step):
        value = jnp.zeros((288, 256), F32)
        for a in range(3):
            value = value + dot(flat(gc_cat[pl.ds(step * 9 + a, 9)]), w_coarse_t[768 * a:768 * (a + 1)])
        value = value * 0.25
        valid = inside(place_ref, step * 9 - 1, 9)
        for row in range(2):
            even, odd = [
                jnp.where(valid, flat(err[2 * row + col, pl.ds(step * 9 + 1 + row, 9)]) + value, 0.0)
                for col in range(2)
            ]
            for at, part in enumerate((before(odd), even, odd, after(even))):
                compact = part.reshape(9, 32, 256)[:, 8:24, :]
                g_fine[row, pl.ds(step * 9, 9), :, 256 * at:256 * (at + 1)] = compact.astype(BF)

    left = jnp.concatenate([own_ref[p].reshape(256, 256).T for p in range(4)], axis=1)
    for a in range(3):
        for b in range(3):
            rights = []
            for row in range(2):
                phase, shift = VARIANT[row + 2 - a]
                for col in range(2):
                    at = col + 2 - b
                    rights.append(g_fine[phase, 1 + shift:17 + shift, :, 256 * at:256 * (at + 1)].reshape(256, 256))
            put(1, 3 * a + b, slice(256, 512), dot(left, jnp.concatenate(rights, axis=0)))
    keep_ref[...] = grads[0]
    send_ref[...] = grads[1]


def join_kernel(keep_ref, other_ref, out_ref):
    out_ref[...] = (keep_ref[...].astype(F32) + other_ref[...].astype(F32)).astype(BF)


def feat_kernel(g_fine, w_post_t, out_ref, wide):
    for row in range(2):
        for col in range(2):
            value = jnp.zeros((256, 256), F32)
            for a in range(3):
                phase, shift = VARIANT[row + a]
                cells = g_fine[phase, 1 + shift:17 + shift, :, 256 * col:256 * col + 768].reshape(256, 768)
                value = value + dot(cells, w_post_t[768 * a:768 * (a + 1)])
            for half in range(2):
                wide[:, row, half, pl.ds(col, 16, stride=2), :] = (
                    value[:, 128 * half:128 * (half + 1)].reshape(16, 16, 128))
    for half in range(2):
        out_ref[:, :, :, 128 * half:128 * (half + 1)] = wide[:, :, half].astype(BF)


TAPS_OF = ((0,), (1, 2), (0, 1), (2,))


def weight_kernel(w_post, w_coarse, w_prior, fold, fold_t, w_post_t, w_coarse_t):
    for i in range(4):
        for j in range(4):
            taps = [3 * a + b for a in TAPS_OF[i] for b in TAPS_OF[j]]
            total = w_prior[256 * taps[0]:256 * (taps[0] + 1)].astype(F32)
            for tap in taps[1:]:
                total = total + w_prior[256 * tap:256 * (tap + 1)].astype(F32)
            total = total.astype(BF)
            fold[i, 256 * j:256 * (j + 1)] = total
            k, l = FOLD.index(i), FOLD.index(j)
            fold_t[k, 512 * l:512 * (l + 1)] = total.T
    for tap in range(9):
        w_coarse_t[256 * tap:256 * (tap + 1)] = w_coarse[256 * (8 - tap):256 * (9 - tap)].T
        w_post_t[256 * tap:256 * (tap + 1)] = w_post[256 * (8 - tap):256 * (9 - tap)].T


def sent(strip, down, right):
    pairs = [
        (r * 16 + c, (r + down) * 16 + c + right)
        for r in range(16) for c in range(16) if 0 <= r + down < 16 and 0 <= c + right < 16
    ]
    return lax.ppermute(strip, ("row", "col"), pairs)


def on_device(feat, noise_fine, noise_coarse, w_post, w_coarse, w_prior):
    scale = 1.0 / 512.0
    own, part, top, bottom, left, right = pl.pallas_call(
        first_kernel,
        out_shape=[
            jax.ShapeDtypeStruct((4, 16, 16, 256), BF),
            jax.ShapeDtypeStruct((4, 17, 32, 256), F32),
            jax.ShapeDtypeStruct((23, 16, 256), BF),
            jax.ShapeDtypeStruct((23, 16, 256), BF),
            jax.ShapeDtypeStruct((18, 24, 256), BF),
            jax.ShapeDtypeStruct((18, 24, 256), BF),
        ],
        in_specs=[pl.BlockSpec(memory_space=pltpu.HBM)] * 4,
        out_specs=in_vmem(6),
        scratch_shapes=[
            pltpu.VMEM((16, 2, 32, 256), BF),
            pltpu.VMEM((16, 2, 32, 256), F32),
            pltpu.VMEM((16, 16, 256), F32),
            pltpu.VMEM((2304, 256), BF),
            pltpu.VMEM((16, 2, 2, 32, 128), F32),
            pltpu.VMEM((16, 2, 2, 32, 128), F32),
            pltpu.VMEM((2, 18, 32, 256), F32),
            pltpu.VMEM((2, 18, 32, 1024), BF),
            pltpu.VMEM((32, 256), F32),
            pltpu.VMEM((18, 24, 256), F32),
            pltpu.SemaphoreType.DMA((7,)),
        ],
        compiler_params=room(59),
        name="first",
    )(feat.reshape(16, 2, 32, 256), noise_fine.reshape(16, 2, 32, 256), noise_coarse, w_post)
    from_left, from_right = sent(right, 0, 1), sent(left, 0, -1)
    from_up, from_down = sent(bottom, 1, 0), sent(top, -1, 0)
    fold, fold_t, w_post_t, w_coarse_t = pl.pallas_call(
        weight_kernel,
        out_shape=[
            jax.ShapeDtypeStruct((4, 1024, 512), BF),
            jax.ShapeDtypeStruct((4, 2048, 256), BF),
            jax.ShapeDtypeStruct((2304, 256), BF),
            jax.ShapeDtypeStruct((2304, 256), BF),
        ],
        in_specs=in_vmem(3),
        out_specs=in_vmem(4),
        compiler_params=room(20),
        cost_estimate=pl.CostEstimate(flops=10000000, bytes_accessed=15000000, transcendentals=0),
        name="weights",
    )(w_post, w_coarse, w_prior)
    left, right = pl.pallas_call(
        middle_kernel,
        out_shape=[jax.ShapeDtypeStruct((10, 24, 256), BF)] * 2,
        in_specs=in_vmem(2),
        out_specs=in_vmem(2),
        scratch_shapes=[pltpu.VMEM((10, 24, 256), F32), pltpu.VMEM((32, 256), F32)],
        compiler_params=room(6),
        name="middle",
    )(from_up, from_down)
    more_left, more_right = sent(right, 0, 1), sent(left, 0, -1)
    row, col = lax.axis_index("row"), lax.axis_index("col")
    place = jnp.stack([row, col, col % 2]).astype(jnp.int32)
    keep, send, g_fine = pl.pallas_call(
        functools.partial(main_kernel, scale),
        out_shape=[
            jax.ShapeDtypeStruct((2, 1152, 512), BF),
            jax.ShapeDtypeStruct((2, 1152, 512), BF),
            jax.ShapeDtypeStruct((2, 18, 16, 1024), BF),
        ],
        in_specs=[pl.BlockSpec(memory_space=pltpu.SMEM)] + in_vmem(13),
        out_specs=in_vmem(3),
        scratch_shapes=[
            pltpu.VMEM((4, 24, 32, 256), F32),
            pltpu.VMEM((22, 32, 256), F32),
            pltpu.VMEM((24, 32, 768), BF),
            pltpu.VMEM((22, 32, 256), F32),
            pltpu.VMEM((22, 32, 768), BF),
            pltpu.VMEM((4, 21, 32, 256), F32),
            pltpu.VMEM((2, 21, 32, 2048), BF),
            pltpu.VMEM((2, 21, 16, 2048), BF),
            pltpu.VMEM((20, 32, 768), BF),
            pltpu.VMEM((20, 16, 768), BF),
            pltpu.VMEM((32, 256), F32),
            pltpu.VMEM((2, 2, 1152, 512), BF),
        ],
        compiler_params=room(32),
        name="tile",
    )(place, own, part, noise_coarse, from_up, from_down, from_left, from_right,
      more_left, more_right, w_coarse, fold, fold_t, w_coarse_t)
    grad_feat = pl.pallas_call(
        feat_kernel,
        out_shape=jax.ShapeDtypeStruct((16, 2, 32, 256), BF),
        in_specs=in_vmem(2),
        out_specs=pl.BlockSpec(memory_space=pltpu.VMEM),
        scratch_shapes=[pltpu.VMEM((16, 2, 2, 32, 128), F32)],
        compiler_params=room(8),
        cost_estimate=pl.CostEstimate(flops=1200000000, bytes_accessed=3000000, transcendentals=0),
        name="feat",
    )(g_fine, w_post_t).reshape(32, 32, 256)
    summed, grad_feat = reduce_scatter(keep, send, grad_feat)
    return grad_feat, summed[1, :, 256:].reshape(-1), summed[1, :, :256].reshape(-1), summed[0].reshape(-1)


def solution(mesh):
    return jax.shard_map(
        on_device,
        mesh=mesh,
        in_specs=(
            P("row", "col", None),
            P("row", "col", None),
            P("row", "col", None),
            P(),
            P(),
            P(),
        ),
        out_specs=(P("row", "col", None), P(("row", "col")), P(("row", "col")), P(("row", "col"))),
        check_vma=False,
    )
```

```python
import functools
import math

import jax
import jax.numpy as jnp
from jax import lax
from jax.experimental import pallas as pl
from jax.experimental.pallas import tpu as pltpu
from jax.sharding import PartitionSpec as P

BF = jnp.bfloat16
F32 = jnp.float32
VARIANT = ((1, -1), (0, 0), (1, 0), (0, 1))
FOLD = (3, 1, 2, 0)


def digits():
    places = []
    for d in range(256):
        row, col = d // 16, d % 16
        places.append({"zl": row // 4, "x": row % 4, "zh": col // 8, "y": (col // 2) % 4, "core": col % 2})
    return places


def index_of(place):
    return (place["zl"] * 4 + place["x"]) * 16 + (place["zh"] * 4 + place["y"]) * 2 + place["core"]


def my_place():
    row, col = lax.axis_index("row"), lax.axis_index("col")
    return {"zl": row // 4, "x": row % 4, "zh": col // 8, "y": (col // 2) % 4, "core": col % 2}


def flipped(place, name, bits):
    return {**place, name: place[name] ^ bits}


def sum_stage(part, name, cut):
    here = my_place()[name]
    arrived = []
    for bits in (1, 3, 2):
        pairs = [(index_of(p), index_of(flipped(p, name, bits))) for p in digits()]
        arrived.append(lax.ppermute(cut(part, here ^ bits), ("row", "col"), pairs))
    total = cut(part, here).astype(F32)
    for piece in arrived:
        total = total + piece.astype(F32)
    return total.astype(BF)


def pick(dim):
    return lambda part, at: lax.dynamic_index_in_dim(part, at, dim, keepdims=False)


def reduce_scatter(keep, send, beside):
    pairs = [(index_of(p), index_of(flipped(p, "core", 1))) for p in digits()]
    other, beside = lax.optimization_barrier((lax.ppermute(send, ("row", "col"), pairs), beside))
    parts = pl.pallas_call(
        join_kernel,
        out_shape=jax.ShapeDtypeStruct((2, 1152, 512), BF),
        in_specs=in_vmem(2),
        out_specs=pl.BlockSpec(memory_space=pltpu.VMEM),
        compiler_params=room(9),
        name="join",
    )(keep, other)
    first = sum_stage(parts[0].reshape(2, 4, 144, 512), "x", pick(1))
    second = sum_stage(parts[1].reshape(2, 4, 2, 72, 512), "y", lambda part, at: pick(1)(pick(0)(part, at // 2), at % 2))
    first = sum_stage(first.reshape(4, 72, 512), "y", pick(0))
    second = sum_stage(second, "x", pick(0))
    parts = sum_stage(jnp.stack([first, second]).reshape(2, 4, 18, 512), "zl", pick(1))
    halves = parts.reshape(2, 2, 9, 512)
    last = my_place()["zh"]
    total = 0.0
    for flip in (0, 1):
        pairs = []
        for p in digits():
            owner = {"zl": 2 * p["core"] + p["y"] // 2, "x": p["x"], "zh": p["y"] % 2, "y": p["zl"],
                     "core": p["zh"] ^ flip}
            pairs.append((index_of(p), index_of(owner)))
        piece = lax.dynamic_index_in_dim(halves, (last + flip) % 2, 1, keepdims=False)
        total = total + lax.ppermute(piece, ("row", "col"), pairs).astype(F32)
    return total, beside


def room(mib):
    return pltpu.CompilerParams(vmem_limit_bytes=mib * 1024 * 1024)


def in_vmem(count):
    return [pl.BlockSpec(memory_space=pltpu.VMEM)] * count


def split_lanes(ref, value):
    for half in range(2):
        ref[:, :, half] = value[..., 128 * half:128 * (half + 1)]


def phase_of(ref, row, col):
    return jnp.concatenate([ref[:, row, half, pl.ds(col, 16, stride=2), :] for half in range(2)], axis=-1)


def line_of(ref, line, col):
    return jnp.concatenate(
        [ref[line // 2, line % 2, half, pl.ds(col, 16, stride=2), :] for half in range(2)], axis=-1)


def split_lanes(ref, value):
    for half in range(2):
        ref[:, :, half] = value[..., 128 * half:128 * (half + 1)]


def phase_of(ref, row, col):
    return jnp.concatenate([ref[:, row, half, pl.ds(col, 16, stride=2), :] for half in range(2)], axis=-1)


def first_kernel(feat_hbm, fine_hbm, low_hbm, post_hbm, own_ref, part_ref, top_ref, bottom_ref,
                 feat_ref, fine_ref, low_ref, w_post, wide, noise, field, cat, spill, sems):
    pairs = ((feat_hbm, feat_ref), (post_hbm.at[:768], w_post.at[:768]), (post_hbm.at[768:1536], w_post.at[768:1536]),
             (post_hbm.at[1536:], w_post.at[1536:]), (fine_hbm.at[:8], fine_ref.at[:8]),
             (fine_hbm.at[8:], fine_ref.at[8:]), (low_hbm, low_ref))
    copies = [pltpu.make_async_copy(source, target, sems.at[at]) for at, (source, target) in enumerate(pairs)]
    for copy in copies:
        copy.start()
    field[...] = jnp.zeros(field.shape, F32)
    spill[...] = jnp.zeros(spill.shape, F32)
    copies[0].wait()
    split_lanes(wide, feat_ref[...].astype(F32))
    for row in range(2):
        for col in range(2):
            cells = phase_of(wide, row, col)
            own_ref[2 * row + col] = cells.astype(BF)
            field[col, 1:17, 8:24, :] = cells
        even, odd = flat(field[0]), flat(field[1])
        for at, part in enumerate((before(odd), even, odd, after(even))):
            cat[row, :, :, 256 * at:256 * (at + 1)] = back_in_rows(part.astype(BF))
    for copy in copies[1:]:
        copy.wait()
    split_lanes(noise, fine_ref[...])
    for row in range(2):
        for col in range(2):
            value = jnp.zeros((544, 256), F32)
            for a in range(3):
                phase, shift = VARIANT[row + a]
                at = 1 + shift - row
                cells = flat(cat[phase, at:at + 17, :, 256 * col:256 * col + 768])
                value = value + dot(cells, w_post[768 * a:768 * (a + 1)])
            part_ref[2 * row + col] = back_in_rows(value)
            part_ref[2 * row + col, row:row + 16, 8:24, :] += phase_of(noise, row, col)
    for out, first, low_first in ((top_ref, -1, 0), (bottom_ref, 24, 13)):
        for r in range(9):
            line = first + r
            row = line % 2
            at = line // 2 + row
            for col in range(2):
                e = 2 * r + col
                out[e] = part_ref[2 * row + col, at, 8:24, :].astype(BF)
                edge = 7 if col else 24
                spill[e:e + 1, :] = part_ref[2 * row + col, at, edge:edge + 1, :]
        out[18:21] = low_ref[low_first:low_first + 3].astype(BF)
        out[21:23] = spill[...].reshape(2, 16, 256).astype(BF)


def middle_kernel(part_ref, low_ref, up_ref, down_ref, left_ref, right_ref, side, spill):
    lows = ((4, low_ref[...]), (1, up_ref[18:21].astype(F32)), (20, down_ref[18:21].astype(F32)))
    for out, long, long_from, other_from, low_from in ((left_ref, 1, -1, 0, 0), (right_ref, 0, 12, 12, 13)):
        side[...] = jnp.zeros(side.shape, F32)
        for row in range(2):
            at = 9 * row
            rows = slice(4 - row, 21 - row)
            side[rows, at:at + 5, :] = part_ref[2 * row + long, :, 8 + long_from:13 + long_from, :]
            side[rows, at + 5:at + 9, :] = part_ref[2 * row + 1 - long, :, 8 + other_from:12 + other_from, :]
        for ref, first in ((up_ref, -8), (down_ref, 31)):
            spill[...] = ref[21:23].astype(F32).reshape(32, 256)
            for r in range(9):
                line = first + r
                row = line % 2
                here, at = line // 2 + 4, 9 * row
                cells = ref[2 * r + long].astype(F32)
                end = spill[2 * r + long:2 * r + long + 1, :]
                if long:
                    side[here, at:at + 1, :] += end
                    side[here, at + 1:at + 5, :] += cells[0:4]
                else:
                    side[here, at:at + 4, :] += cells[12:16]
                    side[here, at + 4:at + 5, :] += end
                side[here, at + 5:at + 9, :] += ref[2 * r + 1 - long].astype(F32)[other_from:other_from + 4]
        for here, block in lows:
            side[here:here + block.shape[0], 18:21, :] = block[:, low_from:low_from + 3, :]
        out[...] = side[...].astype(BF)


def flat(block):
    return block.reshape(block.shape[0] * 32, block.shape[2])


def back_in_rows(block):
    return block.reshape(block.shape[0] // 32, 32, block.shape[1])


def before(block):
    return pltpu.roll(block, 1, 0)


def after(block):
    return pltpu.roll(block, block.shape[0] - 1, 0)


def dot(left, right):
    return jnp.dot(left, right, preferred_element_type=F32)


def inside(place_ref, first_row, rows):
    cell = lax.broadcasted_iota(jnp.int32, (rows * 32, 256), 0)
    line = cell // 32 + first_row + 16 * place_ref[0]
    column = cell % 32 - 8 + 16 * place_ref[1]
    return (line >= 0) & (line < 256) & (column >= 0) & (column < 256)


def three_wide(value, ref, first, rows):
    c = value.shape[1]
    for at, part in enumerate((before(value), value, after(value))):
        ref[pl.ds(first, rows), :, c * at:c * (at + 1)] = back_in_rows(part.astype(BF))


def own_cells(block):
    return block.astype(F32)[:, 8:24, :].reshape(256, block.shape[2]).astype(BF)


def turned(block):
    return own_cells(block).T


def main_kernel(scale, place_ref, own_ref, part_ref, low_ref, up_ref, down_ref, left_ref, right_ref,
                w_coarse, fold, fold_t, w_coarse_t, keep_ref, send_ref, g_fine,
                fine, low, pool_cat, coarse, ctx_cat, err, d_cat, d_own, gc_cat, gc_own, spill, grads):
    def put(which, tap, lanes, value):
        value = (value * scale).astype(BF)
        for half, first, start, stop in ((0, 256 * tap, 0, 256), (1, 256 * tap - 1152, 0, 256)):
            start, stop = max(start, -first), min(stop, 1152 - first)
            if start < stop:
                slot = (place_ref[2] + half) % 2
                grads[slot, which, first + start:first + stop, lanes] = value[start:stop]

    fine[...] = jnp.zeros(fine.shape, F32)
    for row in range(2):
        for col in range(2):
            fine[2 * row + col, 4 - row:21 - row] = part_ref[2 * row + col]
    low[3:19, 8:24, :] = low_ref[...]
    for ref, first, low_first in ((up_ref, -8, 0), (down_ref, 31, 19)):
        spill[...] = ref[21:23].astype(F32).reshape(32, 256)
        for r in range(9):
            line = first + r
            for col in range(2):
                e = 2 * r + col
                edge = 7 if col else 24
                fine[2 * (line % 2) + col, line // 2 + 4, 8:24, :] += ref[e].astype(F32)
                fine[2 * (line % 2) + col, line // 2 + 4, edge:edge + 1, :] += spill[e:e + 1, :]
        low[low_first:low_first + 3, 8:24, :] = ref[18:21].astype(F32)
    for ref, long, long_at, other_at, low_at in ((left_ref, 0, 4, 4, 5), (right_ref, 1, 23, 24, 24)):
        block = ref[...].astype(F32)
        for row in range(2):
            at = 9 * row
            fine[2 * row + long, :, long_at:long_at + 5, :] += block[:, at:at + 5, :]
            fine[2 * row + 1 - long, :, other_at:other_at + 4, :] += block[:, at + 5:at + 9, :]
        low[:, low_at:low_at + 3, :] = block[1:23, 18:21, :]

    @pl.loop(0, 3)
    def _(step):
        total = flat(fine[0, pl.ds(step * 8, 8)])
        for p in range(1, 4):
            total = total + flat(fine[p, pl.ds(step * 8, 8)])
        total = jnp.where(inside(place_ref, step * 8 - 4, 8), total * 0.25, 0.0)
        three_wide(total, pool_cat, step * 8, 8)

    @pl.loop(0, 2)
    def _(step):
        value = flat(low[pl.ds(step * 11, 11)])
        for a in range(3):
            value = value + dot(flat(pool_cat[pl.ds(step * 11 + a, 11)]), w_coarse[768 * a:768 * (a + 1)])
        value = jnp.where(inside(place_ref, step * 11 - 3, 11), value, 0.0)
        coarse[pl.ds(step * 11, 11)] = back_in_rows(value)
        three_wide(value, ctx_cat, step * 11, 11)

    for row in range(2):
        @pl.loop(0, 3)
        def _(step):
            valid = inside(place_ref, step * 7 - 2 - row, 7)
            pieces = []
            for col in range(2):
                prior = jnp.zeros((224, 512), F32)
                for k in range(2):
                    cells = flat(ctx_cat[pl.ds(step * 7 + k, 7), :, 256 * col:256 * col + 512])
                    prior = prior + dot(cells, fold[2 * row + k, 512 * col:512 * col + 512])
                raw = prior[:, 256:]
                small = jnp.exp(-jnp.abs(raw))
                more = 1.0 + small
                sigma = jnp.maximum(raw, 0.0) + jnp.log(more) + 0.5
                gate = jnp.where(raw >= 0.0, 1.0, small) / more
                inverse = 1.0 / sigma
                deviation = flat(fine[2 * row + col, pl.ds(step * 7 + 2 - row, 7)]) - prior[:, :256]
                residual = deviation * inverse * inverse
                err[2 * row + col, pl.ds(step * 7, 7)] = back_in_rows(residual)
                pieces.append(jnp.where(valid, -residual, 0.0))
                pieces.append(jnp.where(valid, (inverse - residual * deviation * inverse) * gate, 0.0))
            parts = (before(pieces[2]), before(pieces[3]), pieces[0], pieces[1], pieces[2], pieces[3],
                     after(pieces[0]), after(pieces[1]))
            for at, part in enumerate(parts):
                part = back_in_rows(part)
                d_cat[row, pl.ds(step * 7, 7), :, 256 * at:256 * (at + 1)] = part.astype(BF)
                d_own[row, pl.ds(step * 7, 7), :, 256 * at:256 * (at + 1)] = part[:, 8:24, :].astype(BF)

    left = turned(ctx_cat[3:19, :, 256:512])
    left = jnp.concatenate([left] * 4, axis=1)
    for a in range(3):
        for b in range(3):
            rights = []
            for k in (2 - a, 3 - a):
                phase, shift = VARIANT[k]
                at = 2 + phase + shift
                for l in (2 - b, 3 - b):
                    rights.append(d_own[phase, at:at + 16, :, 512 * l:512 * (l + 1)].reshape(256, 512))
            put(0, 3 * a + b, slice(0, 512), dot(left, jnp.concatenate(rights, axis=0)))

    @pl.loop(0, 2)
    def _(step):
        value = flat(coarse[pl.ds(step * 10 + 1, 10)])
        for k in range(4):
            phase, shift = VARIANT[k]
            at = step * 10 + shift + phase
            value = value + dot(flat(d_cat[phase, pl.ds(at, 10)]), fold_t[k])
        value = jnp.where(inside(place_ref, step * 10 - 2, 10), value, 0.0)
        three_wide(value, gc_cat, step * 10, 10)
        for at, part in enumerate((before(value), value, after(value))):
            gc_own[pl.ds(step * 10, 10), :, 256 * at:256 * (at + 1)] = back_in_rows(part)[:, 8:24, :].astype(BF)

    left = turned(pool_cat[4:20, :, 256:512])
    for a in range(3):
        for b in range(3):
            right = gc_own[3 - a:19 - a, :, 256 * (2 - b):256 * (3 - b)].reshape(256, 256)
            put(1, 3 * a + b, slice(0, 256), dot(left, right))

    @pl.loop(0, 2)
    def _(step):
        value = jnp.zeros((288, 256), F32)
        for a in range(3):
            value = value + dot(flat(gc_cat[pl.ds(step * 9 + a, 9)]), w_coarse_t[768 * a:768 * (a + 1)])
        value = value * 0.25
        valid = inside(place_ref, step * 9 - 1, 9)
        for row in range(2):
            even, odd = [
                jnp.where(valid, flat(err[2 * row + col, pl.ds(step * 9 + 1 + row, 9)]) + value, 0.0)
                for col in range(2)
            ]
            for at, part in enumerate((before(odd), even, odd, after(even))):
                compact = part.reshape(9, 32, 256)[:, 8:24, :]
                g_fine[row, pl.ds(step * 9, 9), :, 256 * at:256 * (at + 1)] = compact.astype(BF)

    left = jnp.concatenate([own_ref[p].reshape(256, 256).T for p in range(4)], axis=1)
    for a in range(3):
        for b in range(3):
            rights = []
            for row in range(2):
                phase, shift = VARIANT[row + 2 - a]
                for col in range(2):
                    at = col + 2 - b
                    rights.append(g_fine[phase, 1 + shift:17 + shift, :, 256 * at:256 * (at + 1)].reshape(256, 256))
            put(1, 3 * a + b, slice(256, 512), dot(left, jnp.concatenate(rights, axis=0)))
    keep_ref[...] = grads[0]
    send_ref[...] = grads[1]


def join_kernel(keep_ref, other_ref, out_ref):
    out_ref[...] = (keep_ref[...].astype(F32) + other_ref[...].astype(F32)).astype(BF)


def feat_kernel(g_fine, w_post_t, out_ref, wide):
    for row in range(2):
        for col in range(2):
            value = jnp.zeros((256, 256), F32)
            for a in range(3):
                phase, shift = VARIANT[row + a]
                cells = g_fine[phase, 1 + shift:17 + shift, :, 256 * col:256 * col + 768].reshape(256, 768)
                value = value + dot(cells, w_post_t[768 * a:768 * (a + 1)])
            for half in range(2):
                wide[:, row, half, pl.ds(col, 16, stride=2), :] = (
                    value[:, 128 * half:128 * (half + 1)].reshape(16, 16, 128))
    for half in range(2):
        out_ref[:, :, :, 128 * half:128 * (half + 1)] = wide[:, :, half].astype(BF)


TAPS_OF = ((0,), (1, 2), (0, 1), (2,))


def weight_kernel(w_post, w_coarse, w_prior, fold, fold_t, w_post_t, w_coarse_t):
    for i in range(4):
        for j in range(4):
            taps = [3 * a + b for a in TAPS_OF[i] for b in TAPS_OF[j]]
            total = w_prior[256 * taps[0]:256 * (taps[0] + 1)].astype(F32)
            for tap in taps[1:]:
                total = total + w_prior[256 * tap:256 * (tap + 1)].astype(F32)
            total = total.astype(BF)
            fold[i, 256 * j:256 * (j + 1)] = total
            k, l = FOLD.index(i), FOLD.index(j)
            fold_t[k, 512 * l:512 * (l + 1)] = total.T
    for tap in range(9):
        w_coarse_t[256 * tap:256 * (tap + 1)] = w_coarse[256 * (8 - tap):256 * (9 - tap)].T
        w_post_t[256 * tap:256 * (tap + 1)] = w_post[256 * (8 - tap):256 * (9 - tap)].T


def sent(strip, down, right):
    pairs = [
        (r * 16 + c, (r + down) * 16 + c + right)
        for r in range(16) for c in range(16) if 0 <= r + down < 16 and 0 <= c + right < 16
    ]
    return lax.ppermute(strip, ("row", "col"), pairs)


def on_device(feat, noise_fine, noise_coarse, w_post, w_coarse, w_prior):
    scale = 1.0 / 512.0
    own, part, top, bottom = pl.pallas_call(
        first_kernel,
        out_shape=[
            jax.ShapeDtypeStruct((4, 16, 16, 256), BF),
            jax.ShapeDtypeStruct((4, 17, 32, 256), F32),
            jax.ShapeDtypeStruct((23, 16, 256), BF),
            jax.ShapeDtypeStruct((23, 16, 256), BF),
        ],
        in_specs=[pl.BlockSpec(memory_space=pltpu.HBM)] * 4,
        out_specs=in_vmem(4),
        scratch_shapes=[
            pltpu.VMEM((16, 2, 32, 256), BF),
            pltpu.VMEM((16, 2, 32, 256), F32),
            pltpu.VMEM((16, 16, 256), F32),
            pltpu.VMEM((2304, 256), BF),
            pltpu.VMEM((16, 2, 2, 32, 128), F32),
            pltpu.VMEM((16, 2, 2, 32, 128), F32),
            pltpu.VMEM((2, 18, 32, 256), F32),
            pltpu.VMEM((2, 18, 32, 1024), BF),
            pltpu.VMEM((32, 256), F32),
            pltpu.SemaphoreType.DMA((7,)),
        ],
        compiler_params=room(59),
        name="first",
    )(feat.reshape(16, 2, 32, 256), noise_fine.reshape(16, 2, 32, 256), noise_coarse, w_post)
    from_up, from_down = sent(bottom, 1, 0), sent(top, -1, 0)
    fold, fold_t, w_post_t, w_coarse_t = pl.pallas_call(
        weight_kernel,
        out_shape=[
            jax.ShapeDtypeStruct((4, 1024, 512), BF),
            jax.ShapeDtypeStruct((4, 2048, 256), BF),
            jax.ShapeDtypeStruct((2304, 256), BF),
            jax.ShapeDtypeStruct((2304, 256), BF),
        ],
        in_specs=in_vmem(3),
        out_specs=in_vmem(4),
        compiler_params=room(20),
        cost_estimate=pl.CostEstimate(flops=10000000, bytes_accessed=15000000, transcendentals=0),
        name="weights",
    )(w_post, w_coarse, w_prior)
    left, right = pl.pallas_call(
        middle_kernel,
        out_shape=[jax.ShapeDtypeStruct((24, 24, 256), BF)] * 2,
        in_specs=in_vmem(4),
        out_specs=in_vmem(2),
        scratch_shapes=[pltpu.VMEM((24, 24, 256), F32), pltpu.VMEM((32, 256), F32)],
        compiler_params=room(10),
        name="middle",
    )(part, noise_coarse, from_up, from_down)
    from_left, from_right = sent(right, 0, 1), sent(left, 0, -1)
    row, col = lax.axis_index("row"), lax.axis_index("col")
    place = jnp.stack([row, col, col % 2]).astype(jnp.int32)
    keep, send, g_fine = pl.pallas_call(
        functools.partial(main_kernel, scale),
        out_shape=[
            jax.ShapeDtypeStruct((2, 1152, 512), BF),
            jax.ShapeDtypeStruct((2, 1152, 512), BF),
            jax.ShapeDtypeStruct((2, 18, 16, 1024), BF),
        ],
        in_specs=[pl.BlockSpec(memory_space=pltpu.SMEM)] + in_vmem(11),
        out_specs=in_vmem(3),
        scratch_shapes=[
            pltpu.VMEM((4, 24, 32, 256), F32),
            pltpu.VMEM((22, 32, 256), F32),
            pltpu.VMEM((24, 32, 768), BF),
            pltpu.VMEM((22, 32, 256), F32),
            pltpu.VMEM((22, 32, 768), BF),
            pltpu.VMEM((4, 21, 32, 256), F32),
            pltpu.VMEM((2, 21, 32, 2048), BF),
            pltpu.VMEM((2, 21, 16, 2048), BF),
            pltpu.VMEM((20, 32, 768), BF),
            pltpu.VMEM((20, 16, 768), BF),
            pltpu.VMEM((32, 256), F32),
            pltpu.VMEM((2, 2, 1152, 512), BF),
        ],
        compiler_params=room(32),
        name="tile",
    )(place, own, part, noise_coarse, from_up, from_down, from_left, from_right,
      w_coarse, fold, fold_t, w_coarse_t)
    grad_feat = pl.pallas_call(
        feat_kernel,
        out_shape=jax.ShapeDtypeStruct((16, 2, 32, 256), BF),
        in_specs=in_vmem(2),
        out_specs=pl.BlockSpec(memory_space=pltpu.VMEM),
        scratch_shapes=[pltpu.VMEM((16, 2, 2, 32, 128), F32)],
        compiler_params=room(8),
        cost_estimate=pl.CostEstimate(flops=1200000000, bytes_accessed=3000000, transcendentals=0),
        name="feat",
    )(g_fine, w_post_t).reshape(32, 32, 256)
    summed, grad_feat = reduce_scatter(keep, send, grad_feat)
    return grad_feat, summed[1, :, 256:].reshape(-1), summed[1, :, :256].reshape(-1), summed[0].reshape(-1)


def solution(mesh):
    return jax.shard_map(
        on_device,
        mesh=mesh,
        in_specs=(
            P("row", "col", None),
            P("row", "col", None),
            P("row", "col", None),
            P(),
            P(),
            P(),
        ),
        out_specs=(P("row", "col", None), P(("row", "col")), P(("row", "col")), P(("row", "col"))),
        check_vma=False,
    )
```

```python
import functools
import math

import jax
import jax.numpy as jnp
from jax import lax
from jax.experimental import pallas as pl
from jax.experimental.pallas import tpu as pltpu
from jax.sharding import PartitionSpec as P

BF = jnp.bfloat16
F32 = jnp.float32
VARIANT = ((1, -1), (0, 0), (1, 0), (0, 1))
FOLD = (3, 1, 2, 0)


def digits():
    places = []
    for d in range(256):
        row, col = d // 16, d % 16
        places.append({"zl": row // 4, "x": row % 4, "zh": col // 8, "y": (col // 2) % 4, "core": col % 2})
    return places


def index_of(place):
    return (place["zl"] * 4 + place["x"]) * 16 + (place["zh"] * 4 + place["y"]) * 2 + place["core"]


def my_place():
    row, col = lax.axis_index("row"), lax.axis_index("col")
    return {"zl": row // 4, "x": row % 4, "zh": col // 8, "y": (col // 2) % 4, "core": col % 2}


def flipped(place, name, bits):
    return {**place, name: place[name] ^ bits}


def sum_stage(part, name, cut):
    here = my_place()[name]
    arrived = []
    for bits in (1, 3, 2):
        pairs = [(index_of(p), index_of(flipped(p, name, bits))) for p in digits()]
        arrived.append(lax.ppermute(cut(part, here ^ bits), ("row", "col"), pairs))
    total = cut(part, here).astype(F32)
    for piece in arrived:
        total = total + piece.astype(F32)
    return total.astype(BF)


def pick(dim):
    return lambda part, at: lax.dynamic_index_in_dim(part, at, dim, keepdims=False)


def reduce_scatter(keep, send, beside):
    pairs = [(index_of(p), index_of(flipped(p, "core", 1))) for p in digits()]
    other, beside = lax.optimization_barrier((lax.ppermute(send, ("row", "col"), pairs), beside))
    parts = pl.pallas_call(
        join_kernel,
        out_shape=jax.ShapeDtypeStruct((2, 1152, 512), BF),
        in_specs=in_vmem(2),
        out_specs=pl.BlockSpec(memory_space=pltpu.VMEM),
        compiler_params=room(9),
        name="join",
    )(keep, other)
    first = sum_stage(parts[0].reshape(2, 4, 144, 512), "x", pick(1))
    second = sum_stage(parts[1].reshape(2, 4, 2, 72, 512), "y", lambda part, at: pick(1)(pick(0)(part, at // 2), at % 2))
    first = sum_stage(first.reshape(4, 72, 512), "y", pick(0))
    second = sum_stage(second, "x", pick(0))
    parts = sum_stage(jnp.stack([first, second]).reshape(2, 4, 18, 512), "zl", pick(1))
    halves = parts.reshape(2, 2, 9, 512)
    last = my_place()["zh"]
    arrived = []
    for flip in (0, 1):
        pairs = []
        for p in digits():
            owner = {"zl": 2 * p["core"] + p["y"] // 2, "x": p["x"], "zh": p["y"] % 2, "y": p["zl"],
                     "core": p["zh"] ^ flip}
            pairs.append((index_of(p), index_of(owner)))
        piece = lax.dynamic_index_in_dim(halves, (last + flip) % 2, 1, keepdims=False)
        arrived.append(lax.ppermute(piece, ("row", "col"), pairs))
    prior, coarse, post = pl.pallas_call(
        last_kernel,
        out_shape=[jax.ShapeDtypeStruct((rows, 128), F32) for rows in (36, 18, 18)],
        in_specs=in_vmem(2),
        out_specs=in_vmem(3),
        compiler_params=room(4),
        name="last",
    )(*arrived)
    return prior.reshape(-1), coarse.reshape(-1), post.reshape(-1), beside


def room(mib):
    return pltpu.CompilerParams(vmem_limit_bytes=mib * 1024 * 1024)


def in_vmem(count):
    return [pl.BlockSpec(memory_space=pltpu.VMEM)] * count


def split_lanes(ref, value):
    for half in range(2):
        ref[:, :, half] = value[..., 128 * half:128 * (half + 1)]


def phase_of(ref, row, col):
    return jnp.concatenate([ref[:, row, half, pl.ds(col, 16, stride=2), :] for half in range(2)], axis=-1)


def line_of(ref, line, col):
    return jnp.concatenate(
        [ref[line // 2, line % 2, half, pl.ds(col, 16, stride=2), :] for half in range(2)], axis=-1)


def split_lanes(ref, value):
    for half in range(2):
        ref[:, :, half] = value[..., 128 * half:128 * (half + 1)]


def phase_of(ref, row, col):
    return jnp.concatenate([ref[:, row, half, pl.ds(col, 16, stride=2), :] for half in range(2)], axis=-1)


def first_kernel(feat_hbm, fine_hbm, low_hbm, post_hbm, own_ref, part_ref, top_ref, bottom_ref,
                 feat_ref, fine_ref, low_ref, w_post, wide, noise, field, cat, spill, sems):
    pairs = ((feat_hbm, feat_ref), (post_hbm.at[:768], w_post.at[:768]), (post_hbm.at[768:1536], w_post.at[768:1536]),
             (post_hbm.at[1536:], w_post.at[1536:]), (fine_hbm.at[:8], fine_ref.at[:8]),
             (fine_hbm.at[8:], fine_ref.at[8:]), (low_hbm, low_ref))
    copies = [pltpu.make_async_copy(source, target, sems.at[at]) for at, (source, target) in enumerate(pairs)]
    for copy in copies:
        copy.start()
    field[...] = jnp.zeros(field.shape, F32)
    spill[...] = jnp.zeros(spill.shape, F32)
    copies[0].wait()
    split_lanes(wide, feat_ref[...].astype(F32))
    for row in range(2):
        for col in range(2):
            cells = phase_of(wide, row, col)
            own_ref[2 * row + col] = cells.astype(BF)
            field[col, 1:17, 8:24, :] = cells
        even, odd = flat(field[0]), flat(field[1])
        for at, part in enumerate((before(odd), even, odd, after(even))):
            cat[row, :, :, 256 * at:256 * (at + 1)] = back_in_rows(part.astype(BF))
    for copy in copies[1:]:
        copy.wait()
    split_lanes(noise, fine_ref[...])
    for row in range(2):
        for col in range(2):
            value = jnp.zeros((544, 256), F32)
            for a in range(3):
                phase, shift = VARIANT[row + a]
                at = 1 + shift - row
                cells = flat(cat[phase, at:at + 17, :, 256 * col:256 * col + 768])
                value = value + dot(cells, w_post[768 * a:768 * (a + 1)])
            part_ref[2 * row + col] = back_in_rows(value)
            part_ref[2 * row + col, row:row + 16, 8:24, :] += phase_of(noise, row, col)
    for out, first, low_first in ((top_ref, -1, 0), (bottom_ref, 24, 13)):
        for r in range(9):
            line = first + r
            row = line % 2
            at = line // 2 + row
            for col in range(2):
                e = 2 * r + col
                out[e] = part_ref[2 * row + col, at, 8:24, :].astype(BF)
                edge = 7 if col else 24
                spill[e:e + 1, :] = part_ref[2 * row + col, at, edge:edge + 1, :]
        out[18:21] = low_ref[low_first:low_first + 3].astype(BF)
        out[21:23] = spill[...].reshape(2, 16, 256).astype(BF)


def middle_kernel(part_ref, low_ref, up_ref, down_ref, left_ref, right_ref, side, spill):
    lows = ((4, low_ref[...]), (1, up_ref[18:21].astype(F32)), (20, down_ref[18:21].astype(F32)))
    for out, long, long_from, other_from, low_from in ((left_ref, 1, -1, 0, 0), (right_ref, 0, 12, 12, 13)):
        side[...] = jnp.zeros(side.shape, F32)
        for row in range(2):
            at = 9 * row
            rows = slice(4 - row, 21 - row)
            side[rows, at:at + 5, :] = part_ref[2 * row + long, :, 8 + long_from:13 + long_from, :]
            side[rows, at + 5:at + 9, :] = part_ref[2 * row + 1 - long, :, 8 + other_from:12 + other_from, :]
        for ref, first in ((up_ref, -8), (down_ref, 31)):
            spill[...] = ref[21:23].astype(F32).reshape(32, 256)
            for r in range(9):
                line = first + r
                row = line % 2
                here, at = line // 2 + 4, 9 * row
                cells = ref[2 * r + long].astype(F32)
                end = spill[2 * r + long:2 * r + long + 1, :]
                if long:
                    side[here, at:at + 1, :] += end
                    side[here, at + 1:at + 5, :] += cells[0:4]
                else:
                    side[here, at:at + 4, :] += cells[12:16]
                    side[here, at + 4:at + 5, :] += end
                side[here, at + 5:at + 9, :] += ref[2 * r + 1 - long].astype(F32)[other_from:other_from + 4]
        for here, block in lows:
            side[here:here + block.shape[0], 18:21, :] = block[:, low_from:low_from + 3, :]
        out[...] = side[...].astype(BF)


def flat(block):
    return block.reshape(block.shape[0] * 32, block.shape[2])


def back_in_rows(block):
    return block.reshape(block.shape[0] // 32, 32, block.shape[1])


def before(block):
    return pltpu.roll(block, 1, 0)


def after(block):
    return pltpu.roll(block, block.shape[0] - 1, 0)


def dot(left, right):
    return jnp.dot(left, right, preferred_element_type=F32)


def inside(place_ref, first_row, rows):
    cell = lax.broadcasted_iota(jnp.int32, (rows * 32, 256), 0)
    line = cell // 32 + first_row + 16 * place_ref[0]
    column = cell % 32 - 8 + 16 * place_ref[1]
    return (line >= 0) & (line < 256) & (column >= 0) & (column < 256)


def three_wide(value, ref, first, rows):
    c = value.shape[1]
    for at, part in enumerate((before(value), value, after(value))):
        ref[pl.ds(first, rows), :, c * at:c * (at + 1)] = back_in_rows(part.astype(BF))


def own_cells(block):
    return block.astype(F32)[:, 8:24, :].reshape(256, block.shape[2]).astype(BF)


def turned(block):
    return own_cells(block).T


def main_kernel(scale, place_ref, own_ref, part_ref, low_ref, up_ref, down_ref, left_ref, right_ref,
                w_coarse, fold, fold_t, w_coarse_t, keep_ref, send_ref, g_fine,
                fine, low, pool_cat, coarse, ctx_cat, err, d_cat, d_own, gc_cat, gc_own, spill, grads):
    def put(which, tap, lanes, value):
        value = (value * scale).astype(BF)
        for half, first, start, stop in ((0, 256 * tap, 0, 256), (1, 256 * tap - 1152, 0, 256)):
            start, stop = max(start, -first), min(stop, 1152 - first)
            if start < stop:
                slot = (place_ref[2] + half) % 2
                grads[slot, which, first + start:first + stop, lanes] = value[start:stop]

    fine[...] = jnp.zeros(fine.shape, F32)
    for row in range(2):
        for col in range(2):
            fine[2 * row + col, 4 - row:21 - row] = part_ref[2 * row + col]
    low[3:19, 8:24, :] = low_ref[...]
    for ref, first, low_first in ((up_ref, -8, 0), (down_ref, 31, 19)):
        spill[...] = ref[21:23].astype(F32).reshape(32, 256)
        for r in range(9):
            line = first + r
            for col in range(2):
                e = 2 * r + col
                edge = 7 if col else 24
                fine[2 * (line % 2) + col, line // 2 + 4, 8:24, :] += ref[e].astype(F32)
                fine[2 * (line % 2) + col, line // 2 + 4, edge:edge + 1, :] += spill[e:e + 1, :]
        low[low_first:low_first + 3, 8:24, :] = ref[18:21].astype(F32)
    for ref, long, long_at, other_at, low_at in ((left_ref, 0, 4, 4, 5), (right_ref, 1, 23, 24, 24)):
        block = ref[...].astype(F32)
        for row in range(2):
            at = 9 * row
            fine[2 * row + long, :, long_at:long_at + 5, :] += block[:, at:at + 5, :]
            fine[2 * row + 1 - long, :, other_at:other_at + 4, :] += block[:, at + 5:at + 9, :]
        low[:, low_at:low_at + 3, :] = block[1:23, 18:21, :]

    @pl.loop(0, 3)
    def _(step):
        total = flat(fine[0, pl.ds(step * 8, 8)])
        for p in range(1, 4):
            total = total + flat(fine[p, pl.ds(step * 8, 8)])
        total = jnp.where(inside(place_ref, step * 8 - 4, 8), total * 0.25, 0.0)
        three_wide(total, pool_cat, step * 8, 8)

    @pl.loop(0, 2)
    def _(step):
        value = flat(low[pl.ds(step * 11, 11)])
        for a in range(3):
            value = value + dot(flat(pool_cat[pl.ds(step * 11 + a, 11)]), w_coarse[768 * a:768 * (a + 1)])
        value = jnp.where(inside(place_ref, step * 11 - 3, 11), value, 0.0)
        coarse[pl.ds(step * 11, 11)] = back_in_rows(value)
        three_wide(value, ctx_cat, step * 11, 11)

    for row in range(2):
        @pl.loop(0, 3)
        def _(step):
            valid = inside(place_ref, step * 7 - 2 - row, 7)
            pieces = []
            for col in range(2):
                prior = jnp.zeros((224, 512), F32)
                for k in range(2):
                    cells = flat(ctx_cat[pl.ds(step * 7 + k, 7), :, 256 * col:256 * col + 512])
                    prior = prior + dot(cells, fold[2 * row + k, 512 * col:512 * col + 512])
                raw = prior[:, 256:]
                small = jnp.exp(-jnp.abs(raw))
                more = 1.0 + small
                sigma = jnp.maximum(raw, 0.0) + jnp.log(more) + 0.5
                gate = jnp.where(raw >= 0.0, 1.0, small) / more
                inverse = 1.0 / sigma
                deviation = flat(fine[2 * row + col, pl.ds(step * 7 + 2 - row, 7)]) - prior[:, :256]
                residual = deviation * inverse * inverse
                err[2 * row + col, pl.ds(step * 7, 7)] = back_in_rows(residual)
                pieces.append(jnp.where(valid, -residual, 0.0))
                pieces.append(jnp.where(valid, (inverse - residual * deviation * inverse) * gate, 0.0))
            parts = (before(pieces[2]), before(pieces[3]), pieces[0], pieces[1], pieces[2], pieces[3],
                     after(pieces[0]), after(pieces[1]))
            for at, part in enumerate(parts):
                part = back_in_rows(part)
                d_cat[row, pl.ds(step * 7, 7), :, 256 * at:256 * (at + 1)] = part.astype(BF)
                d_own[row, pl.ds(step * 7, 7), :, 256 * at:256 * (at + 1)] = part[:, 8:24, :].astype(BF)

    left = turned(ctx_cat[3:19, :, 256:512])
    left = jnp.concatenate([left] * 4, axis=1)
    for a in range(3):
        for b in range(3):
            rights = []
            for k in (2 - a, 3 - a):
                phase, shift = VARIANT[k]
                at = 2 + phase + shift
                for l in (2 - b, 3 - b):
                    rights.append(d_own[phase, at:at + 16, :, 512 * l:512 * (l + 1)].reshape(256, 512))
            put(0, 3 * a + b, slice(0, 512), dot(left, jnp.concatenate(rights, axis=0)))

    @pl.loop(0, 2)
    def _(step):
        value = flat(coarse[pl.ds(step * 10 + 1, 10)])
        for k in range(4):
            phase, shift = VARIANT[k]
            at = step * 10 + shift + phase
            value = value + dot(flat(d_cat[phase, pl.ds(at, 10)]), fold_t[k])
        value = jnp.where(inside(place_ref, step * 10 - 2, 10), value, 0.0)
        three_wide(value, gc_cat, step * 10, 10)
        for at, part in enumerate((before(value), value, after(value))):
            gc_own[pl.ds(step * 10, 10), :, 256 * at:256 * (at + 1)] = back_in_rows(part)[:, 8:24, :].astype(BF)

    left = turned(pool_cat[4:20, :, 256:512])
    for a in range(3):
        for b in range(3):
            right = gc_own[3 - a:19 - a, :, 256 * (2 - b):256 * (3 - b)].reshape(256, 256)
            put(1, 3 * a + b, slice(0, 256), dot(left, right))

    @pl.loop(0, 2)
    def _(step):
        value = jnp.zeros((288, 256), F32)
        for a in range(3):
            value = value + dot(flat(gc_cat[pl.ds(step * 9 + a, 9)]), w_coarse_t[768 * a:768 * (a + 1)])
        value = value * 0.25
        valid = inside(place_ref, step * 9 - 1, 9)
        for row in range(2):
            even, odd = [
                jnp.where(valid, flat(err[2 * row + col, pl.ds(step * 9 + 1 + row, 9)]) + value, 0.0)
                for col in range(2)
            ]
            for at, part in enumerate((before(odd), even, odd, after(even))):
                compact = part.reshape(9, 32, 256)[:, 8:24, :]
                g_fine[row, pl.ds(step * 9, 9), :, 256 * at:256 * (at + 1)] = compact.astype(BF)

    left = jnp.concatenate([own_ref[p].reshape(256, 256).T for p in range(4)], axis=1)
    for a in range(3):
        for b in range(3):
            rights = []
            for row in range(2):
                phase, shift = VARIANT[row + 2 - a]
                for col in range(2):
                    at = col + 2 - b
                    rights.append(g_fine[phase, 1 + shift:17 + shift, :, 256 * at:256 * (at + 1)].reshape(256, 256))
            put(1, 3 * a + b, slice(256, 512), dot(left, jnp.concatenate(rights, axis=0)))
    keep_ref[...] = grads[0]
    send_ref[...] = grads[1]


def join_kernel(keep_ref, other_ref, out_ref):
    out_ref[...] = (keep_ref[...].astype(F32) + other_ref[...].astype(F32)).astype(BF)


def last_kernel(one_ref, two_ref, prior_ref, coarse_ref, post_ref):
    total = one_ref[...].astype(F32) + two_ref[...].astype(F32)
    for line in range(9):
        for at in range(4):
            lanes = slice(128 * at, 128 * (at + 1))
            prior_ref[4 * line + at:4 * line + at + 1, :] = total[0, line:line + 1, lanes]
            out, first = (coarse_ref, 2 * line + at) if at < 2 else (post_ref, 2 * line + at - 2)
            out[first:first + 1, :] = total[1, line:line + 1, lanes]


def feat_kernel(g_fine, w_post_t, out_ref, wide):
    for row in range(2):
        for col in range(2):
            value = jnp.zeros((256, 256), F32)
            for a in range(3):
                phase, shift = VARIANT[row + a]
                cells = g_fine[phase, 1 + shift:17 + shift, :, 256 * col:256 * col + 768].reshape(256, 768)
                value = value + dot(cells, w_post_t[768 * a:768 * (a + 1)])
            for half in range(2):
                wide[:, row, half, pl.ds(col, 16, stride=2), :] = (
                    value[:, 128 * half:128 * (half + 1)].reshape(16, 16, 128))
    for half in range(2):
        out_ref[:, :, :, 128 * half:128 * (half + 1)] = wide[:, :, half].astype(BF)


TAPS_OF = ((0,), (1, 2), (0, 1), (2,))


def weight_kernel(w_post, w_coarse, w_prior, fold, fold_t, w_post_t, w_coarse_t):
    for i in range(4):
        for j in range(4):
            taps = [3 * a + b for a in TAPS_OF[i] for b in TAPS_OF[j]]
            total = w_prior[256 * taps[0]:256 * (taps[0] + 1)].astype(F32)
            for tap in taps[1:]:
                total = total + w_prior[256 * tap:256 * (tap + 1)].astype(F32)
            total = total.astype(BF)
            fold[i, 256 * j:256 * (j + 1)] = total
            k, l = FOLD.index(i), FOLD.index(j)
            fold_t[k, 512 * l:512 * (l + 1)] = total.T
    for tap in range(9):
        w_coarse_t[256 * tap:256 * (tap + 1)] = w_coarse[256 * (8 - tap):256 * (9 - tap)].T
        w_post_t[256 * tap:256 * (tap + 1)] = w_post[256 * (8 - tap):256 * (9 - tap)].T


def sent(strip, down, right):
    pairs = [
        (r * 16 + c, (r + down) * 16 + c + right)
        for r in range(16) for c in range(16) if 0 <= r + down < 16 and 0 <= c + right < 16
    ]
    return lax.ppermute(strip, ("row", "col"), pairs)


def on_device(feat, noise_fine, noise_coarse, w_post, w_coarse, w_prior):
    scale = 1.0 / 512.0
    own, part, top, bottom = pl.pallas_call(
        first_kernel,
        out_shape=[
            jax.ShapeDtypeStruct((4, 16, 16, 256), BF),
            jax.ShapeDtypeStruct((4, 17, 32, 256), F32),
            jax.ShapeDtypeStruct((23, 16, 256), BF),
            jax.ShapeDtypeStruct((23, 16, 256), BF),
        ],
        in_specs=[pl.BlockSpec(memory_space=pltpu.HBM)] * 4,
        out_specs=in_vmem(4),
        scratch_shapes=[
            pltpu.VMEM((16, 2, 32, 256), BF),
            pltpu.VMEM((16, 2, 32, 256), F32),
            pltpu.VMEM((16, 16, 256), F32),
            pltpu.VMEM((2304, 256), BF),
            pltpu.VMEM((16, 2, 2, 32, 128), F32),
            pltpu.VMEM((16, 2, 2, 32, 128), F32),
            pltpu.VMEM((2, 18, 32, 256), F32),
            pltpu.VMEM((2, 18, 32, 1024), BF),
            pltpu.VMEM((32, 256), F32),
            pltpu.SemaphoreType.DMA((7,)),
        ],
        compiler_params=room(59),
        name="first",
    )(feat.reshape(16, 2, 32, 256), noise_fine.reshape(16, 2, 32, 256), noise_coarse, w_post)
    from_up, from_down = sent(bottom, 1, 0), sent(top, -1, 0)
    fold, fold_t, w_post_t, w_coarse_t = pl.pallas_call(
        weight_kernel,
        out_shape=[
            jax.ShapeDtypeStruct((4, 1024, 512), BF),
            jax.ShapeDtypeStruct((4, 2048, 256), BF),
            jax.ShapeDtypeStruct((2304, 256), BF),
            jax.ShapeDtypeStruct((2304, 256), BF),
        ],
        in_specs=in_vmem(3),
        out_specs=in_vmem(4),
        compiler_params=room(20),
        cost_estimate=pl.CostEstimate(flops=10000000, bytes_accessed=15000000, transcendentals=0),
        name="weights",
    )(w_post, w_coarse, w_prior)
    left, right = pl.pallas_call(
        middle_kernel,
        out_shape=[jax.ShapeDtypeStruct((24, 24, 256), BF)] * 2,
        in_specs=in_vmem(4),
        out_specs=in_vmem(2),
        scratch_shapes=[pltpu.VMEM((24, 24, 256), F32), pltpu.VMEM((32, 256), F32)],
        compiler_params=room(10),
        name="middle",
    )(part, noise_coarse, from_up, from_down)
    from_left, from_right = sent(right, 0, 1), sent(left, 0, -1)
    row, col = lax.axis_index("row"), lax.axis_index("col")
    place = jnp.stack([row, col, col % 2]).astype(jnp.int32)
    keep, send, g_fine = pl.pallas_call(
        functools.partial(main_kernel, scale),
        out_shape=[
            jax.ShapeDtypeStruct((2, 1152, 512), BF),
            jax.ShapeDtypeStruct((2, 1152, 512), BF),
            jax.ShapeDtypeStruct((2, 18, 16, 1024), BF),
        ],
        in_specs=[pl.BlockSpec(memory_space=pltpu.SMEM)] + in_vmem(11),
        out_specs=in_vmem(3),
        scratch_shapes=[
            pltpu.VMEM((4, 24, 32, 256), F32),
            pltpu.VMEM((22, 32, 256), F32),
            pltpu.VMEM((24, 32, 768), BF),
            pltpu.VMEM((22, 32, 256), F32),
            pltpu.VMEM((22, 32, 768), BF),
            pltpu.VMEM((4, 21, 32, 256), F32),
            pltpu.VMEM((2, 21, 32, 2048), BF),
            pltpu.VMEM((2, 21, 16, 2048), BF),
            pltpu.VMEM((20, 32, 768), BF),
            pltpu.VMEM((20, 16, 768), BF),
            pltpu.VMEM((32, 256), F32),
            pltpu.VMEM((2, 2, 1152, 512), BF),
        ],
        compiler_params=room(32),
        name="tile",
    )(place, own, part, noise_coarse, from_up, from_down, from_left, from_right,
      w_coarse, fold, fold_t, w_coarse_t)
    grad_feat = pl.pallas_call(
        feat_kernel,
        out_shape=jax.ShapeDtypeStruct((16, 2, 32, 256), BF),
        in_specs=in_vmem(2),
        out_specs=pl.BlockSpec(memory_space=pltpu.VMEM),
        scratch_shapes=[pltpu.VMEM((16, 2, 2, 32, 128), F32)],
        compiler_params=room(6),
        cost_estimate=pl.CostEstimate(flops=1200000000, bytes_accessed=3000000, transcendentals=0),
        name="feat",
    )(g_fine, w_post_t).reshape(32, 32, 256)
    prior, coarse, post, grad_feat = reduce_scatter(keep, send, grad_feat)
    return grad_feat, post, coarse, prior


def solution(mesh):
    return jax.shard_map(
        on_device,
        mesh=mesh,
        in_specs=(
            P("row", "col", None),
            P("row", "col", None),
            P("row", "col", None),
            P(),
            P(),
            P(),
        ),
        out_specs=(P("row", "col", None), P(("row", "col")), P(("row", "col")), P(("row", "col"))),
        check_vma=False,
    )
```

```python
import functools
import math

import jax
import jax.numpy as jnp
from jax import lax
from jax.experimental import pallas as pl
from jax.experimental.pallas import tpu as pltpu
from jax.sharding import PartitionSpec as P

BF = jnp.bfloat16
F32 = jnp.float32
VARIANT = ((1, -1), (0, 0), (1, 0), (0, 1))
FOLD = (3, 1, 2, 0)


def digits():
    places = []
    for d in range(256):
        row, col = d // 16, d % 16
        places.append({"zl": row // 4, "x": row % 4, "zh": col // 8, "y": (col // 2) % 4, "core": col % 2})
    return places


def index_of(place):
    return (place["zl"] * 4 + place["x"]) * 16 + (place["zh"] * 4 + place["y"]) * 2 + place["core"]


def my_place():
    row, col = lax.axis_index("row"), lax.axis_index("col")
    return {"zl": row // 4, "x": row % 4, "zh": col // 8, "y": (col // 2) % 4, "core": col % 2}


def flipped(place, name, bits):
    return {**place, name: place[name] ^ bits}


def sum_stage(part, name, cut, beside=None):
    here = my_place()[name]
    arrived = []
    for bits in (1, 3, 2):
        pairs = [(index_of(p), index_of(flipped(p, name, bits))) for p in digits()]
        arrived.append(lax.ppermute(cut(part, here ^ bits), ("row", "col"), pairs))
    if beside is not None:
        arrived, beside = lax.optimization_barrier((arrived, beside))
    total = cut(part, here).astype(F32)
    for piece in arrived:
        total = total + piece.astype(F32)
    total = total.astype(BF)
    return total if beside is None else (total, beside)


def pick(dim):
    return lambda part, at: lax.dynamic_index_in_dim(part, at, dim, keepdims=False)


def reduce_scatter(keep, send, beside):
    pairs = [(index_of(p), index_of(flipped(p, "core", 1))) for p in digits()]
    other = lax.ppermute(send, ("row", "col"), pairs)
    parts = pl.pallas_call(
        join_kernel,
        out_shape=jax.ShapeDtypeStruct((2, 1152, 512), BF),
        in_specs=in_vmem(2),
        out_specs=pl.BlockSpec(memory_space=pltpu.VMEM),
        compiler_params=room(9),
        name="join",
    )(keep, other)
    first, beside = sum_stage(parts[0].reshape(2, 4, 144, 512), "x", pick(1), beside)
    second = sum_stage(parts[1].reshape(2, 4, 2, 72, 512), "y", lambda part, at: pick(1)(pick(0)(part, at // 2), at % 2))
    first = sum_stage(first.reshape(4, 72, 512), "y", pick(0))
    second = sum_stage(second, "x", pick(0))
    parts = sum_stage(jnp.stack([first, second]).reshape(2, 4, 18, 512), "zl", pick(1))
    halves = parts.reshape(2, 2, 9, 512)
    last = my_place()["zh"]
    arrived = []
    for flip in (0, 1):
        pairs = []
        for p in digits():
            owner = {"zl": 2 * p["core"] + p["y"] // 2, "x": p["x"], "zh": p["y"] % 2, "y": p["zl"],
                     "core": p["zh"] ^ flip}
            pairs.append((index_of(p), index_of(owner)))
        piece = lax.dynamic_index_in_dim(halves, (last + flip) % 2, 1, keepdims=False)
        arrived.append(lax.ppermute(piece, ("row", "col"), pairs))
    prior, coarse, post = pl.pallas_call(
        last_kernel,
        out_shape=[jax.ShapeDtypeStruct((rows, 128), F32) for rows in (36, 18, 18)],
        in_specs=in_vmem(2),
        out_specs=in_vmem(3),
        compiler_params=room(4),
        name="last",
    )(*arrived)
    return prior.reshape(-1), coarse.reshape(-1), post.reshape(-1), beside


def room(mib):
    return pltpu.CompilerParams(vmem_limit_bytes=mib * 1024 * 1024)


def in_vmem(count):
    return [pl.BlockSpec(memory_space=pltpu.VMEM)] * count


def split_lanes(ref, value):
    for half in range(2):
        ref[:, :, half] = value[..., 128 * half:128 * (half + 1)]


def phase_of(ref, row, col):
    return jnp.concatenate([ref[:, row, half, pl.ds(col, 16, stride=2), :] for half in range(2)], axis=-1)


def line_of(ref, line, col):
    return jnp.concatenate(
        [ref[line // 2, line % 2, half, pl.ds(col, 16, stride=2), :] for half in range(2)], axis=-1)


def split_lanes(ref, value):
    for half in range(2):
        ref[:, :, half] = value[..., 128 * half:128 * (half + 1)]


def phase_of(ref, row, col):
    return jnp.concatenate([ref[:, row, half, pl.ds(col, 16, stride=2), :] for half in range(2)], axis=-1)


def first_kernel(feat_hbm, fine_hbm, low_hbm, post_hbm, own_ref, part_ref, top_ref, bottom_ref,
                 feat_ref, fine_ref, low_ref, w_post, wide, noise, field, cat, spill, sems):
    pairs = ((feat_hbm, feat_ref), (post_hbm.at[:768], w_post.at[:768]), (post_hbm.at[768:1536], w_post.at[768:1536]),
             (post_hbm.at[1536:], w_post.at[1536:]), (fine_hbm.at[:8], fine_ref.at[:8]),
             (fine_hbm.at[8:], fine_ref.at[8:]), (low_hbm, low_ref))
    copies = [pltpu.make_async_copy(source, target, sems.at[at]) for at, (source, target) in enumerate(pairs)]
    for copy in copies:
        copy.start()
    field[...] = jnp.zeros(field.shape, F32)
    spill[...] = jnp.zeros(spill.shape, F32)
    copies[0].wait()
    split_lanes(wide, feat_ref[...].astype(F32))
    for row in range(2):
        for col in range(2):
            cells = phase_of(wide, row, col)
            own_ref[2 * row + col] = cells.astype(BF)
            field[col, 1:17, 8:24, :] = cells
        even, odd = flat(field[0]), flat(field[1])
        for at, part in enumerate((before(odd), even, odd, after(even))):
            cat[row, :, :, 256 * at:256 * (at + 1)] = back_in_rows(part.astype(BF))
    for copy in copies[1:]:
        copy.wait()
    split_lanes(noise, fine_ref[...])
    for row in range(2):
        for col in range(2):
            value = jnp.zeros((544, 256), F32)
            for a in range(3):
                phase, shift = VARIANT[row + a]
                at = 1 + shift - row
                cells = flat(cat[phase, at:at + 17, :, 256 * col:256 * col + 768])
                value = value + dot(cells, w_post[768 * a:768 * (a + 1)])
            part_ref[2 * row + col] = back_in_rows(value)
            part_ref[2 * row + col, row:row + 16, 8:24, :] += phase_of(noise, row, col)
    for out, first, low_first in ((top_ref, -1, 0), (bottom_ref, 24, 13)):
        for r in range(9):
            line = first + r
            row = line % 2
            at = line // 2 + row
            for col in range(2):
                e = 2 * r + col
                out[e] = part_ref[2 * row + col, at, 8:24, :].astype(BF)
                edge = 7 if col else 24
                spill[e:e + 1, :] = part_ref[2 * row + col, at, edge:edge + 1, :]
        out[18:21] = low_ref[low_first:low_first + 3].astype(BF)
        out[21:23] = spill[...].reshape(2, 16, 256).astype(BF)


def middle_kernel(part_ref, low_ref, up_ref, down_ref, left_ref, right_ref, side, spill):
    lows = ((4, low_ref[...]), (1, up_ref[18:21].astype(F32)), (20, down_ref[18:21].astype(F32)))
    for out, long, long_from, other_from, low_from in ((left_ref, 1, -1, 0, 0), (right_ref, 0, 12, 12, 13)):
        side[...] = jnp.zeros(side.shape, F32)
        for row in range(2):
            at = 9 * row
            rows = slice(4 - row, 21 - row)
            side[rows, at:at + 5, :] = part_ref[2 * row + long, :, 8 + long_from:13 + long_from, :]
            side[rows, at + 5:at + 9, :] = part_ref[2 * row + 1 - long, :, 8 + other_from:12 + other_from, :]
        for ref, first in ((up_ref, -8), (down_ref, 31)):
            spill[...] = ref[21:23].astype(F32).reshape(32, 256)
            for r in range(9):
                line = first + r
                row = line % 2
                here, at = line // 2 + 4, 9 * row
                cells = ref[2 * r + long].astype(F32)
                end = spill[2 * r + long:2 * r + long + 1, :]
                if long:
                    side[here, at:at + 1, :] += end
                    side[here, at + 1:at + 5, :] += cells[0:4]
                else:
                    side[here, at:at + 4, :] += cells[12:16]
                    side[here, at + 4:at + 5, :] += end
                side[here, at + 5:at + 9, :] += ref[2 * r + 1 - long].astype(F32)[other_from:other_from + 4]
        for here, block in lows:
            side[here:here + block.shape[0], 18:21, :] = block[:, low_from:low_from + 3, :]
        out[...] = side[...].astype(BF)


def flat(block):
    return block.reshape(block.shape[0] * 32, block.shape[2])


def back_in_rows(block):
    return block.reshape(block.shape[0] // 32, 32, block.shape[1])


def before(block):
    return pltpu.roll(block, 1, 0)


def after(block):
    return pltpu.roll(block, block.shape[0] - 1, 0)


def dot(left, right):
    return jnp.dot(left, right, preferred_element_type=F32)


def inside(place_ref, first_row, rows):
    cell = lax.broadcasted_iota(jnp.int32, (rows * 32, 256), 0)
    line = cell // 32 + first_row + 16 * place_ref[0]
    column = cell % 32 - 8 + 16 * place_ref[1]
    return (line >= 0) & (line < 256) & (column >= 0) & (column < 256)


def three_wide(value, ref, first, rows):
    c = value.shape[1]
    for at, part in enumerate((before(value), value, after(value))):
        ref[pl.ds(first, rows), :, c * at:c * (at + 1)] = back_in_rows(part.astype(BF))


def own_cells(block):
    return block.astype(F32)[:, 8:24, :].reshape(256, block.shape[2]).astype(BF)


def turned(block):
    return own_cells(block).T


def main_kernel(scale, place_ref, own_ref, part_ref, low_ref, up_ref, down_ref, left_ref, right_ref,
                w_coarse, fold, fold_t, w_coarse_t, keep_ref, send_ref, g_fine,
                fine, low, pool_cat, coarse, ctx_cat, err, d_cat, d_own, gc_cat, gc_own, spill, grads):
    def put(which, tap, lanes, value):
        value = (value * scale).astype(BF)
        for half, first, start, stop in ((0, 256 * tap, 0, 256), (1, 256 * tap - 1152, 0, 256)):
            start, stop = max(start, -first), min(stop, 1152 - first)
            if start < stop:
                slot = (place_ref[2] + half) % 2
                grads[slot, which, first + start:first + stop, lanes] = value[start:stop]

    fine[...] = jnp.zeros(fine.shape, F32)
    for row in range(2):
        for col in range(2):
            fine[2 * row + col, 4 - row:21 - row] = part_ref[2 * row + col]
    low[3:19, 8:24, :] = low_ref[...]
    for ref, first, low_first in ((up_ref, -8, 0), (down_ref, 31, 19)):
        spill[...] = ref[21:23].astype(F32).reshape(32, 256)
        for r in range(9):
            line = first + r
            for col in range(2):
                e = 2 * r + col
                edge = 7 if col else 24
                fine[2 * (line % 2) + col, line // 2 + 4, 8:24, :] += ref[e].astype(F32)
                fine[2 * (line % 2) + col, line // 2 + 4, edge:edge + 1, :] += spill[e:e + 1, :]
        low[low_first:low_first + 3, 8:24, :] = ref[18:21].astype(F32)
    for ref, long, long_at, other_at, low_at in ((left_ref, 0, 4, 4, 5), (right_ref, 1, 23, 24, 24)):
        block = ref[...].astype(F32)
        for row in range(2):
            at = 9 * row
            fine[2 * row + long, :, long_at:long_at + 5, :] += block[:, at:at + 5, :]
            fine[2 * row + 1 - long, :, other_at:other_at + 4, :] += block[:, at + 5:at + 9, :]
        low[:, low_at:low_at + 3, :] = block[1:23, 18:21, :]

    @pl.loop(0, 3)
    def _(step):
        total = flat(fine[0, pl.ds(step * 8, 8)])
        for p in range(1, 4):
            total = total + flat(fine[p, pl.ds(step * 8, 8)])
        total = jnp.where(inside(place_ref, step * 8 - 4, 8), total * 0.25, 0.0)
        three_wide(total, pool_cat, step * 8, 8)

    @pl.loop(0, 2)
    def _(step):
        value = flat(low[pl.ds(step * 11, 11)])
        for a in range(3):
            value = value + dot(flat(pool_cat[pl.ds(step * 11 + a, 11)]), w_coarse[768 * a:768 * (a + 1)])
        value = jnp.where(inside(place_ref, step * 11 - 3, 11), value, 0.0)
        coarse[pl.ds(step * 11, 11)] = back_in_rows(value)
        three_wide(value, ctx_cat, step * 11, 11)

    for row in range(2):
        @pl.loop(0, 3)
        def _(step):
            valid = inside(place_ref, step * 7 - 2 - row, 7)
            pieces = []
            for col in range(2):
                prior = jnp.zeros((224, 512), F32)
                for k in range(2):
                    cells = flat(ctx_cat[pl.ds(step * 7 + k, 7), :, 256 * col:256 * col + 512])
                    prior = prior + dot(cells, fold[2 * row + k, 512 * col:512 * col + 512])
                raw = prior[:, 256:]
                small = jnp.exp(-jnp.abs(raw))
                more = 1.0 + small
                sigma = jnp.maximum(raw, 0.0) + jnp.log(more) + 0.5
                gate = jnp.where(raw >= 0.0, 1.0, small) / more
                inverse = 1.0 / sigma
                deviation = flat(fine[2 * row + col, pl.ds(step * 7 + 2 - row, 7)]) - prior[:, :256]
                residual = deviation * inverse * inverse
                err[2 * row + col, pl.ds(step * 7, 7)] = back_in_rows(residual)
                pieces.append(jnp.where(valid, -residual, 0.0))
                pieces.append(jnp.where(valid, (inverse - residual * deviation * inverse) * gate, 0.0))
            parts = (before(pieces[2]), before(pieces[3]), pieces[0], pieces[1], pieces[2], pieces[3],
                     after(pieces[0]), after(pieces[1]))
            for at, part in enumerate(parts):
                part = back_in_rows(part)
                d_cat[row, pl.ds(step * 7, 7), :, 256 * at:256 * (at + 1)] = part.astype(BF)
                d_own[row, pl.ds(step * 7, 7), :, 256 * at:256 * (at + 1)] = part[:, 8:24, :].astype(BF)

    left = turned(ctx_cat[3:19, :, 256:512])
    left = jnp.concatenate([left] * 4, axis=1)
    for a in range(3):
        for b in range(3):
            rights = []
            for k in (2 - a, 3 - a):
                phase, shift = VARIANT[k]
                at = 2 + phase + shift
                for l in (2 - b, 3 - b):
                    rights.append(d_own[phase, at:at + 16, :, 512 * l:512 * (l + 1)].reshape(256, 512))
            put(0, 3 * a + b, slice(0, 512), dot(left, jnp.concatenate(rights, axis=0)))

    @pl.loop(0, 2)
    def _(step):
        value = flat(coarse[pl.ds(step * 10 + 1, 10)])
        for k in range(4):
            phase, shift = VARIANT[k]
            at = step * 10 + shift + phase
            value = value + dot(flat(d_cat[phase, pl.ds(at, 10)]), fold_t[k])
        value = jnp.where(inside(place_ref, step * 10 - 2, 10), value, 0.0)
        three_wide(value, gc_cat, step * 10, 10)
        for at, part in enumerate((before(value), value, after(value))):
            gc_own[pl.ds(step * 10, 10), :, 256 * at:256 * (at + 1)] = back_in_rows(part)[:, 8:24, :].astype(BF)

    left = turned(pool_cat[4:20, :, 256:512])
    for a in range(3):
        for b in range(3):
            right = gc_own[3 - a:19 - a, :, 256 * (2 - b):256 * (3 - b)].reshape(256, 256)
            put(1, 3 * a + b, slice(0, 256), dot(left, right))

    @pl.loop(0, 2)
    def _(step):
        value = jnp.zeros((288, 256), F32)
        for a in range(3):
            value = value + dot(flat(gc_cat[pl.ds(step * 9 + a, 9)]), w_coarse_t[768 * a:768 * (a + 1)])
        value = value * 0.25
        valid = inside(place_ref, step * 9 - 1, 9)
        for row in range(2):
            even, odd = [
                jnp.where(valid, flat(err[2 * row + col, pl.ds(step * 9 + 1 + row, 9)]) + value, 0.0)
                for col in range(2)
            ]
            for at, part in enumerate((before(odd), even, odd, after(even))):
                compact = part.reshape(9, 32, 256)[:, 8:24, :]
                g_fine[row, pl.ds(step * 9, 9), :, 256 * at:256 * (at + 1)] = compact.astype(BF)

    left = jnp.concatenate([own_ref[p].reshape(256, 256).T for p in range(4)], axis=1)
    for a in range(3):
        for b in range(3):
            rights = []
            for row in range(2):
                phase, shift = VARIANT[row + 2 - a]
                for col in range(2):
                    at = col + 2 - b
                    rights.append(g_fine[phase, 1 + shift:17 + shift, :, 256 * at:256 * (at + 1)].reshape(256, 256))
            put(1, 3 * a + b, slice(256, 512), dot(left, jnp.concatenate(rights, axis=0)))
    keep_ref[...] = grads[0]
    send_ref[...] = grads[1]


def join_kernel(keep_ref, other_ref, out_ref):
    out_ref[...] = (keep_ref[...].astype(F32) + other_ref[...].astype(F32)).astype(BF)


def last_kernel(one_ref, two_ref, prior_ref, coarse_ref, post_ref):
    total = one_ref[...].astype(F32) + two_ref[...].astype(F32)
    for line in range(9):
        for at in range(4):
            lanes = slice(128 * at, 128 * (at + 1))
            prior_ref[4 * line + at:4 * line + at + 1, :] = total[0, line:line + 1, lanes]
            out, first = (coarse_ref, 2 * line + at) if at < 2 else (post_ref, 2 * line + at - 2)
            out[first:first + 1, :] = total[1, line:line + 1, lanes]


def feat_kernel(g_fine, w_post_t, out_ref, wide):
    for row in range(2):
        for col in range(2):
            value = jnp.zeros((256, 256), F32)
            for a in range(3):
                phase, shift = VARIANT[row + a]
                cells = g_fine[phase, 1 + shift:17 + shift, :, 256 * col:256 * col + 768].reshape(256, 768)
                value = value + dot(cells, w_post_t[768 * a:768 * (a + 1)])
            for half in range(2):
                wide[:, row, half, pl.ds(col, 16, stride=2), :] = (
                    value[:, 128 * half:128 * (half + 1)].reshape(16, 16, 128))
    for half in range(2):
        out_ref[:, :, :, 128 * half:128 * (half + 1)] = wide[:, :, half].astype(BF)


TAPS_OF = ((0,), (1, 2), (0, 1), (2,))


def weight_kernel(w_post, w_coarse, w_prior, fold, fold_t, w_post_t, w_coarse_t):
    for i in range(4):
        for j in range(4):
            taps = [3 * a + b for a in TAPS_OF[i] for b in TAPS_OF[j]]
            total = w_prior[256 * taps[0]:256 * (taps[0] + 1)].astype(F32)
            for tap in taps[1:]:
                total = total + w_prior[256 * tap:256 * (tap + 1)].astype(F32)
            total = total.astype(BF)
            fold[i, 256 * j:256 * (j + 1)] = total
            k, l = FOLD.index(i), FOLD.index(j)
            fold_t[k, 512 * l:512 * (l + 1)] = total.T
    for tap in range(9):
        w_coarse_t[256 * tap:256 * (tap + 1)] = w_coarse[256 * (8 - tap):256 * (9 - tap)].T
        w_post_t[256 * tap:256 * (tap + 1)] = w_post[256 * (8 - tap):256 * (9 - tap)].T


def sent(strip, down, right):
    pairs = [
        (r * 16 + c, (r + down) * 16 + c + right)
        for r in range(16) for c in range(16) if 0 <= r + down < 16 and 0 <= c + right < 16
    ]
    return lax.ppermute(strip, ("row", "col"), pairs)


def on_device(feat, noise_fine, noise_coarse, w_post, w_coarse, w_prior):
    scale = 1.0 / 512.0
    own, part, top, bottom = pl.pallas_call(
        first_kernel,
        out_shape=[
            jax.ShapeDtypeStruct((4, 16, 16, 256), BF),
            jax.ShapeDtypeStruct((4, 17, 32, 256), F32),
            jax.ShapeDtypeStruct((23, 16, 256), BF),
            jax.ShapeDtypeStruct((23, 16, 256), BF),
        ],
        in_specs=[pl.BlockSpec(memory_space=pltpu.HBM)] * 4,
        out_specs=in_vmem(4),
        scratch_shapes=[
            pltpu.VMEM((16, 2, 32, 256), BF),
            pltpu.VMEM((16, 2, 32, 256), F32),
            pltpu.VMEM((16, 16, 256), F32),
            pltpu.VMEM((2304, 256), BF),
            pltpu.VMEM((16, 2, 2, 32, 128), F32),
            pltpu.VMEM((16, 2, 2, 32, 128), F32),
            pltpu.VMEM((2, 18, 32, 256), F32),
            pltpu.VMEM((2, 18, 32, 1024), BF),
            pltpu.VMEM((32, 256), F32),
            pltpu.SemaphoreType.DMA((7,)),
        ],
        compiler_params=room(59),
        name="first",
    )(feat.reshape(16, 2, 32, 256), noise_fine.reshape(16, 2, 32, 256), noise_coarse, w_post)
    from_up, from_down = sent(bottom, 1, 0), sent(top, -1, 0)
    fold, fold_t, w_post_t, w_coarse_t = pl.pallas_call(
        weight_kernel,
        out_shape=[
            jax.ShapeDtypeStruct((4, 1024, 512), BF),
            jax.ShapeDtypeStruct((4, 2048, 256), BF),
            jax.ShapeDtypeStruct((2304, 256), BF),
            jax.ShapeDtypeStruct((2304, 256), BF),
        ],
        in_specs=in_vmem(3),
        out_specs=in_vmem(4),
        compiler_params=room(20),
        cost_estimate=pl.CostEstimate(flops=10000000, bytes_accessed=15000000, transcendentals=0),
        name="weights",
    )(w_post, w_coarse, w_prior)
    left, right = pl.pallas_call(
        middle_kernel,
        out_shape=[jax.ShapeDtypeStruct((24, 24, 256), BF)] * 2,
        in_specs=in_vmem(4),
        out_specs=in_vmem(2),
        scratch_shapes=[pltpu.VMEM((24, 24, 256), F32), pltpu.VMEM((32, 256), F32)],
        compiler_params=room(10),
        name="middle",
    )(part, noise_coarse, from_up, from_down)
    from_left, from_right = sent(right, 0, 1), sent(left, 0, -1)
    row, col = lax.axis_index("row"), lax.axis_index("col")
    place = jnp.stack([row, col, col % 2]).astype(jnp.int32)
    keep, send, g_fine = pl.pallas_call(
        functools.partial(main_kernel, scale),
        out_shape=[
            jax.ShapeDtypeStruct((2, 1152, 512), BF),
            jax.ShapeDtypeStruct((2, 1152, 512), BF),
            jax.ShapeDtypeStruct((2, 18, 16, 1024), BF),
        ],
        in_specs=[pl.BlockSpec(memory_space=pltpu.SMEM)] + in_vmem(11),
        out_specs=in_vmem(3),
        scratch_shapes=[
            pltpu.VMEM((4, 24, 32, 256), F32),
            pltpu.VMEM((22, 32, 256), F32),
            pltpu.VMEM((24, 32, 768), BF),
            pltpu.VMEM((22, 32, 256), F32),
            pltpu.VMEM((22, 32, 768), BF),
            pltpu.VMEM((4, 21, 32, 256), F32),
            pltpu.VMEM((2, 21, 32, 2048), BF),
            pltpu.VMEM((2, 21, 16, 2048), BF),
            pltpu.VMEM((20, 32, 768), BF),
            pltpu.VMEM((20, 16, 768), BF),
            pltpu.VMEM((32, 256), F32),
            pltpu.VMEM((2, 2, 1152, 512), BF),
        ],
        compiler_params=room(32),
        name="tile",
    )(place, own, part, noise_coarse, from_up, from_down, from_left, from_right,
      w_coarse, fold, fold_t, w_coarse_t)
    grad_feat = pl.pallas_call(
        feat_kernel,
        out_shape=jax.ShapeDtypeStruct((16, 2, 32, 256), BF),
        in_specs=in_vmem(2),
        out_specs=pl.BlockSpec(memory_space=pltpu.VMEM),
        scratch_shapes=[pltpu.VMEM((16, 2, 2, 32, 128), F32)],
        compiler_params=room(6),
        cost_estimate=pl.CostEstimate(flops=1200000000, bytes_accessed=3000000, transcendentals=0),
        name="feat",
    )(g_fine, w_post_t).reshape(32, 32, 256)
    prior, coarse, post, grad_feat = reduce_scatter(keep, send, grad_feat)
    return grad_feat, post, coarse, prior


def solution(mesh):
    return jax.shard_map(
        on_device,
        mesh=mesh,
        in_specs=(
            P("row", "col", None),
            P("row", "col", None),
            P("row", "col", None),
            P(),
            P(),
            P(),
        ),
        out_specs=(P("row", "col", None), P(("row", "col")), P(("row", "col")), P(("row", "col"))),
        check_vma=False,
    )
```
